32 devices in a mesh: cls: 4 (over z), vol: 8 (over y, x, core).
Axes of the slice: x: 2, y: 2, z: 4, core: 2. Of those that a mesh axis runs over, the one named last changes fastest.
Arguments:
- images: bfloat16 [256, 256, 2, 256], P(('cls', 'vol')), may hold values from -8 to 8
- projections: bfloat16 [4, 128, 256, 2, 256], P('cls', None, 'vol'), may hold values from -0.049718446 to 0.049718446
- assignment: int32 [256, 1], P(('cls', 'vol')), may hold values from 0 to 3; in each aligned block of 8 rows (0 to 7, 8 to 15, ...) at most 4 rows name the same one
- interp_cells: int32 [128, 4, 256], replicated, may hold values from 0 to 65535, as said below
- interp_weights: float32 [128, 4, 256], replicated, may hold values from 0 to 1, as said below
Outputs:
- class_volume: float32 [4, 256, 256, 256], P('cls', 'vol')
The draws below stay inside these ranges and needn't reach their ends.
Inputs may be any that keep to these rules, and one draw needn't show every extreme that they name: `assignment`: among the 8 particles of one device (aligned blocks of 8 rows), at most 4 name the same class. `interp_cells`: for each direction and column u the four cells are (x, y), (x + 1, y), (x, y + 1), (x + 1, y + 1) modulo 256, in that order. `interp_weights`: for each direction and column u the four weights are nonnegative and sum to one.
All inputs are finite; a program needn't handle non-finite values.
Results may differ from the reference program's by a relative error of at most 0.0027.
Values may be sent and summed in bfloat16 or wider, within the bound.
No kernel may reach another device: no remote copies, remote signals or barrier semaphores. Data moves between devices by JAX's collectives and lax.ppermute only.
A program may use at most 256 MiB of HBM per device.

```python
import math
import jax
import jax.numpy as jnp
import numpy as np
from jax import lax

GRID = 256
DIRS = 128
P_DEV = 8
CLASSES = 4
CAP = 4
PARTICLES = 256


COSINE_TABLE = (np.cos(np.arange(4096) * (2.0 * np.pi / 4096.0)) * 1024.0).astype(np.int32)


SINE_TABLE = (np.sin(np.arange(4096) * (2.0 * np.pi / 4096.0)) * 1024.0).astype(np.int32)


def projection_field(key):
    factor = 3.0 / math.sqrt(2.0 * GRID * GRID)
    noise = jax.random.normal(jax.random.fold_in(key, 11), (CLASSES, DIRS, GRID, 2, GRID), jnp.float32)
    return jnp.clip(noise, -6.0, 6.0) * factor


def draw_projections(key, part):
    field = projection_field(key)
    return field.astype(jnp.bfloat16)


def draw_images(key, part):
    noise_key = jax.random.fold_in(key, 23)
    image = jnp.clip(jax.random.normal(noise_key, (PARTICLES, GRID, 2, GRID), jnp.float32), -6.0, 6.0)
    return jnp.clip(image, -8.0, 8.0).astype(jnp.bfloat16)


def interpolation(key):
    angles = jax.random.randint(jax.random.fold_in(key, 41), (DIRS,), 0, 4096)
    cosine = jnp.asarray(COSINE_TABLE)[angles]
    sine_part = jnp.asarray(SINE_TABLE)[angles]
    offset = jnp.arange(GRID, dtype=jnp.int32) - GRID // 2
    along_x = offset[None, :] * cosine[:, None]
    along_y = offset[None, :] * sine_part[:, None]
    base_x = GRID // 2 + along_x // 1024
    base_y = GRID // 2 + along_y // 1024
    frac_x = along_x % 1024
    frac_y = along_y % 1024
    cells = []
    weights = []
    for step_x, step_y in ((0, 0), (1, 0), (0, 1), (1, 1)):
        cell_x = (base_x + step_x) % GRID
        cell_y = (base_y + step_y) % GRID
        cells.append(cell_x * GRID + cell_y)
        weight_x = frac_x if step_x == 1 else 1024 - frac_x
        weight_y = frac_y if step_y == 1 else 1024 - frac_y
        weights.append(weight_x.astype(jnp.float32) * weight_y.astype(jnp.float32) / 1048576.0)
    return (jnp.stack(cells, axis=1).astype(jnp.int32), jnp.stack(weights, axis=1))


def draw_interp_cells(key, part):
    cells, weights = interpolation(key)
    return cells


def draw_interp_weights(key, part):
    cells, weights = interpolation(key)
    return weights.astype(jnp.float32)


def routed_block(own_key, own, number, rows, count, top, bound, skew):
    ranking = jax.random.permutation(own_key, count)
    heavy_load, ordinary = load_shares(count, rows * top, bound, skew, True), load_shares(count, rows * top, bound, skew, False)
    places = jnp.arange(count)

    def named(sizes, rotation):
        used = int((sizes > 0).sum())
        fixed = max(1, used // 4)
        shifted = fixed + (places - fixed + rotation * (used - fixed)) % max(1, count - fixed)
        return jnp.zeros((count,), jnp.int32).at[ranking[jnp.where(places < fixed, places, shifted)]].set(jnp.asarray(sizes, jnp.int32))

    sizes = jnp.where(number % 4 == 0, named(heavy_load, number // 4), named(ordinary, number - number // 4 - 1))
    mixed = jax.random.permutation(jax.random.fold_in(own, 3), count)
    giver, taker = mixed[0:count // 2 * 2:2], mixed[1:count // 2 * 2:2]
    room = jnp.minimum(sizes[giver] - 1, bound - sizes[taker]) // 2
    room = jnp.where((giver == ranking[0]) | (taker == ranking[0]) | (sizes[taker] == 0), 0, jnp.maximum(room, 0))
    shifted = jax.random.randint(jax.random.fold_in(own, 4), (count // 2,), 0, 1 << 20) % (room + 1)
    sizes = sizes.at[giver].add(-shifted).at[taker].add(shifted)
    labels = jnp.searchsorted(jnp.cumsum(sizes), jnp.arange(rows * top), side="right").astype(jnp.int32)
    grid = labels.reshape(top, rows).T
    grid = grid[jax.random.permutation(jax.random.fold_in(own, 1), rows)]
    rotation = jax.random.randint(jax.random.fold_in(own, 2), (rows, 1), 0, top)
    return jnp.take_along_axis(grid, (jnp.arange(top)[None, :] + rotation) % top, axis=1)


def load_shares(count, total, bound, skew, full):
    portions = [(1 << 20) // math.isqrt(rank ** skew) + 1 for rank in range(1, count + 1)]
    largest = bound if full else min(bound, max(-(-total // count), total * portions[0] // sum(portions)))
    least = 1 if total - largest >= count - 1 else 0
    holding, spare = [largest] + [least] * (count - 1), total - largest - least * (count - 1)
    while spare > 0:
        candidates = [i for i in range(1, count) if holding[i] < largest] or [i for i in range(1, count) if holding[i] < bound]
        mass, budget = sum([portions[i] for i in candidates]), spare
        for i in candidates:
            extra = min(bound - holding[i], max(1, budget * portions[i] // mass), spare)
            holding[i] = holding[i] + extra
            spare = spare - extra
    return np.array(holding)


def setup_inputs(seed: int = 0) -> dict:
    splits = jax.random.split(jax.random.key(seed), 6)
    images = draw_images(jax.random.fold_in(splits[5], 71), 0)
    projections = draw_projections(jax.random.fold_in(splits[5], 71), 0)
    assignment_keys = jax.random.split(jax.random.fold_in(splits[2], 1), PARTICLES // P_DEV)
    assignment_turns = jax.random.permutation(jax.random.fold_in(splits[2], 3), PARTICLES // P_DEV)
    assignment = jax.vmap(lambda own, number: routed_block(jax.random.fold_in(splits[2], 2), own, number, P_DEV, CLASSES, 1, CAP, 2))(assignment_keys, assignment_turns).reshape((PARTICLES, 1))
    interp_cells = draw_interp_cells(jax.random.fold_in(splits[5], 71), 0)
    interp_weights = draw_interp_weights(jax.random.fold_in(splits[5], 71), 0)
    return {"images": images, "projections": projections, "assignment": assignment, "interp_cells": interp_cells, "interp_weights": interp_weights}


def reference(images, projections, assignment, interp_cells, interp_weights):
    classes = assignment[:, 0].astype(jnp.int32)
    window = 2 * PARTICLES // CLASSES
    order = jnp.argsort(classes, stable=True).astype(jnp.int32)
    member = (classes[None, :] == jnp.arange(CLASSES, dtype=jnp.int32)[:, None]).astype(jnp.int32)
    counts = jnp.sum(member, axis=1)
    starts = jnp.cumsum(counts) - counts
    flat_images = images.reshape(PARTICLES, GRID * 2 * GRID)
    cells_flat = interp_cells.reshape(-1).astype(jnp.int32)

    def one_class(class_id):
        positions = starts[class_id] + jnp.arange(window, dtype=jnp.int32)
        valid = jnp.arange(window, dtype=jnp.int32) < counts[class_id]
        rows = order[jnp.clip(positions, 0, PARTICLES - 1)]
        picked = jnp.where(valid[:, None], flat_images[rows], jnp.zeros((), jnp.bfloat16))
        refs = lax.dynamic_index_in_dim(projections, class_id, 0, keepdims=False).reshape(DIRS, GRID * 2 * GRID)
        scores = jnp.dot(picked, refs.T, preferred_element_type=jnp.float32)
        highest = jnp.max(scores, axis=1, keepdims=True)
        expo = jnp.exp(scores - highest)
        posterior = (expo / jnp.sum(expo, axis=1, keepdims=True)).astype(jnp.bfloat16)
        average = jnp.dot(posterior.T, picked, preferred_element_type=jnp.float32)
        spread = average.reshape(DIRS, GRID, 2, GRID)
        contribution = jnp.transpose(spread, (1, 2, 0, 3))[:, :, :, None, :] * interp_weights[None, None, :, :, :]
        fourier_plane = jnp.zeros((GRID * 2, GRID * GRID), jnp.float32)
        fourier_plane = fourier_plane.at[:, cells_flat].add(contribution.reshape(GRID * 2, -1))
        fourier_plane = fourier_plane.reshape(GRID, 2, GRID, GRID)
        spectrum = lax.complex(fourier_plane[:, 0], fourier_plane[:, 1])
        spatial = jnp.fft.ifftn(spectrum, norm="ortho")
        return jnp.transpose(jnp.real(spatial), (1, 2, 0)).astype(jnp.float32)

    return lax.map(one_class, jnp.arange(CLASSES, dtype=jnp.int32))
```

```python
import functools
import math

import jax
import jax.numpy as jnp
import numpy as np
from jax import lax
from jax.experimental import pallas as pl
from jax.experimental.pallas import tpu as pltpu
from jax.sharding import PartitionSpec as P

F32 = jnp.float32
BF16 = jnp.bfloat16
LANES = 128
HALF = 64
CHUNK = 128
VMEM = pltpu.VMEM


def split_table(table):
    high = table.astype(jnp.bfloat16)
    low = (table - high.astype(np.float64)).astype(jnp.bfloat16)
    return high, low


def tables(grid, slabs):
    half = grid // 2
    scale = 1.0 / math.sqrt(grid)
    index = np.arange(grid)
    angle = 2.0 * np.pi / grid
    phase = (index[:, None] * np.arange(half)[None, :]) % grid
    cosine = np.cos(phase * angle)
    sine = np.sin(phase * angle)
    sine[:, 0] = np.cos(((index * half) % grid) * angle)
    table_y = np.concatenate([cosine, sine], axis=1) * scale
    rows = half + 8
    phase = (np.arange(rows)[:, None] * index[None, :]) % grid
    live = (np.arange(rows) <= half)[:, None]
    table_x = np.concatenate([np.cos(phase * angle) * live, np.sin(phase * angle) * live], axis=0) * scale
    phase = (index[:, None] * index[None, :]) % grid
    table_z = np.stack([np.cos(phase * angle), -np.sin(phase * angle)], axis=1).reshape(2 * grid, grid) * scale
    order = np.concatenate([np.arange(half), [half], np.arange(grid - 1, half, -1)])
    restore = (order[None, :] == index[:, None]).astype(jnp.bfloat16)
    return split_table(table_y), split_table(table_x), split_table(table_z), restore


def dot(a, b):
    return jnp.dot(a, b, preferred_element_type=F32)


def dot_t(a, b):
    return lax.dot_general(a, b, (((1,), (1,)), ((), ())), preferred_element_type=F32)


def two_terms(value):
    high = value.astype(BF16)
    low = (value - high.astype(F32)).astype(BF16)
    return high, low


def score_kernel(cap, dirs, images_ref, refs_ref, out_ref, sums):
    sources, groups, rows16, _ = images_ref.shape
    rows = sources * rows16
    steps = rows16 // cap
    sums[...] = jnp.zeros_like(sums)

    def step(g, carry):
        block = images_ref[:, pl.ds(g, 1), :, :].reshape(rows, LANES)
        sums[...] += dot_t(refs_ref[g], block)
        return carry

    lax.fori_loop(0, groups, step, 0)
    column = lax.broadcasted_iota(jnp.int32, (dirs, rows), 1)
    part = (column & (rows16 - 1)) // cap
    kept = jnp.zeros((dirs, rows), F32)
    for j in range(steps):
        kept = kept + jnp.where(part == j, sums[j * dirs : (j + 1) * dirs, :], 0.0)
    slots = sources * cap
    row_id = lax.broadcasted_iota(jnp.int32, (rows, slots), 0)
    slot_id = lax.broadcasted_iota(jnp.int32, (rows, slots), 1)
    gather = (row_id // rows16 * cap + row_id % cap) == slot_id
    out_ref[...] = jnp.dot(
        kept, gather.astype(F32), preferred_element_type=F32, precision=lax.Precision.HIGHEST
    )


def scores_call(images, refs, cap, dirs):
    sources, groups, rows16, _ = images.shape
    return pl.pallas_call(
        functools.partial(score_kernel, cap, dirs),
        out_shape=jax.ShapeDtypeStruct((dirs, sources * cap), F32),
        in_specs=[pl.BlockSpec(memory_space=VMEM)] * 2,
        out_specs=pl.BlockSpec(memory_space=VMEM),
        scratch_shapes=[VMEM((refs.shape[1], sources * rows16), F32)],
        compiler_params=pltpu.CompilerParams(vmem_limit_bytes=48 * 2**20),
        name="scores",
    )(images, refs)


def scatter_kernel(
    cap,
    width,
    grid,
    total_ref,
    chunk_row_ref,
    chunk_start_ref,
    point_ref,
    parts_ref,
    images_ref,
    weights_ref,
    keys_ref,
    out_ref,
    values,
    buffer_a,
    buffer_b,
    sums,
    spread,
):
    sources, groups, rows16, _ = images_ref.shape
    rows = sources * rows16
    steps = rows16 // cap
    dirs, slots = parts_ref.shape[1:]
    joined = steps * dirs
    halves = LANES // width

    total = parts_ref[0]
    for i in range(1, parts_ref.shape[0]):
        total = total + parts_ref[i]
    expo = jnp.exp(total - jnp.max(total, axis=0, keepdims=True))
    posterior = (expo / jnp.sum(expo, axis=0, keepdims=True)).astype(BF16)
    slot_id = lax.broadcasted_iota(jnp.int32, (slots, rows), 0)
    row_id = lax.broadcasted_iota(jnp.int32, (slots, rows), 1)
    repeat = ((row_id // rows16 * cap + row_id % cap) == slot_id).astype(F32).astype(BF16)
    wide = dot(posterior, repeat)
    part = (lax.broadcasted_iota(jnp.int32, (dirs, rows), 1) & (rows16 - 1)) // cap
    for j in range(steps):
        spread[j * dirs : (j + 1) * dirs, :] = jnp.where(part == j, wide, 0.0).astype(BF16)

    lane_j = lax.broadcasted_iota(jnp.int32, (joined, LANES), 1)

    def average(g, carry):
        block = images_ref[:, pl.ds(g, 1), :, :].reshape(rows, LANES)
        mean = dot(spread[...], block)
        weight = weights_ref[g]
        for h in range(halves):
            shifted = mean if h == 0 else pltpu.roll(mean, LANES - h * width, 1)
            behind = pltpu.roll(weight, HALF - 4 * h, 1)
            start = pl.multiple_of((h * groups + g) * joined, joined)
            values[pl.ds(start, joined), :] = jnp.where(lane_j < HALF, shifted, behind)
        return carry

    lax.fori_loop(0, groups, average, 0)

    buffer_a[...] = jnp.zeros_like(buffer_a)
    buffer_b[...] = jnp.zeros_like(buffer_b)
    sums[...] = jnp.zeros_like(sums)

    lane = lax.broadcasted_iota(jnp.int32, (CHUNK, LANES), 1)
    lane_y = lax.broadcasted_iota(jnp.int32, (grid, LANES), 1)
    cell_y = lax.broadcasted_iota(jnp.int32, (grid, CHUNK), 0)
    lane_8 = lax.broadcasted_iota(jnp.int32, (8, LANES), 1)
    pick_row = lax.broadcasted_iota(jnp.int32, (width, LANES), 0)
    pick_lane = lax.broadcasted_iota(jnp.int32, (width, LANES), 1)
    pick = ((pick_lane == pick_row) | (pick_lane == pick_row + HALF)).astype(F32).astype(BF16)

    def fetch(c, buffer):
        start = chunk_start_ref[c]
        for i in range(CHUNK):
            buffer[pl.ds(i, 1), :] = values[pl.ds(point_ref[start + i], 1), :]

    def transposed(plane):
        high = plane.astype(BF16).astype(F32)
        both = jnp.where(lane_y < HALF, high, pltpu.roll(plane - high, HALF, 1)).astype(BF16)
        return dot_t(pick, both)

    def put(x, flipped):
        for side in range(grid // LANES):
            out_ref[side, pl.ds(x, width, stride=grid), :] = flipped[:, side * LANES : (side + 1) * LANES]

    def work(c, buffer):
        row = chunk_row_ref[c]
        before = chunk_row_ref[jnp.maximum(c - 1, 0)]
        start = chunk_start_ref[c]
        base = start >> 7
        offset = start & (LANES - 1)
        turn = LANES - offset
        first = pltpu.roll(jnp.broadcast_to(keys_ref[pl.ds(base, 1), :], (8, LANES)), turn, 1)
        second = pltpu.roll(jnp.broadcast_to(keys_ref[pl.ds(base + 1, 1), :], (8, LANES)), turn, 1)
        key = jnp.where(lane_8 < turn, first, second)
        valid = (key >> 23) == row
        y = (key >> 15) & (grid - 1)
        low_y = jnp.where(valid, y, -1)[0:1, :]
        high_y = jnp.where(valid, (y + 1) & (grid - 1), -1)[0:1, :]
        hot = jnp.concatenate(
            [
                jnp.where(cell_y == low_y, 1.0, 0.0).astype(BF16),
                jnp.where(cell_y == high_y, 1.0, 0.0).astype(BF16),
            ],
            axis=1,
        )
        data = buffer[...]
        twice = jnp.where(lane < HALF, data, pltpu.roll(data, HALF, 1))
        weight = [jnp.broadcast_to(data[:, HALF + j : HALF + j + 1], (CHUNK, LANES)) for j in range(4)]
        low_h, low_l = two_terms(twice * jnp.where(lane < HALF, weight[0], weight[1]))
        high_h, high_l = two_terms(twice * jnp.where(lane < HALF, weight[2], weight[3]))
        operand = jnp.concatenate(
            [jnp.concatenate([low_h, low_l], axis=1), jnp.concatenate([high_h, high_l], axis=1)], axis=0
        )
        result = dot(hot, operand)
        result = result[:, :LANES] + result[:, LANES:]
        old = sums[...]
        put((before + (grid - 1)) & (grid - 1), transposed(old))
        moved = jnp.where(lane_y < HALF, pltpu.roll(old, HALF, 1), 0.0)
        sums[...] = result + jnp.where(row == before, old, moved)

    fetch(0, buffer_a)

    def pair(m, carry):
        fetch(2 * m + 1, buffer_b)
        work(2 * m, buffer_a)
        fetch(2 * m + 2, buffer_a)
        work(2 * m + 1, buffer_b)
        return carry

    lax.fori_loop(0, total_ref[0], pair, 0)
    last = sums[...]
    put(grid - 2, transposed(last))
    wrapped = transposed(pltpu.roll(last, HALF, 1))
    for side in range(grid // LANES):
        place = pl.ds(grid - 1, width, stride=grid)
        out_ref[side, place, :] = out_ref[side, place, :] + wrapped[:, side * LANES : (side + 1) * LANES]


def scatter_call(pairs, chunk_row, chunk_start, point, parts, images, weights, keys, cap, width, grid):
    sources, groups, rows16, _ = images.shape
    dirs = parts.shape[1]
    points = dirs * grid
    smem = pl.BlockSpec(memory_space=pltpu.SMEM)
    vmem = pl.BlockSpec(memory_space=VMEM)
    return pl.pallas_call(
        functools.partial(scatter_kernel, cap, width, grid),
        out_shape=jax.ShapeDtypeStruct((grid // LANES, width * grid, LANES), F32),
        in_specs=[smem] * 4 + [vmem] * 4,
        out_specs=vmem,
        scratch_shapes=[
            VMEM((points, LANES), F32),
            VMEM((CHUNK, LANES), F32),
            VMEM((CHUNK, LANES), F32),
            VMEM((grid, LANES), F32),
            VMEM((weights.shape[1], sources * rows16), BF16),
        ],
        compiler_params=pltpu.CompilerParams(vmem_limit_bytes=60 * 2**20),
        name="scatter",
    )(pairs, chunk_row, chunk_start, point, parts, images, weights, keys)


def plane_kernel(slabs, data_ref, yh_ref, yl_ref, xh_ref, xl_ref, out_ref, rows16):
    width, grid = data_ref.shape[1] // 2, data_ref.shape[2]
    half = grid // 2
    slab = grid // slabs
    lane = lax.broadcasted_iota(jnp.int32, (grid, half), 1)

    def one(z, carry):
        parts = []
        for r in range(2):
            plane = jnp.concatenate([data_ref[side, 2 * z + r] for side in range(grid // LANES)], axis=1)
            high, low = two_terms(plane)
            parts.append(dot(high, yh_ref[...]) + dot(low, yh_ref[...]) + dot(high, yl_ref[...]))
        cos_r, sin_r = parts[0][:, :half], parts[0][:, half:]
        cos_i, sin_i = parts[1][:, :half], parts[1][:, half:]
        zero_r = jnp.where(lane == 0, 0.0, sin_r)
        zero_i = jnp.where(lane == 0, 0.0, sin_i)
        real = jnp.concatenate([cos_r - zero_i, jnp.where(lane == 0, sin_r, cos_r + sin_i)], axis=1)
        imag = jnp.concatenate([cos_i + zero_r, jnp.where(lane == 0, sin_i, cos_i - sin_r)], axis=1)
        high, low = two_terms(jnp.concatenate([real, imag], axis=1))
        both = dot(xh_ref[...], high) + dot(xh_ref[...], low) + dot(xl_ref[...], high)
        rows = half + 8
        cos_r, cos_i = both[:rows, :grid], both[:rows, grid:]
        sin_r, sin_i = both[rows:, :grid], both[rows:, grid:]
        fields = ((cos_r - sin_i, cos_r + sin_i), (cos_i + sin_r, cos_i - sin_r))
        for c in range(2):
            plus, minus = fields[c]
            for side in range(grid // LANES):
                cut = slice(side * LANES, (side + 1) * LANES)
                place = 2 * z + c
                rows16[side, pl.ds(place, half, stride=2 * width), :] = plus[:half, cut]
                rows16[side, pl.ds(half * 2 * width + place, half, stride=2 * width), :] = minus[1 : half + 1, cut]
        return carry

    lax.fori_loop(0, width, one, 0)
    for d in range(slabs):
        if d < slabs // 2:
            start = slab * d
        else:
            start = half + grid - slab * d - slab
        size = slab * 2 * width
        for side in range(grid // LANES):
            block = rows16[side, start * 2 * width : start * 2 * width + size, :]
            out_ref[d, :, :, side * LANES : (side + 1) * LANES] = block.astype(BF16).reshape(slab, 2 * width, LANES)


def planes_call(data, table_y, table_x, slabs):
    sides, values, grid, _ = data.shape
    step = min(16, values)
    slab = grid // slabs
    fixed = lambda i: (0, 0)
    return pl.pallas_call(
        functools.partial(plane_kernel, slabs),
        grid=(values // step,),
        out_shape=jax.ShapeDtypeStruct((slabs, slab, values, grid), BF16),
        in_specs=[
            pl.BlockSpec((sides, step, grid, LANES), lambda i: (0, i, 0, 0)),
            pl.BlockSpec(table_y[0].shape, fixed),
            pl.BlockSpec(table_y[1].shape, fixed),
            pl.BlockSpec(table_x[0].shape, fixed),
            pl.BlockSpec(table_x[1].shape, fixed),
        ],
        out_specs=pl.BlockSpec((slabs, slab, step, grid), lambda i: (0, 0, i, 0)),
        scratch_shapes=[VMEM((sides, grid * step, LANES), F32)],
        compiler_params=pltpu.CompilerParams(vmem_limit_bytes=56 * 2**20),
        name="planes",
    )(data, *table_y, *table_x)


def volume_kernel(flip_ref, data_ref, restore_ref, zh_ref, zl_ref, out_ref):
    slabs, _, width, grid = data_ref.shape
    block = data_ref[...].reshape(slabs * width, grid)
    turned = dot_t(restore_ref[...], block).astype(BF16)
    out_ref[0] = dot(turned, zh_ref[...]) + dot(turned, zl_ref[...])


def volume_call(flip, data, restore, table_z):
    slabs, slab, width, grid = data.shape
    fixed = lambda i, flip_ref: (0, 0)
    return pl.pallas_call(
        volume_kernel,
        grid_spec=pltpu.PrefetchScalarGridSpec(
            num_scalar_prefetch=1,
            grid=(slab,),
            in_specs=[
                pl.BlockSpec((slabs, 1, width, grid), lambda i, flip_ref: (0, i, 0, 0)),
                pl.BlockSpec(restore.shape, fixed),
                pl.BlockSpec(table_z[0].shape, fixed),
                pl.BlockSpec(table_z[1].shape, fixed),
            ],
            out_specs=pl.BlockSpec(
                (1, grid, grid), lambda i, flip_ref: (jnp.where(flip_ref[0] == 1, slab - 1 - i, i), 0, 0)
            ),
        ),
        out_shape=jax.ShapeDtypeStruct((slab, grid, grid), F32),
        compiler_params=pltpu.CompilerParams(vmem_limit_bytes=48 * 2**20),
        name="volume",
    )(flip, data, restore, *table_z)


def sorted_points(interp_cells, grid):
    dirs = interp_cells.shape[0]
    points = dirs * grid
    base = interp_cells[:, 0, :].T.reshape(-1)
    row = (base // grid + 1) & (grid - 1)
    key = (row << 23) | ((base & (grid - 1)) << 15) | jnp.arange(points, dtype=jnp.int32)
    key = lax.sort(key, is_stable=False)
    rows = jnp.arange(grid, dtype=jnp.int32)
    count = jnp.sum((row[None, :] == rows[:, None]).astype(jnp.int32), axis=1)
    first = jnp.cumsum(count) - count
    chunks = jnp.maximum((count + (CHUNK - 1)) // CHUNK, 1)
    ends = jnp.cumsum(chunks)
    most = grid + points // CHUNK + 2
    number = jnp.arange(most, dtype=jnp.int32)
    chunk_row = jnp.minimum(jnp.sum((ends[None, :] <= number[:, None]).astype(jnp.int32), axis=1), grid - 1)
    mine = (rows[None, :] == chunk_row[:, None]).astype(jnp.int32)
    shift = first - (ends - chunks) * CHUNK
    chunk_start = jnp.sum(mine * shift[None, :], axis=1) + number * CHUNK
    chunk_start = jnp.where(number < ends[-1], chunk_start, points)
    pairs = ((ends[-1] + 1) // 2).reshape(1)
    point = jnp.concatenate([key & (points - 1), jnp.zeros((CHUNK,), jnp.int32)])
    keys = jnp.concatenate([key, jnp.full((8 * LANES,), -1, jnp.int32)]).reshape(-1, LANES)
    return pairs, chunk_row, chunk_start, point, keys


def shards(images, projections, assignment, interp_cells, interp_weights):
    class_count = lax.axis_size("cls")
    slab_count = lax.axis_size("vol")
    local_count, grid = images.shape[0], images.shape[1]
    dirs = projections.shape[1]
    slab = grid // slab_count
    width = 2 * slab
    halves = LANES // width
    capacity = 2 * local_count // class_count
    steps = 16 // capacity
    groups = grid // (halves * steps)

    classes = assignment[:, 0]
    onehot = (classes[:, None] == jnp.arange(class_count, dtype=jnp.int32)[None, :]).astype(jnp.int32)
    before = jnp.cumsum(onehot, axis=0) - onehot
    slot_index = classes * capacity + jnp.sum(before * onehot, axis=1)
    slot_table = jnp.full((class_count * capacity,), local_count, jnp.int32)
    slot_table = slot_table.at[slot_index].set(jnp.arange(local_count, dtype=jnp.int32))
    split = images.reshape(local_count, slab_count, slab, 2, halves, groups, steps)
    split = jnp.transpose(split, (0, 1, 5, 6, 4, 2, 3)).reshape(local_count, slab_count, groups, steps, LANES)
    outgoing = split.at[slot_table].get(mode="fill", fill_value=0)
    outgoing = outgoing.reshape(class_count, capacity, slab_count, groups, steps, LANES)
    outgoing = jnp.transpose(outgoing, (0, 2, 3, 4, 1, 5))
    outgoing = outgoing.reshape(class_count * slab_count, groups, steps * capacity, LANES)
    arrived = lax.all_to_all(outgoing, ("cls", "vol"), split_axis=0, concat_axis=0, tiled=True)

    references = projections[0].reshape(dirs, slab, 2, halves, groups, steps)
    references = jnp.transpose(references, (4, 5, 0, 3, 1, 2)).reshape(groups, steps * dirs, LANES)
    weights = interp_weights.reshape(dirs, 4, halves, groups, steps)
    weights = jnp.transpose(weights, (3, 4, 0, 2, 1)).reshape(groups, steps * dirs, 4 * halves)
    weights = jnp.pad(weights, ((0, 0), (0, 0), (0, LANES - 4 * halves)))
    pairs, chunk_row, chunk_start, point, keys = sorted_points(interp_cells, grid)
    table_y, table_x, table_z, restore = tables(grid, slab_count)

    partial_value = scores_call(arrived, references, capacity, dirs)
    copies = jnp.broadcast_to(partial_value[None], (slab_count,) + partial_value.shape)
    parts = lax.all_to_all(copies, "vol", split_axis=0, concat_axis=0, tiled=True)
    plane = scatter_call(
        pairs, chunk_row, chunk_start, point, parts, arrived, weights, keys, capacity, width, grid
    )
    plane = plane.reshape(grid // LANES, width, grid, LANES)
    sent = planes_call(plane, table_y, table_x, slab_count)
    received = lax.all_to_all(sent, "vol", split_axis=0, concat_axis=0, tiled=True)
    flip = (lax.axis_index("vol") >= slab_count // 2).astype(jnp.int32).reshape(1)
    return volume_call(flip, received, restore, table_z)[None]


def solution(mesh):
    in_specs = (
        P(("cls", "vol"), None, None, None),
        P("cls", None, "vol", None, None),
        P(("cls", "vol"), None),
        P(),
        P(),
    )
    out_specs = P("cls", "vol", None, None)
    return jax.shard_map(shards, mesh=mesh, in_specs=in_specs, out_specs=out_specs, check_vma=False)
```

```python
import functools
import math

import jax
import jax.numpy as jnp
import numpy as np
from jax import lax
from jax.experimental import pallas as pl
from jax.experimental.pallas import tpu as pltpu
from jax.sharding import PartitionSpec as P

F32 = jnp.float32
BF16 = jnp.bfloat16
LANES = 128
HALF = 64
CHUNK = 128
VMEM = pltpu.VMEM


def split_table(table):
    high = table.astype(jnp.bfloat16)
    low = (table - high.astype(np.float64)).astype(jnp.bfloat16)
    return high, low


def tables(grid, slabs):
    half = grid // 2
    scale = 1.0 / math.sqrt(grid)
    index = np.arange(grid)
    angle = 2.0 * np.pi / grid
    phase = (index[:, None] * np.arange(half)[None, :]) % grid
    cosine = np.cos(phase * angle)
    sine = np.sin(phase * angle)
    sine[:, 0] = np.cos(((index * half) % grid) * angle)
    table_y = np.concatenate([cosine, sine], axis=1) * scale
    rows = half + 8
    phase = (np.arange(rows)[:, None] * index[None, :]) % grid
    live = (np.arange(rows) <= half)[:, None]
    table_x = np.concatenate([np.cos(phase * angle) * live, np.sin(phase * angle) * live], axis=0) * scale
    phase = (index[:, None] * index[None, :]) % grid
    table_z = np.stack([np.cos(phase * angle), -np.sin(phase * angle)], axis=1).reshape(2 * grid, grid) * scale
    order = np.concatenate([np.arange(half), [half], np.arange(grid - 1, half, -1)])
    restore = (order[None, :] == index[:, None]).astype(jnp.bfloat16)
    return split_table(table_y), split_table(table_x), split_table(table_z), restore


def dot(a, b):
    return jnp.dot(a, b, preferred_element_type=F32)


def dot_t(a, b):
    return lax.dot_general(a, b, (((1,), (1,)), ((), ())), preferred_element_type=F32)


def two_terms(value):
    high = value.astype(BF16)
    low = (value - high.astype(F32)).astype(BF16)
    return high, low


def route_kernel(cap, slabs, width, classes_ref, images_ref, eye_ref, order_ref, out_ref, lines):
    count, _, _, grid = images_ref.shape
    halves = LANES // width
    piece = grid // halves
    lane = lax.broadcasted_iota(jnp.int32, (piece, LANES), 1)
    lines[...] = jnp.zeros_like(lines)

    def place(p, carry):
        own = classes_ref[p, 0]
        rank = 0
        for q in range(count):
            rank = rank + jnp.where((classes_ref[q, 0] == own) & (q < p), 1, 0)
        image = images_ref[p].reshape(-1, grid)
        turned = dot(dot_t(eye_ref[...], image).astype(BF16), order_ref[...])
        for w in range(slabs):
            tile = w * width // LANES * LANES
            block = jnp.zeros((piece, LANES), F32)
            for h in range(halves):
                part = turned[h * piece : (h + 1) * piece, tile : tile + LANES]
                shift = (h * width - (w * width - tile)) % LANES
                part = part if shift == 0 else pltpu.roll(part, shift, 1)
                block = jnp.where((lane >= h * width) & (lane < (h + 1) * width), part, block)
            lines[own * slabs + w, pl.ds(rank, piece, stride=cap), :] = block
        return carry

    lax.fori_loop(0, count, place, 0)
    out_ref[...] = lines[...].astype(BF16).reshape(out_ref.shape)


def route_call(images, assignment, eye, order, class_count, slabs, width, cap):
    count, grid = images.shape[0], images.shape[1]
    rows = grid // (LANES // width) * cap
    vmem = pl.BlockSpec(memory_space=VMEM)
    return pl.pallas_call(
        functools.partial(route_kernel, cap, slabs, width),
        out_shape=jax.ShapeDtypeStruct((class_count * slabs, rows // 16, 16, LANES), BF16),
        in_specs=[pl.BlockSpec(memory_space=pltpu.SMEM)] + [vmem] * 3,
        out_specs=vmem,
        scratch_shapes=[VMEM((class_count * slabs, rows, LANES), F32)],
        compiler_params=pltpu.CompilerParams(vmem_limit_bytes=48 * 2**20),
        name="route",
    )(assignment, images, eye, order)


def score_kernel(cap, dirs, images_ref, refs_ref, out_ref, sums):
    sources, groups, rows16, _ = images_ref.shape
    rows = sources * rows16
    steps = rows16 // cap
    sums[...] = jnp.zeros_like(sums)

    def step(g, carry):
        blocks = [images_ref[:, pl.ds(2 * g + i, 1), :, :].reshape(rows, LANES) for i in range(2)]
        refs = [refs_ref[2 * g + i] for i in range(2)]
        sums[...] += dot_t(jnp.concatenate(refs, axis=1), jnp.concatenate(blocks, axis=1))
        return carry

    lax.fori_loop(0, groups // 2, step, 0)
    column = lax.broadcasted_iota(jnp.int32, (dirs, rows), 1)
    part = (column & (rows16 - 1)) // cap
    kept = jnp.zeros((dirs, rows), F32)
    for j in range(steps):
        kept = kept + jnp.where(part == j, sums[j * dirs : (j + 1) * dirs, :], 0.0)
    slots = sources * cap
    row_id = lax.broadcasted_iota(jnp.int32, (rows, slots), 0)
    slot_id = lax.broadcasted_iota(jnp.int32, (rows, slots), 1)
    gather = (row_id // rows16 * cap + row_id % cap) == slot_id
    out_ref[...] = jnp.dot(
        kept, gather.astype(F32), preferred_element_type=F32, precision=lax.Precision.HIGHEST
    )


def scores_call(images, refs, cap, dirs):
    sources, groups, rows16, _ = images.shape
    return pl.pallas_call(
        functools.partial(score_kernel, cap, dirs),
        out_shape=jax.ShapeDtypeStruct((dirs, sources * cap), F32),
        in_specs=[pl.BlockSpec(memory_space=VMEM)] * 2,
        out_specs=pl.BlockSpec(memory_space=VMEM),
        scratch_shapes=[VMEM((refs.shape[1], sources * rows16), F32)],
        compiler_params=pltpu.CompilerParams(vmem_limit_bytes=48 * 2**20),
        name="scores",
    )(images, refs)


def scatter_kernel(
    cap,
    width,
    grid,
    total_ref,
    chunk_row_ref,
    chunk_start_ref,
    chunk_size_ref,
    point_ref,
    parts_ref,
    images_ref,
    weights_ref,
    out_ref,
    values,
    buffer_a,
    buffer_b,
    sums,
    spread,
):
    sources, groups, rows16, _ = images_ref.shape
    rows = sources * rows16
    steps = rows16 // cap
    dirs, slots = parts_ref.shape[1:]
    joined = steps * dirs
    halves = LANES // width

    total = parts_ref[0]
    for i in range(1, parts_ref.shape[0]):
        total = total + parts_ref[i]
    expo = jnp.exp(total - jnp.max(total, axis=0, keepdims=True))
    posterior = (expo / jnp.sum(expo, axis=0, keepdims=True)).astype(BF16)
    slot_id = lax.broadcasted_iota(jnp.int32, (slots, rows), 0)
    row_id = lax.broadcasted_iota(jnp.int32, (slots, rows), 1)
    repeat = ((row_id // rows16 * cap + row_id % cap) == slot_id).astype(F32).astype(BF16)
    wide = dot(posterior, repeat)
    part = (lax.broadcasted_iota(jnp.int32, (dirs, rows), 1) & (rows16 - 1)) // cap
    for j in range(steps):
        spread[j * dirs : (j + 1) * dirs, :] = jnp.where(part == j, wide, 0.0).astype(BF16)

    lane_j = lax.broadcasted_iota(jnp.int32, (joined, LANES), 1)

    def average(g, carry):
        block = images_ref[:, pl.ds(g, 1), :, :].reshape(rows, LANES)
        mean = dot(spread[...], block)
        weight = weights_ref[g]
        for h in range(halves):
            shifted = mean if h == 0 else pltpu.roll(mean, LANES - h * width, 1)
            behind = pltpu.roll(weight, HALF - 8 * h, 1)
            start = pl.multiple_of((h * groups + g) * joined, joined)
            values[pl.ds(start, joined), :] = jnp.where(lane_j < HALF, shifted, behind)
        return carry

    lax.fori_loop(0, groups, average, 0)

    buffer_a[...] = jnp.zeros_like(buffer_a)
    buffer_b[...] = jnp.zeros_like(buffer_b)
    sums[...] = jnp.zeros_like(sums)

    place = lax.broadcasted_iota(jnp.int32, (CHUNK, LANES), 0)
    lane = lax.broadcasted_iota(jnp.int32, (CHUNK, grid), 1)
    at_y = lane.astype(F32).astype(BF16)
    at_next = ((lane + (grid - 1)) & (grid - 1)).astype(F32).astype(BF16)
    one = jnp.ones((CHUNK, grid), BF16)
    none = jnp.zeros((CHUNK, grid), BF16)

    def fetch(c, buffer):
        start = chunk_start_ref[c]
        for i in range(CHUNK):
            buffer[pl.ds(i, 1), :] = values[pl.ds(point_ref[start + i], 1), :]

    def put(x, plane):
        for side in range(grid // LANES):
            out_ref[side, pl.ds(x, width, stride=grid), :] = plane[:, side * LANES : (side + 1) * LANES]

    def work(c, buffer):
        row = chunk_row_ref[c]
        before = chunk_row_ref[jnp.maximum(c - 1, 0)]
        data = buffer[...]
        y = jnp.broadcast_to(data[:, HALF + 4 : HALF + 5], (CHUNK, LANES))
        y = jnp.where(place < chunk_size_ref[c], y, -1.0).astype(BF16)
        y = jnp.concatenate([y] * (grid // LANES), axis=1)
        hot = jnp.concatenate([jnp.where(at_y == y, one, none), jnp.where(at_next == y, one, none)], axis=0)
        turned = data.T
        mean = turned[:width]
        weight = [jnp.broadcast_to(turned[HALF + j : HALF + j + 1], (width, CHUNK)) for j in range(4)]
        operand = jnp.concatenate(
            [
                jnp.concatenate([mean * weight[0], mean * weight[2]], axis=1),
                jnp.concatenate([mean * weight[1], mean * weight[3]], axis=1),
            ],
            axis=0,
        )
        high, low = two_terms(operand)
        result = dot(jnp.concatenate([high, low], axis=0), hot)
        result = result[: 2 * width] + result[2 * width :]
        same = row == before
        old_low, old_high = sums[:width], sums[width:]
        put((before + (grid - 1)) & (grid - 1), old_low)
        sums[:width] = result[:width] + jnp.where(same, old_low, old_high)
        sums[width:] = result[width:] + jnp.where(same, old_high, 0.0)

    fetch(0, buffer_a)

    def pair(m, carry):
        fetch(2 * m + 1, buffer_b)
        work(2 * m, buffer_a)
        fetch(2 * m + 2, buffer_a)
        work(2 * m + 1, buffer_b)
        return carry

    lax.fori_loop(0, total_ref[0], pair, 0)
    put(grid - 2, sums[:width])
    for side in range(grid // LANES):
        wrapped = pl.ds(grid - 1, width, stride=grid)
        cut = slice(side * LANES, (side + 1) * LANES)
        out_ref[side, wrapped, :] = out_ref[side, wrapped, :] + sums[width:, cut]


def scatter_call(plan, parts, images, weights, cap, width, grid):
    sources, groups, rows16, _ = images.shape
    dirs = parts.shape[1]
    points = dirs * grid
    smem = pl.BlockSpec(memory_space=pltpu.SMEM)
    vmem = pl.BlockSpec(memory_space=VMEM)
    return pl.pallas_call(
        functools.partial(scatter_kernel, cap, width, grid),
        out_shape=jax.ShapeDtypeStruct((grid // LANES, width * grid, LANES), F32),
        in_specs=[smem] * 5 + [vmem] * 3,
        out_specs=vmem,
        scratch_shapes=[
            VMEM((points, LANES), F32),
            VMEM((CHUNK, LANES), F32),
            VMEM((CHUNK, LANES), F32),
            VMEM((2 * width, grid), F32),
            VMEM((weights.shape[1], sources * rows16), BF16),
        ],
        compiler_params=pltpu.CompilerParams(vmem_limit_bytes=60 * 2**20),
        name="scatter",
    )(*plan, parts, images, weights)


def plane_kernel(slabs, data_ref, yh_ref, yl_ref, xh_ref, xl_ref, out_ref, rows16):
    width, grid = data_ref.shape[1] // 2, data_ref.shape[2]
    half = grid // 2
    slab = grid // slabs
    lane = lax.broadcasted_iota(jnp.int32, (grid, half), 1)

    def one(z, carry):
        parts = []
        for r in range(2):
            plane = jnp.concatenate([data_ref[side, 2 * z + r] for side in range(grid // LANES)], axis=1)
            high, low = two_terms(plane)
            parts.append(dot(high, yh_ref[...]) + dot(low, yh_ref[...]) + dot(high, yl_ref[...]))
        cos_r, sin_r = parts[0][:, :half], parts[0][:, half:]
        cos_i, sin_i = parts[1][:, :half], parts[1][:, half:]
        zero_r = jnp.where(lane == 0, 0.0, sin_r)
        zero_i = jnp.where(lane == 0, 0.0, sin_i)
        real = jnp.concatenate([cos_r - zero_i, jnp.where(lane == 0, sin_r, cos_r + sin_i)], axis=1)
        imag = jnp.concatenate([cos_i + zero_r, jnp.where(lane == 0, sin_i, cos_i - sin_r)], axis=1)
        high, low = two_terms(jnp.concatenate([real, imag], axis=1))
        both = dot(xh_ref[...], high) + dot(xh_ref[...], low) + dot(xl_ref[...], high)
        rows = half + 8
        cos_r, cos_i = both[:rows, :grid], both[:rows, grid:]
        sin_r, sin_i = both[rows:, :grid], both[rows:, grid:]
        fields = ((cos_r - sin_i, cos_r + sin_i), (cos_i + sin_r, cos_i - sin_r))
        for c in range(2):
            plus, minus = fields[c]
            for side in range(grid // LANES):
                cut = slice(side * LANES, (side + 1) * LANES)
                place = 2 * z + c
                rows16[side, pl.ds(place, half, stride=2 * width), :] = plus[:half, cut]
                rows16[side, pl.ds(half * 2 * width + place, half, stride=2 * width), :] = minus[1 : half + 1, cut]
        return carry

    lax.fori_loop(0, width, one, 0)
    for d in range(slabs):
        if d < slabs // 2:
            start = slab * d
        else:
            start = half + grid - slab * d - slab
        size = slab * 2 * width
        for side in range(grid // LANES):
            block = rows16[side, start * 2 * width : start * 2 * width + size, :]
            out_ref[d, :, :, side * LANES : (side + 1) * LANES] = block.astype(BF16).reshape(slab, 2 * width, LANES)


def planes_call(data, table_y, table_x, slabs):
    sides, values, grid, _ = data.shape
    step = min(16, values)
    slab = grid // slabs
    fixed = lambda i: (0, 0)
    return pl.pallas_call(
        functools.partial(plane_kernel, slabs),
        grid=(values // step,),
        out_shape=jax.ShapeDtypeStruct((slabs, slab, values, grid), BF16),
        in_specs=[
            pl.BlockSpec((sides, step, grid, LANES), lambda i: (0, i, 0, 0)),
            pl.BlockSpec(table_y[0].shape, fixed),
            pl.BlockSpec(table_y[1].shape, fixed),
            pl.BlockSpec(table_x[0].shape, fixed),
            pl.BlockSpec(table_x[1].shape, fixed),
        ],
        out_specs=pl.BlockSpec((slabs, slab, step, grid), lambda i: (0, 0, i, 0)),
        scratch_shapes=[VMEM((sides, grid * step, LANES), F32)],
        compiler_params=pltpu.CompilerParams(vmem_limit_bytes=56 * 2**20),
        name="planes",
    )(data, *table_y, *table_x)


def volume_kernel(flip_ref, data_ref, restore_ref, zh_ref, zl_ref, out_ref):
    slabs, span, width, grid = data_ref.shape
    for i in range(span):
        block = data_ref[:, i].reshape(slabs * width, grid)
        turned = dot_t(restore_ref[...], block).astype(BF16)
        value = dot(turned, zh_ref[...]) + dot(turned, zl_ref[...])
        out_ref[jnp.where(flip_ref[0] == 1, span - 1 - i, i)] = value


def volume_call(flip, data, restore, table_z):
    slabs, slab, width, grid = data.shape
    span = 4
    steps = slab // span
    fixed = lambda i, flip_ref: (0, 0)
    return pl.pallas_call(
        volume_kernel,
        grid_spec=pltpu.PrefetchScalarGridSpec(
            num_scalar_prefetch=1,
            grid=(steps,),
            in_specs=[
                pl.BlockSpec((slabs, span, width, grid), lambda i, flip_ref: (0, i, 0, 0)),
                pl.BlockSpec(restore.shape, fixed),
                pl.BlockSpec(table_z[0].shape, fixed),
                pl.BlockSpec(table_z[1].shape, fixed),
            ],
            out_specs=pl.BlockSpec(
                (span, grid, grid), lambda i, flip_ref: (jnp.where(flip_ref[0] == 1, steps - 1 - i, i), 0, 0)
            ),
        ),
        out_shape=jax.ShapeDtypeStruct((slab, grid, grid), F32),
        compiler_params=pltpu.CompilerParams(vmem_limit_bytes=48 * 2**20),
        name="volume",
    )(flip, data, restore, *table_z)


def sorted_points(interp_cells, grid):
    dirs = interp_cells.shape[0]
    points = dirs * grid
    base = interp_cells[:, 0, :].T.reshape(-1)
    row = (base // grid + 1) & (grid - 1)
    key = row * points + jnp.arange(points, dtype=jnp.int32)
    key = lax.sort(key, is_stable=False)
    rows = jnp.arange(grid, dtype=jnp.int32)
    count = jnp.sum((row[None, :] == rows[:, None]).astype(jnp.int32), axis=1)
    first = jnp.cumsum(count) - count
    chunks = jnp.maximum((count + (CHUNK - 1)) // CHUNK, 1)
    ends = jnp.cumsum(chunks)
    most = grid + points // CHUNK + 2
    number = jnp.arange(most, dtype=jnp.int32)
    chunk_row = jnp.minimum(jnp.sum((ends[None, :] <= number[:, None]).astype(jnp.int32), axis=1), grid - 1)
    mine = (rows[None, :] == chunk_row[:, None]).astype(jnp.int32)
    shift = first - (ends - chunks) * CHUNK
    chunk_start = jnp.sum(mine * shift[None, :], axis=1) + number * CHUNK
    row_end = jnp.sum(mine * (first + count)[None, :], axis=1)
    used = number < ends[-1]
    chunk_size = jnp.where(used, jnp.clip(row_end - chunk_start, 0, CHUNK), 0)
    chunk_start = jnp.where(used, chunk_start, points)
    pairs = ((ends[-1] + 1) // 2).reshape(1)
    point = jnp.concatenate([key & (points - 1), jnp.zeros((CHUNK,), jnp.int32)])
    return pairs, chunk_row, chunk_start, chunk_size, point


def shards(images, projections, assignment, interp_cells, interp_weights):
    class_count = lax.axis_size("cls")
    slab_count = lax.axis_size("vol")
    local_count, grid = images.shape[0], images.shape[1]
    dirs = projections.shape[1]
    slab = grid // slab_count
    width = 2 * slab
    halves = LANES // width
    capacity = 2 * local_count // class_count
    steps = 16 // capacity
    groups = grid // (halves * steps)

    eye = jnp.asarray(np.eye(grid), BF16)
    order = jnp.asarray(np.eye(2 * grid), BF16)
    outgoing = route_call(images, assignment, eye, order, class_count, slab_count, width, capacity)
    arrived = lax.all_to_all(outgoing, ("cls", "vol"), split_axis=0, concat_axis=0, tiled=True)

    references = projections[0].reshape(dirs, slab, 2, halves, groups, steps)
    references = jnp.transpose(references, (4, 5, 0, 3, 1, 2)).reshape(groups, steps * dirs, LANES)
    corner_y = (interp_cells[:, 0:1, :] & (grid - 1)).astype(F32)
    weights = jnp.concatenate([interp_weights, corner_y, jnp.zeros((dirs, 3, grid), F32)], axis=1)
    weights = weights.reshape(dirs, 8, halves, groups, steps)
    weights = jnp.transpose(weights, (3, 4, 0, 2, 1)).reshape(groups, steps * dirs, 8 * halves)
    weights = jnp.pad(weights, ((0, 0), (0, 0), (0, LANES - 8 * halves)))
    plan = sorted_points(interp_cells, grid)
    table_y, table_x, table_z, restore = tables(grid, slab_count)

    partial_value = scores_call(arrived, references, capacity, dirs)
    copies = jnp.broadcast_to(partial_value[None], (slab_count,) + partial_value.shape)
    parts = lax.all_to_all(copies, "vol", split_axis=0, concat_axis=0, tiled=True)
    plane = scatter_call(plan, parts, arrived, weights, capacity, width, grid)
    plane = plane.reshape(grid // LANES, width, grid, LANES)
    sent = planes_call(plane, table_y, table_x, slab_count)
    received = lax.all_to_all(sent, "vol", split_axis=0, concat_axis=0, tiled=True)
    flip = (lax.axis_index("vol") >= slab_count // 2).astype(jnp.int32).reshape(1)
    return volume_call(flip, received, restore, table_z)[None]


def solution(mesh):
    in_specs = (
        P(("cls", "vol"), None, None, None),
        P("cls", None, "vol", None, None),
        P(("cls", "vol"), None),
        P(),
        P(),
    )
    out_specs = P("cls", "vol", None, None)
    return jax.shard_map(shards, mesh=mesh, in_specs=in_specs, out_specs=out_specs, check_vma=False)
```

```python
import functools
import math

import jax
import jax.numpy as jnp
import numpy as np
from jax import lax
from jax.experimental import pallas as pl
from jax.experimental.pallas import tpu as pltpu
from jax.sharding import PartitionSpec as P

F32 = jnp.float32
BF16 = jnp.bfloat16
LANES = 128
HALF = 64
CHUNK = 128
PAD = 8
VMEM = pltpu.VMEM


def split_table(table):
    high = table.astype(jnp.bfloat16)
    low = (table - high.astype(np.float64)).astype(jnp.bfloat16)
    return high, low


def plane_pairs(grid, slabs):
    slab = grid // slabs
    pairs = []
    for w in range(slabs):
        if w < slabs // 2:
            first = slab * w + 1
        else:
            first = slab * (slabs - 1 - w) + slab // 2 + 1
        for i in range(slab // 2):
            z = first + i
            pairs.append((z, 0 if 2 * z == grid else grid - z))
    return np.array(pairs).reshape(slabs, slab // 2, 2)


def tables(grid, slabs):
    half = grid // 2
    scale = 1.0 / math.sqrt(grid)
    index = np.arange(grid)
    angle = 2.0 * np.pi / grid
    phase = (index[:, None] * np.arange(half)[None, :]) % grid
    cosine = np.cos(phase * angle)
    sine = np.sin(phase * angle)
    sine[:, 0] = np.cos(((index * half) % grid) * angle)
    table_y = np.concatenate([cosine, sine], axis=1) * scale
    rows = half + 8
    phase = (np.arange(rows)[:, None] * index[None, :]) % grid
    live = (np.arange(rows) <= half)[:, None]
    table_x = np.concatenate([np.cos(phase * angle) * live, np.sin(phase * angle) * live], axis=0) * scale
    z = plane_pairs(grid, slabs)[:, :, 0].reshape(-1)
    phase = (z[:, None] * index[None, :]) % grid
    single = (2 * z == grid)[:, None]
    for_sum = np.where(single, 1.0, np.cos(phase * angle))
    for_difference = np.where(single, np.cos(phase * angle), -np.sin(phase * angle))
    table_z = np.stack([for_sum, for_difference], axis=1).reshape(grid, grid) * scale
    order = np.concatenate([np.arange(half), [half], np.arange(grid - 1, half, -1)])
    restore = (order[None, :] == index[:, None]).astype(jnp.bfloat16)
    return split_table(table_y), split_table(table_x), split_table(table_z), restore


def lane_order(grid, slabs):
    rows = plane_pairs(grid, slabs).transpose(0, 2, 1).reshape(-1)
    source = (2 * rows[:, None] + np.arange(2)[None, :]).reshape(-1)
    return (np.arange(2 * grid)[:, None] == source[None, :]).astype(jnp.bfloat16)


def dot(a, b):
    return jnp.dot(a, b, preferred_element_type=F32)


def dot_t(a, b):
    return lax.dot_general(a, b, (((1,), (1,)), ((), ())), preferred_element_type=F32)


def two_terms(value):
    high = value.astype(BF16)
    low = (value - high.astype(F32)).astype(BF16)
    return high, low


def route_kernel(cap, slabs, width, classes_ref, images_ref, eye_ref, order_ref, out_ref, lines):
    count, _, _, grid = images_ref.shape
    halves = LANES // width
    piece = grid // halves
    lane = lax.broadcasted_iota(jnp.int32, (piece, LANES), 1)
    lines[...] = jnp.zeros_like(lines)

    def place(p, carry):
        own = classes_ref[p, 0]
        rank = 0
        for q in range(count):
            rank = rank + jnp.where((classes_ref[q, 0] == own) & (q < p), 1, 0)
        image = images_ref[p].reshape(-1, grid)
        turned = dot(dot_t(eye_ref[...], image).astype(BF16), order_ref[...])
        for w in range(slabs):
            tile = w * width // LANES * LANES
            block = jnp.zeros((piece, LANES), F32)
            for h in range(halves):
                part = turned[h * piece : (h + 1) * piece, tile : tile + LANES]
                shift = (h * width - (w * width - tile)) % LANES
                part = part if shift == 0 else pltpu.roll(part, shift, 1)
                block = jnp.where((lane >= h * width) & (lane < (h + 1) * width), part, block)
            lines[own * slabs + w, pl.ds(rank, piece, stride=cap), :] = block
        return carry

    lax.fori_loop(0, count, place, 0)
    out_ref[...] = lines[...].astype(BF16).reshape(out_ref.shape)


def route_call(images, assignment, eye, order, class_count, slabs, width, cap):
    count, grid = images.shape[0], images.shape[1]
    rows = grid // (LANES // width) * cap
    vmem = pl.BlockSpec(memory_space=VMEM)
    return pl.pallas_call(
        functools.partial(route_kernel, cap, slabs, width),
        out_shape=jax.ShapeDtypeStruct((class_count * slabs, rows // 16, 16, LANES), BF16),
        in_specs=[pl.BlockSpec(memory_space=pltpu.SMEM)] + [vmem] * 3,
        out_specs=vmem,
        scratch_shapes=[VMEM((class_count * slabs, rows, LANES), F32)],
        compiler_params=pltpu.CompilerParams(vmem_limit_bytes=48 * 2**20),
        name="route",
    )(assignment, images, eye, order)


def score_kernel(cap, dirs, images_ref, refs_ref, out_ref, sums):
    sources, groups, rows16, _ = images_ref.shape
    rows = sources * rows16
    steps = rows16 // cap
    sums[...] = jnp.zeros_like(sums)

    def step(g, carry):
        blocks = [images_ref[:, pl.ds(2 * g + i, 1), :, :].reshape(rows, LANES) for i in range(2)]
        refs = [refs_ref[2 * g + i] for i in range(2)]
        sums[...] += dot_t(jnp.concatenate(refs, axis=1), jnp.concatenate(blocks, axis=1))
        return carry

    lax.fori_loop(0, groups // 2, step, 0)
    column = lax.broadcasted_iota(jnp.int32, (dirs, rows), 1)
    part = (column & (rows16 - 1)) // cap
    kept = jnp.zeros((dirs, rows), F32)
    for j in range(steps):
        kept = kept + jnp.where(part == j, sums[j * dirs : (j + 1) * dirs, :], 0.0)
    slots = sources * cap
    row_id = lax.broadcasted_iota(jnp.int32, (rows, slots), 0)
    slot_id = lax.broadcasted_iota(jnp.int32, (rows, slots), 1)
    gather = (row_id // rows16 * cap + row_id % cap) == slot_id
    out_ref[...] = jnp.dot(
        kept, gather.astype(F32), preferred_element_type=F32, precision=lax.Precision.HIGHEST
    )


def scores_call(images, refs, cap, dirs):
    sources, groups, rows16, _ = images.shape
    return pl.pallas_call(
        functools.partial(score_kernel, cap, dirs),
        out_shape=jax.ShapeDtypeStruct((dirs, sources * cap), F32),
        in_specs=[pl.BlockSpec(memory_space=VMEM)] * 2,
        out_specs=pl.BlockSpec(memory_space=VMEM),
        scratch_shapes=[VMEM((refs.shape[1], sources * rows16), F32)],
        compiler_params=pltpu.CompilerParams(vmem_limit_bytes=48 * 2**20),
        name="scores",
    )(images, refs)


def scatter_kernel(
    cap,
    width,
    grid,
    total_ref,
    chunk_row_ref,
    chunk_start_ref,
    chunk_size_ref,
    point_ref,
    parts_ref,
    images_ref,
    weights_ref,
    out_ref,
    values,
    buffer_a,
    buffer_b,
    sums,
    spread,
):
    sources, groups, rows16, _ = images_ref.shape
    rows = sources * rows16
    steps = rows16 // cap
    dirs, slots = parts_ref.shape[1:]
    joined = steps * dirs
    halves = LANES // width

    total = parts_ref[0]
    for i in range(1, parts_ref.shape[0]):
        total = total + parts_ref[i]
    expo = jnp.exp(total - jnp.max(total, axis=0, keepdims=True))
    posterior = (expo / jnp.sum(expo, axis=0, keepdims=True)).astype(BF16)
    slot_id = lax.broadcasted_iota(jnp.int32, (slots, rows), 0)
    row_id = lax.broadcasted_iota(jnp.int32, (slots, rows), 1)
    repeat = ((row_id // rows16 * cap + row_id % cap) == slot_id).astype(F32).astype(BF16)
    wide = dot(posterior, repeat)
    part = (lax.broadcasted_iota(jnp.int32, (dirs, rows), 1) & (rows16 - 1)) // cap
    for j in range(steps):
        spread[j * dirs : (j + 1) * dirs, :] = jnp.where(part == j, wide, 0.0).astype(BF16)

    lane_j = lax.broadcasted_iota(jnp.int32, (joined, LANES), 1)

    def average(g, carry):
        block = images_ref[:, pl.ds(g, 1), :, :].reshape(rows, LANES)
        mean = dot(spread[...], block)
        weight = weights_ref[g]
        for h in range(halves):
            shifted = mean if h == 0 else pltpu.roll(mean, LANES - h * width, 1)
            behind = pltpu.roll(weight, HALF - 8 * h, 1)
            start = pl.multiple_of((h * groups + g) * joined, joined)
            values[pl.ds(start, joined), :] = jnp.where(lane_j < HALF, shifted, behind)
        return carry

    lax.fori_loop(0, groups, average, 0)

    buffer_a[...] = jnp.zeros_like(buffer_a)
    buffer_b[...] = jnp.zeros_like(buffer_b)
    sums[...] = jnp.zeros_like(sums)

    place = lax.broadcasted_iota(jnp.int32, (CHUNK, LANES), 0)
    lane = lax.broadcasted_iota(jnp.int32, (CHUNK, grid), 1)
    at_y = lane.astype(F32).astype(BF16)
    at_next = ((lane + (grid - 1)) & (grid - 1)).astype(F32).astype(BF16)
    one = jnp.ones((CHUNK, grid), BF16)
    none = jnp.zeros((CHUNK, grid), BF16)

    def fetch(c, buffer):
        start = chunk_start_ref[c]
        for i in range(0, CHUNK, 16):
            lines = [values[pl.ds(point_ref[start + i + j], 1), :] for j in range(16)]
            for j in range(16):
                buffer[pl.ds(i + j, 1), :] = lines[j]

    def put(x, plane):
        for side in range(grid // LANES):
            out_ref[side, pl.ds(x, width, stride=grid + PAD), :] = plane[:, side * LANES : (side + 1) * LANES]

    def work(c, buffer):
        row = chunk_row_ref[c]
        before = chunk_row_ref[jnp.maximum(c - 1, 0)]
        data = buffer[...]
        y = jnp.broadcast_to(data[:, HALF + 4 : HALF + 5], (CHUNK, LANES))
        y = jnp.where(place < chunk_size_ref[c], y, -1.0).astype(BF16)
        y = jnp.concatenate([y] * (grid // LANES), axis=1)
        hot = jnp.concatenate([jnp.where(at_y == y, one, none), jnp.where(at_next == y, one, none)], axis=0)
        turned = data.T
        mean = turned[:width]
        weight = [jnp.broadcast_to(turned[HALF + j : HALF + j + 1], (width, CHUNK)) for j in range(4)]
        operand = jnp.concatenate(
            [
                jnp.concatenate([mean * weight[0], mean * weight[2]], axis=1),
                jnp.concatenate([mean * weight[1], mean * weight[3]], axis=1),
            ],
            axis=0,
        )
        high, low = two_terms(operand)
        result = dot(jnp.concatenate([high, low], axis=0), hot)
        result = result[: 2 * width] + result[2 * width :]
        same = row == before
        old_low, old_high = sums[:width], sums[width:]
        put((before + (grid - 1)) & (grid - 1), old_low)
        sums[:width] = result[:width] + jnp.where(same, old_low, old_high)
        sums[width:] = result[width:] + jnp.where(same, old_high, 0.0)

    fetch(0, buffer_a)

    def pair(m, carry):
        fetch(2 * m + 1, buffer_b)
        work(2 * m, buffer_a)
        fetch(2 * m + 2, buffer_a)
        work(2 * m + 1, buffer_b)
        return carry

    lax.fori_loop(0, total_ref[0], pair, 0)
    put(grid - 2, sums[:width])
    for side in range(grid // LANES):
        wrapped = pl.ds(grid - 1, width, stride=grid + PAD)
        cut = slice(side * LANES, (side + 1) * LANES)
        out_ref[side, wrapped, :] = out_ref[side, wrapped, :] + sums[width:, cut]


def scatter_call(plan, parts, images, weights, cap, width, grid):
    sources, groups, rows16, _ = images.shape
    dirs = parts.shape[1]
    points = dirs * grid
    smem = pl.BlockSpec(memory_space=pltpu.SMEM)
    vmem = pl.BlockSpec(memory_space=VMEM)
    return pl.pallas_call(
        functools.partial(scatter_kernel, cap, width, grid),
        out_shape=jax.ShapeDtypeStruct((grid // LANES, width * (grid + PAD), LANES), F32),
        in_specs=[smem] * 5 + [vmem] * 3,
        out_specs=vmem,
        scratch_shapes=[
            VMEM((points, LANES), F32),
            VMEM((CHUNK, LANES), F32),
            VMEM((CHUNK, LANES), F32),
            VMEM((2 * width, grid), F32),
            VMEM((weights.shape[1], sources * rows16), BF16),
        ],
        compiler_params=pltpu.CompilerParams(vmem_limit_bytes=60 * 2**20),
        name="scatter",
    )(*plan, parts, images, weights)


def plane_kernel(slabs, grid, flag_ref, data_ref, yh_ref, yl_ref, xh_ref, xl_ref, out_ref, lines):
    pairs = data_ref.shape[2] // 2
    half = grid // 2
    rows = half + 8
    slab = grid // slabs
    count = 2 * pairs
    lane = lax.broadcasted_iota(jnp.int32, (grid, half), 1)
    last = (pl.program_id(0) == pl.num_programs(0) - 1) & (flag_ref[0] == 1)

    def along_y(plane):
        high, low = two_terms(plane)
        both = dot(high, yh_ref[...]) + dot(low, yh_ref[...]) + dot(high, yl_ref[...])
        return both[:, :half], both[:, half:]

    def transformed(real, imag):
        cos_r, sin_r = along_y(real)
        cos_i, sin_i = along_y(imag)
        zero_r = jnp.where(lane == 0, 0.0, sin_r)
        zero_i = jnp.where(lane == 0, 0.0, sin_i)
        real = jnp.concatenate([cos_r - zero_i, jnp.where(lane == 0, sin_r, cos_r + sin_i)], axis=1)
        imag = jnp.concatenate([cos_i + zero_r, jnp.where(lane == 0, sin_i, cos_i - sin_r)], axis=1)
        return real, imag

    def along_x(table, operand):
        high, low = operand
        start = table * rows
        upper, lower = xh_ref[start : start + rows], xl_ref[start : start + rows]
        return dot(upper, high) + dot(upper, low) + dot(lower, high)

    def one(i, carry):
        planes = [
            [
                jnp.concatenate([data_ref[part, side, 2 * i + r][:grid] for part in range(grid // LANES)], axis=1)
                for r in range(2)
            ]
            for side in range(2)
        ]
        (a_r, a_i), (b_r, b_i) = planes
        single = last & (i == pairs - 1)
        sum_r, sum_i = transformed(jnp.where(single, b_r, a_r + b_r), jnp.where(single, b_i, a_i + b_i))
        dif_r, dif_i = transformed(jnp.where(single, -a_i, a_r - b_r), jnp.where(single, a_r, a_i - b_i))
        cosine = along_x(0, two_terms(jnp.concatenate([sum_r, dif_i], axis=1)))
        sine = along_x(1, two_terms(jnp.concatenate([sum_i, dif_r], axis=1)))
        fields = (
            (cosine[:, :grid] - sine[:, :grid], cosine[:, :grid] + sine[:, :grid]),
            (cosine[:, grid:] + sine[:, grid:], cosine[:, grid:] - sine[:, grid:]),
        )
        for c in range(2):
            plus, minus = fields[c]
            for part in range(grid // LANES):
                cut = slice(part * LANES, (part + 1) * LANES)
                place = 2 * i + c
                lines[part, pl.ds(place, half, stride=count), :] = plus[:half, cut]
                lines[part, pl.ds(half * count + place, half, stride=count), :] = minus[1 : half + 1, cut]
        return carry

    lax.fori_loop(0, pairs, one, 0)
    for d in range(slabs):
        if d < slabs // 2:
            start = slab * d
        else:
            start = half + grid - slab * d - slab
        size = slab * count
        for part in range(grid // LANES):
            block = lines[part, start * count : start * count + size, :]
            out_ref[d, :, :, part * LANES : (part + 1) * LANES] = block.astype(BF16).reshape(slab, count, LANES)


def planes_call(flag, data, table_y, table_x, slabs, grid):
    parts, sides, values, pitch, _ = data.shape
    step = min(16, values)
    slab = grid // slabs
    fixed = lambda i, flag_ref: (0, 0)
    return pl.pallas_call(
        functools.partial(plane_kernel, slabs, grid),
        grid_spec=pltpu.PrefetchScalarGridSpec(
            num_scalar_prefetch=1,
            grid=(values // step,),
            in_specs=[
                pl.BlockSpec((parts, sides, step, pitch, LANES), lambda i, flag_ref: (0, 0, i, 0, 0)),
                pl.BlockSpec(table_y[0].shape, fixed),
                pl.BlockSpec(table_y[1].shape, fixed),
                pl.BlockSpec(table_x[0].shape, fixed),
                pl.BlockSpec(table_x[1].shape, fixed),
            ],
            out_specs=pl.BlockSpec((slabs, slab, step, grid), lambda i, flag_ref: (0, 0, i, 0)),
            scratch_shapes=[VMEM((parts, grid * step, LANES), F32)],
        ),
        out_shape=jax.ShapeDtypeStruct((slabs, slab, values, grid), BF16),
        compiler_params=pltpu.CompilerParams(vmem_limit_bytes=56 * 2**20),
        name="planes",
    )(flag, data, *table_y, *table_x)


def volume_kernel(flip_ref, data_ref, restore_ref, zh_ref, zl_ref, out_ref):
    slabs, span, width, grid = data_ref.shape
    for i in range(span):
        block = data_ref[:, i].reshape(slabs * width, grid)
        turned = dot_t(restore_ref[...], block).astype(BF16)
        value = dot(turned, zh_ref[...]) + dot(turned, zl_ref[...])
        out_ref[jnp.where(flip_ref[0] == 1, span - 1 - i, i)] = value


def volume_call(flip, data, restore, table_z):
    slabs, slab, width, grid = data.shape
    span = 4
    steps = slab // span
    fixed = lambda i, flip_ref: (0, 0)
    return pl.pallas_call(
        volume_kernel,
        grid_spec=pltpu.PrefetchScalarGridSpec(
            num_scalar_prefetch=1,
            grid=(steps,),
            in_specs=[
                pl.BlockSpec((slabs, span, width, grid), lambda i, flip_ref: (0, i, 0, 0)),
                pl.BlockSpec(restore.shape, fixed),
                pl.BlockSpec(table_z[0].shape, fixed),
                pl.BlockSpec(table_z[1].shape, fixed),
            ],
            out_specs=pl.BlockSpec(
                (span, grid, grid), lambda i, flip_ref: (jnp.where(flip_ref[0] == 1, steps - 1 - i, i), 0, 0)
            ),
        ),
        out_shape=jax.ShapeDtypeStruct((slab, grid, grid), F32),
        compiler_params=pltpu.CompilerParams(vmem_limit_bytes=48 * 2**20),
        name="volume",
    )(flip, data, restore, *table_z)


def sorted_points(interp_cells, grid):
    dirs = interp_cells.shape[0]
    points = dirs * grid
    base = interp_cells[:, 0, :].T.reshape(-1)
    row = (base // grid + 1) & (grid - 1)
    key = row * points + jnp.arange(points, dtype=jnp.int32)
    key = lax.sort(key, is_stable=False)
    rows = jnp.arange(grid, dtype=jnp.int32)
    count = jnp.sum((row[None, :] == rows[:, None]).astype(jnp.int32), axis=1)
    first = jnp.cumsum(count) - count
    chunks = jnp.maximum((count + (CHUNK - 1)) // CHUNK, 1)
    ends = jnp.cumsum(chunks)
    most = grid + points // CHUNK + 2
    number = jnp.arange(most, dtype=jnp.int32)
    chunk_row = jnp.minimum(jnp.sum((ends[None, :] <= number[:, None]).astype(jnp.int32), axis=1), grid - 1)
    mine = (rows[None, :] == chunk_row[:, None]).astype(jnp.int32)
    shift = first - (ends - chunks) * CHUNK
    chunk_start = jnp.sum(mine * shift[None, :], axis=1) + number * CHUNK
    row_end = jnp.sum(mine * (first + count)[None, :], axis=1)
    used = number < ends[-1]
    chunk_size = jnp.where(used, jnp.clip(row_end - chunk_start, 0, CHUNK), 0)
    chunk_start = jnp.where(used, chunk_start, points)
    pairs = ((ends[-1] + 1) // 2).reshape(1)
    point = jnp.concatenate([key & (points - 1), jnp.zeros((CHUNK,), jnp.int32)])
    return pairs, chunk_row, chunk_start, chunk_size, point


def paired_rows(rows, slabs):
    half = rows.shape[1] // 2
    own = lax.axis_index("vol")
    low = own < slabs // 2
    middle = own == slabs // 2
    upper = lax.ppermute(rows[:, half:], "vol", [(i, slabs - 1 - i) for i in range(slabs)])
    first = rows[:, :1]
    moved = [(0, slabs // 2)] + [(i, slabs - i) for i in range(1, slabs // 2)]
    other = lax.ppermute(first, "vol", moved)
    tail = jnp.concatenate([upper[:, 1:], jnp.where(middle, first, other)], axis=1)
    positive = jnp.where(low, rows[:, 1 : half + 1], tail)
    head = jnp.concatenate([jnp.where(middle, other, first), rows[:, 1:half]], axis=1)
    negative = jnp.flip(jnp.where(low, upper, head), axis=1)
    return jnp.concatenate([positive, negative], axis=1)


def shards(images, projections, assignment, interp_cells, interp_weights):
    class_count = lax.axis_size("cls")
    slab_count = lax.axis_size("vol")
    local_count, grid = images.shape[0], images.shape[1]
    dirs = projections.shape[1]
    slab = grid // slab_count
    width = 2 * slab
    halves = LANES // width
    capacity = 2 * local_count // class_count
    steps = 16 // capacity
    groups = grid // (halves * steps)

    eye = jnp.asarray(np.eye(grid), BF16)
    order = jnp.asarray(lane_order(grid, slab_count))
    outgoing = route_call(images, assignment, eye, order, class_count, slab_count, width, capacity)
    arrived = lax.all_to_all(outgoing, ("cls", "vol"), split_axis=0, concat_axis=0, tiled=True)

    references = paired_rows(projections[0], slab_count)
    references = references.reshape(dirs, slab, 2, halves, groups, steps)
    references = jnp.transpose(references, (4, 5, 0, 3, 1, 2)).reshape(groups, steps * dirs, LANES)
    corner_y = (interp_cells[:, 0:1, :] & (grid - 1)).astype(F32)
    weights = jnp.concatenate([interp_weights, corner_y, jnp.zeros((dirs, 3, grid), F32)], axis=1)
    weights = weights.reshape(dirs, 8, halves, groups, steps)
    weights = jnp.transpose(weights, (3, 4, 0, 2, 1)).reshape(groups, steps * dirs, 8 * halves)
    weights = jnp.pad(weights, ((0, 0), (0, 0), (0, LANES - 8 * halves)))
    plan = sorted_points(interp_cells, grid)
    table_y, table_x, table_z, restore = tables(grid, slab_count)

    arrived, references, weights, plan = lax.optimization_barrier((arrived, references, weights, plan))
    partial_value = scores_call(arrived, references, capacity, dirs)
    copies = jnp.broadcast_to(partial_value[None], (slab_count,) + partial_value.shape)
    parts = lax.all_to_all(copies, "vol", split_axis=0, concat_axis=0, tiled=True)
    plane = scatter_call(plan, parts, arrived, weights, capacity, width, grid)
    plane = plane.reshape(grid // LANES, 2, slab, grid + PAD, LANES)
    own = lax.axis_index("vol")
    single = (own == slab_count // 2).astype(jnp.int32).reshape(1)
    flip = (own >= slab_count // 2).astype(jnp.int32).reshape(1)
    sent = planes_call(single, plane, table_y, table_x, slab_count, grid)
    received = lax.all_to_all(sent, "vol", split_axis=0, concat_axis=0, tiled=True)
    return volume_call(flip, received, restore, table_z)[None]


def solution(mesh):
    in_specs = (
        P(("cls", "vol"), None, None, None),
        P("cls", None, "vol", None, None),
        P(("cls", "vol"), None),
        P(),
        P(),
    )
    out_specs = P("cls", "vol", None, None)
    return jax.shard_map(shards, mesh=mesh, in_specs=in_specs, out_specs=out_specs, check_vma=False)
```

```python
import functools
import math

import jax
import jax.numpy as jnp
import numpy as np
from jax import lax
from jax.experimental import pallas as pl
from jax.experimental.pallas import tpu as pltpu
from jax.sharding import PartitionSpec as P

F32 = jnp.float32
BF16 = jnp.bfloat16
LANES = 128
HALF = 64
CHUNK = 128
PAD = 8
UNROLL = 8
VMEM = pltpu.VMEM


def split_table(table):
    high = table.astype(jnp.bfloat16)
    low = (table - high.astype(np.float64)).astype(jnp.bfloat16)
    return high, low


def plane_pairs(grid, slabs):
    slab = grid // slabs
    half = slab // 2
    pairs = []
    for w in range(slabs):
        for i in range(half):
            if w < slabs // 2:
                first = slab * w + 1 + i
            else:
                first = slab * w + half - 1 - i
            if 2 * first == grid:
                pairs.append((0, first))
            else:
                pairs.append((first, grid - first))
    return np.array(pairs).reshape(slabs, half, 2)


def tables(grid, slabs):
    half = grid // 2
    scale = 1.0 / math.sqrt(grid)
    index = np.arange(grid)
    angle = 2.0 * np.pi / grid
    phase = (index[:, None] * np.arange(half)[None, :]) % grid
    cosine = np.cos(phase * angle)
    sine = np.sin(phase * angle)
    sine[:, 0] = np.cos(((index * half) % grid) * angle)
    table_y = np.concatenate([cosine, sine], axis=1) * scale
    rows = half + 8
    phase = (np.arange(rows)[:, None] * index[None, :]) % grid
    live = (np.arange(rows) <= half)[:, None]
    table_x = np.concatenate([np.cos(phase * angle) * live, np.sin(phase * angle) * live], axis=0) * scale
    pairs = plane_pairs(grid, slabs).reshape(-1, 2)
    single = (2 * pairs[:, 1] == grid)[:, None]
    z = np.where(single[:, 0], pairs[:, 1], pairs[:, 0])
    phase = (z[:, None] * index[None, :]) % grid
    for_sum = np.where(single, 1.0, np.cos(phase * angle))
    for_difference = np.where(single, np.cos(phase * angle), -np.sin(phase * angle))
    table_z = np.stack([for_sum, for_difference], axis=1).reshape(grid, grid) * scale
    order = np.concatenate([np.arange(half), [half], np.arange(grid - 1, half, -1)])
    restore = (order[None, :] == index[:, None]).astype(jnp.bfloat16)
    return split_table(table_y), split_table(table_x), split_table(table_z), restore


def lane_order(grid, slabs):
    rows = plane_pairs(grid, slabs).transpose(0, 2, 1).reshape(-1)
    source = (2 * rows[:, None] + np.arange(2)[None, :]).reshape(-1)
    return (np.arange(2 * grid)[:, None] == source[None, :]).astype(jnp.bfloat16)


def dot(a, b):
    return jnp.dot(a, b, preferred_element_type=F32)


def dot_t(a, b):
    return lax.dot_general(a, b, (((1,), (1,)), ((), ())), preferred_element_type=F32)


def two_terms(value):
    high = value.astype(BF16)
    low = (value - high.astype(F32)).astype(BF16)
    return high, low


def route_kernel(cap, slabs, width, classes_ref, images_ref, eye_ref, order_ref, out_ref, lines):
    count, _, _, grid = images_ref.shape
    halves = LANES // width
    piece = grid // halves
    lane = lax.broadcasted_iota(jnp.int32, (piece, LANES), 1)
    lines[...] = jnp.zeros_like(lines)

    def place(p, carry):
        own = classes_ref[p, 0]
        rank = 0
        for q in range(count):
            rank = rank + jnp.where((classes_ref[q, 0] == own) & (q < p), 1, 0)
        image = images_ref[p].reshape(-1, grid)
        turned = dot(dot_t(eye_ref[...], image).astype(BF16), order_ref[...])
        for w in range(slabs):
            tile = w * width // LANES * LANES
            block = jnp.zeros((piece, LANES), F32)
            for h in range(halves):
                part = turned[h * piece : (h + 1) * piece, tile : tile + LANES]
                shift = (h * width - (w * width - tile)) % LANES
                part = part if shift == 0 else pltpu.roll(part, shift, 1)
                block = jnp.where((lane >= h * width) & (lane < (h + 1) * width), part, block)
            lines[own * slabs + w, pl.ds(rank, piece, stride=cap), :] = block
        return carry

    lax.fori_loop(0, count, place, 0)
    out_ref[...] = lines[...].astype(BF16).reshape(out_ref.shape)


def route_call(images, assignment, eye, order, class_count, slabs, width, cap):
    count, grid = images.shape[0], images.shape[1]
    rows = grid // (LANES // width) * cap
    vmem = pl.BlockSpec(memory_space=VMEM)
    return pl.pallas_call(
        functools.partial(route_kernel, cap, slabs, width),
        out_shape=jax.ShapeDtypeStruct((class_count * slabs, rows // 16, 16, LANES), BF16),
        in_specs=[pl.BlockSpec(memory_space=pltpu.SMEM)] + [vmem] * 3,
        out_specs=vmem,
        scratch_shapes=[VMEM((class_count * slabs, rows, LANES), F32)],
        compiler_params=pltpu.CompilerParams(vmem_limit_bytes=48 * 2**20),
        name="route",
    )(assignment, images, eye, order)


def score_kernel(cap, dirs, unit, images_ref, kept_ref, joined_ref, out_ref, sums):
    sources, groups, rows16, _ = images_ref.shape
    rows = sources * rows16
    steps = rows16 // cap
    sums[...] = jnp.zeros_like(sums)
    lane = lax.broadcasted_iota(jnp.int32, (steps * dirs, LANES), 1)
    even = (lane & unit) == 0

    def step(g, carry):
        kept = kept_ref[g].astype(F32)
        joined = joined_ref[g].astype(F32)
        refs = [
            jnp.where(even, kept, pltpu.roll(joined, unit, 1)).astype(BF16),
            jnp.where(even, pltpu.roll(kept, LANES - unit, 1), joined).astype(BF16),
        ]
        blocks = [images_ref[:, pl.ds(g + i * (groups // 2), 1), :, :].reshape(rows, LANES) for i in range(2)]
        sums[...] += dot_t(jnp.concatenate(refs, axis=1), jnp.concatenate(blocks, axis=1))
        return carry

    lax.fori_loop(0, groups // 2, step, 0)
    column = lax.broadcasted_iota(jnp.int32, (dirs, rows), 1)
    part = (column & (rows16 - 1)) // cap
    kept = jnp.zeros((dirs, rows), F32)
    for j in range(steps):
        kept = kept + jnp.where(part == j, sums[j * dirs : (j + 1) * dirs, :], 0.0)
    slots = sources * cap
    row_id = lax.broadcasted_iota(jnp.int32, (rows, slots), 0)
    slot_id = lax.broadcasted_iota(jnp.int32, (rows, slots), 1)
    gather = (row_id // rows16 * cap + row_id % cap) == slot_id
    out_ref[...] = jnp.dot(
        kept, gather.astype(F32), preferred_element_type=F32, precision=lax.Precision.HIGHEST
    )


def scores_call(images, kept, joined, cap, dirs, unit):
    sources, groups, rows16, _ = images.shape
    return pl.pallas_call(
        functools.partial(score_kernel, cap, dirs, unit),
        out_shape=jax.ShapeDtypeStruct((dirs, sources * cap), F32),
        in_specs=[pl.BlockSpec(memory_space=VMEM)] * 3,
        out_specs=pl.BlockSpec(memory_space=VMEM),
        scratch_shapes=[VMEM((kept.shape[1], sources * rows16), F32)],
        compiler_params=pltpu.CompilerParams(vmem_limit_bytes=48 * 2**20),
        name="scores",
    )(images, kept, joined)


def scatter_kernel(
    cap,
    width,
    grid,
    turns_ref,
    chunk_row_ref,
    chunk_start_ref,
    chunk_size_ref,
    point_ref,
    parts_ref,
    images_ref,
    weights_ref,
    out_ref,
    values,
    sums,
    spread,
    *buffers,
):
    sources, groups, rows16, _ = images_ref.shape
    rows = sources * rows16
    steps = rows16 // cap
    dirs, slots = parts_ref.shape[1:]
    joined = steps * dirs
    halves = LANES // width

    total = parts_ref[0]
    for i in range(1, parts_ref.shape[0]):
        total = total + parts_ref[i]
    expo = jnp.exp(total - jnp.max(total, axis=0, keepdims=True))
    posterior = (expo / jnp.sum(expo, axis=0, keepdims=True)).astype(BF16)
    slot_id = lax.broadcasted_iota(jnp.int32, (slots, rows), 0)
    row_id = lax.broadcasted_iota(jnp.int32, (slots, rows), 1)
    repeat = ((row_id // rows16 * cap + row_id % cap) == slot_id).astype(F32).astype(BF16)
    wide = dot(posterior, repeat)
    part = (lax.broadcasted_iota(jnp.int32, (dirs, rows), 1) & (rows16 - 1)) // cap
    for j in range(steps):
        spread[j * dirs : (j + 1) * dirs, :] = jnp.where(part == j, wide, 0.0).astype(BF16)

    lane_j = lax.broadcasted_iota(jnp.int32, (joined, LANES), 1)

    def average(g, carry):
        block = images_ref[:, pl.ds(g, 1), :, :].reshape(rows, LANES)
        mean = dot(spread[...], block)
        weight = weights_ref[g]
        for h in range(halves):
            shifted = mean if h == 0 else pltpu.roll(mean, LANES - h * width, 1)
            behind = pltpu.roll(weight, HALF - 8 * h, 1)
            start = pl.multiple_of((h * groups + g) * joined, joined)
            values[pl.ds(start, joined), :] = jnp.where(lane_j < HALF, shifted, behind)
        return carry

    lax.fori_loop(0, groups, average, 0)

    for buffer in buffers:
        buffer[...] = jnp.zeros_like(buffer)
    sums[...] = jnp.zeros_like(sums)

    place = lax.broadcasted_iota(jnp.int32, (CHUNK, LANES), 0)
    lane = lax.broadcasted_iota(jnp.int32, (CHUNK, grid), 1)
    at_y = lane.astype(F32).astype(BF16)
    at_next = ((lane + (grid - 1)) & (grid - 1)).astype(F32).astype(BF16)
    one = jnp.ones((CHUNK, grid), BF16)
    none = jnp.zeros((CHUNK, grid), BF16)

    def fetch(c, buffer):
        start = chunk_start_ref[c]
        for i in range(0, CHUNK, 16):
            lines = [values[pl.ds(point_ref[start + i + j], 1), :] for j in range(16)]
            for j in range(16):
                buffer[pl.ds(i + j, 1), :] = lines[j]

    def put(x, plane):
        for side in range(grid // LANES):
            out_ref[side, pl.ds(x, width, stride=grid + PAD), :] = plane[:, side * LANES : (side + 1) * LANES]

    def work(c, buffer):
        row = chunk_row_ref[c]
        before = chunk_row_ref[jnp.maximum(c - 1, 0)]
        data = buffer[...]
        y = jnp.broadcast_to(data[:, HALF + 4 : HALF + 5], (CHUNK, LANES))
        y = jnp.where(place < chunk_size_ref[c], y, -1.0).astype(BF16)
        y = jnp.concatenate([y] * (grid // LANES), axis=1)
        hot = jnp.concatenate([jnp.where(at_y == y, one, none), jnp.where(at_next == y, one, none)], axis=0)
        turned = data.T
        mean = turned[:width]
        weight = [jnp.broadcast_to(turned[HALF + j : HALF + j + 1], (width, CHUNK)) for j in range(4)]
        operand = jnp.concatenate(
            [
                jnp.concatenate([mean * weight[0], mean * weight[2]], axis=1),
                jnp.concatenate([mean * weight[1], mean * weight[3]], axis=1),
            ],
            axis=0,
        )
        high, low = two_terms(operand)
        result = dot(jnp.concatenate([high, low], axis=0), hot)
        result = result[: 2 * width] + result[2 * width :]
        same = row == before
        old_low, old_high = sums[:width], sums[width:]
        put((before + (grid - 1)) & (grid - 1), old_low)
        sums[:width] = result[:width] + jnp.where(same, old_low, old_high)
        sums[width:] = result[width:] + jnp.where(same, old_high, 0.0)

    fetch(0, buffers[0])

    def several(m, carry):
        for i in range(UNROLL):
            fetch(UNROLL * m + i + 1, buffers[(i + 1) % UNROLL])
            work(UNROLL * m + i, buffers[i])
        return carry

    lax.fori_loop(0, turns_ref[0], several, 0)
    put(grid - 2, sums[:width])
    for side in range(grid // LANES):
        wrapped = pl.ds(grid - 1, width, stride=grid + PAD)
        cut = slice(side * LANES, (side + 1) * LANES)
        out_ref[side, wrapped, :] = out_ref[side, wrapped, :] + sums[width:, cut]


def scatter_call(plan, parts, images, weights, cap, width, grid):
    sources, groups, rows16, _ = images.shape
    dirs = parts.shape[1]
    points = dirs * grid
    smem = pl.BlockSpec(memory_space=pltpu.SMEM)
    vmem = pl.BlockSpec(memory_space=VMEM)
    return pl.pallas_call(
        functools.partial(scatter_kernel, cap, width, grid),
        out_shape=jax.ShapeDtypeStruct((grid // LANES, width * (grid + PAD), LANES), F32),
        in_specs=[smem] * 5 + [vmem] * 3,
        out_specs=vmem,
        scratch_shapes=[
            VMEM((points, LANES), F32),
            VMEM((2 * width, grid), F32),
            VMEM((weights.shape[1], sources * rows16), BF16),
        ]
        + [VMEM((CHUNK, LANES), F32)] * UNROLL,
        compiler_params=pltpu.CompilerParams(vmem_limit_bytes=60 * 2**20),
        name="scatter",
    )(*plan, parts, images, weights)


def plane_kernel(slabs, grid, flag_ref, data_ref, yh_ref, yl_ref, xh_ref, xl_ref, out_ref, lines):
    pairs = data_ref.shape[2] // 2
    half = grid // 2
    rows = half + 8
    slab = grid // slabs
    count = 2 * pairs
    lane = lax.broadcasted_iota(jnp.int32, (grid, half), 1)
    last = (pl.program_id(0) == pl.num_programs(0) - 1) & (flag_ref[0] == 1)

    def along_y(plane):
        high, low = two_terms(plane)
        both = dot(high, yh_ref[...]) + dot(low, yh_ref[...]) + dot(high, yl_ref[...])
        return both[:, :half], both[:, half:]

    def transformed(real, imag):
        cos_r, sin_r = along_y(real)
        cos_i, sin_i = along_y(imag)
        zero_r = jnp.where(lane == 0, 0.0, sin_r)
        zero_i = jnp.where(lane == 0, 0.0, sin_i)
        real = jnp.concatenate([cos_r - zero_i, jnp.where(lane == 0, sin_r, cos_r + sin_i)], axis=1)
        imag = jnp.concatenate([cos_i + zero_r, jnp.where(lane == 0, sin_i, cos_i - sin_r)], axis=1)
        return real, imag

    def along_x(table, operand):
        high, low = operand
        start = table * rows
        upper, lower = xh_ref[start : start + rows], xl_ref[start : start + rows]
        return dot(upper, high) + dot(upper, low) + dot(lower, high)

    def one(i, carry):
        planes = [
            [
                jnp.concatenate([data_ref[part, side, 2 * i + r][:grid] for part in range(grid // LANES)], axis=1)
                for r in range(2)
            ]
            for side in range(2)
        ]
        (a_r, a_i), (b_r, b_i) = planes
        single = last & (i == pairs - 1)
        sum_r, sum_i = transformed(jnp.where(single, a_r, a_r + b_r), jnp.where(single, a_i, a_i + b_i))
        dif_r, dif_i = transformed(jnp.where(single, -b_i, a_r - b_r), jnp.where(single, b_r, a_i - b_i))
        cosine = along_x(0, two_terms(jnp.concatenate([sum_r, dif_i], axis=1)))
        sine = along_x(1, two_terms(jnp.concatenate([sum_i, dif_r], axis=1)))
        fields = (
            (cosine[:, :grid] - sine[:, :grid], cosine[:, :grid] + sine[:, :grid]),
            (cosine[:, grid:] + sine[:, grid:], cosine[:, grid:] - sine[:, grid:]),
        )
        for c in range(2):
            plus, minus = fields[c]
            for part in range(grid // LANES):
                cut = slice(part * LANES, (part + 1) * LANES)
                place = 2 * i + c
                lines[part, pl.ds(place, half, stride=count), :] = plus[:half, cut]
                lines[part, pl.ds(half * count + place, half, stride=count), :] = minus[1 : half + 1, cut]
        return carry

    lax.fori_loop(0, pairs, one, 0)
    for d in range(slabs):
        if d < slabs // 2:
            start = slab * d
        else:
            start = half + grid - slab * d - slab
        size = slab * count
        for part in range(grid // LANES):
            block = lines[part, start * count : start * count + size, :]
            out_ref[d, :, :, part * LANES : (part + 1) * LANES] = block.astype(BF16).reshape(slab, count, LANES)


def planes_call(flag, data, table_y, table_x, slabs, grid):
    parts, sides, values, pitch, _ = data.shape
    step = min(16, values)
    slab = grid // slabs
    fixed = lambda i, flag_ref: (0, 0)
    return pl.pallas_call(
        functools.partial(plane_kernel, slabs, grid),
        grid_spec=pltpu.PrefetchScalarGridSpec(
            num_scalar_prefetch=1,
            grid=(values // step,),
            in_specs=[
                pl.BlockSpec((parts, sides, step, pitch, LANES), lambda i, flag_ref: (0, 0, i, 0, 0)),
                pl.BlockSpec(table_y[0].shape, fixed),
                pl.BlockSpec(table_y[1].shape, fixed),
                pl.BlockSpec(table_x[0].shape, fixed),
                pl.BlockSpec(table_x[1].shape, fixed),
            ],
            out_specs=pl.BlockSpec((slabs, slab, step, grid), lambda i, flag_ref: (0, 0, i, 0)),
            scratch_shapes=[VMEM((parts, grid * step, LANES), F32)],
        ),
        out_shape=jax.ShapeDtypeStruct((slabs, slab, values, grid), BF16),
        compiler_params=pltpu.CompilerParams(vmem_limit_bytes=56 * 2**20),
        name="planes",
    )(flag, data, *table_y, *table_x)


def volume_kernel(flip_ref, data_ref, restore_ref, zh_ref, zl_ref, out_ref):
    slabs, span, width, grid = data_ref.shape
    for i in range(span):
        block = data_ref[:, i].reshape(slabs * width, grid)
        turned = dot_t(restore_ref[...], block).astype(BF16)
        value = dot(turned, zh_ref[...]) + dot(turned, zl_ref[...])
        out_ref[jnp.where(flip_ref[0] == 1, span - 1 - i, i)] = value


def volume_call(flip, data, restore, table_z):
    slabs, slab, width, grid = data.shape
    span = 4
    steps = slab // span
    fixed = lambda i, flip_ref: (0, 0)
    return pl.pallas_call(
        volume_kernel,
        grid_spec=pltpu.PrefetchScalarGridSpec(
            num_scalar_prefetch=1,
            grid=(steps,),
            in_specs=[
                pl.BlockSpec((slabs, span, width, grid), lambda i, flip_ref: (0, i, 0, 0)),
                pl.BlockSpec(restore.shape, fixed),
                pl.BlockSpec(table_z[0].shape, fixed),
                pl.BlockSpec(table_z[1].shape, fixed),
            ],
            out_specs=pl.BlockSpec(
                (span, grid, grid), lambda i, flip_ref: (jnp.where(flip_ref[0] == 1, steps - 1 - i, i), 0, 0)
            ),
        ),
        out_shape=jax.ShapeDtypeStruct((slab, grid, grid), F32),
        compiler_params=pltpu.CompilerParams(vmem_limit_bytes=48 * 2**20),
        name="volume",
    )(flip, data, restore, *table_z)


def sorted_points(interp_cells, grid):
    dirs = interp_cells.shape[0]
    points = dirs * grid
    base = interp_cells[:, 0, :].T.reshape(-1)
    row = (base // grid + 1) & (grid - 1)
    key = row * points + jnp.arange(points, dtype=jnp.int32)
    key = lax.sort(key, is_stable=False)
    rows = jnp.arange(grid, dtype=jnp.int32)
    count = jnp.sum((row[None, :] == rows[:, None]).astype(jnp.int32), axis=1)
    first = jnp.cumsum(count) - count
    chunks = jnp.maximum((count + (CHUNK - 1)) // CHUNK, 1)
    ends = jnp.cumsum(chunks)
    most = grid + points // CHUNK + UNROLL + 1
    number = jnp.arange(most, dtype=jnp.int32)
    chunk_row = jnp.minimum(jnp.sum((ends[None, :] <= number[:, None]).astype(jnp.int32), axis=1), grid - 1)
    mine = (rows[None, :] == chunk_row[:, None]).astype(jnp.int32)
    shift = first - (ends - chunks) * CHUNK
    chunk_start = jnp.sum(mine * shift[None, :], axis=1) + number * CHUNK
    row_end = jnp.sum(mine * (first + count)[None, :], axis=1)
    used = number < ends[-1]
    chunk_size = jnp.where(used, jnp.clip(row_end - chunk_start, 0, CHUNK), 0)
    chunk_start = jnp.where(used, chunk_start, points)
    turns = ((ends[-1] + (UNROLL - 1)) // UNROLL).reshape(1)
    point = jnp.concatenate([key & (points - 1), jnp.zeros((CHUNK,), jnp.int32)])
    return turns, chunk_row, chunk_start, chunk_size, point


def lay_out(rows, steps):
    dirs, count, _, grid = rows.shape
    blocks = LANES // (2 * count)
    rows = rows.reshape(dirs, count, 2, blocks, grid // blocks)
    return jnp.transpose(rows, (4, 0, 3, 1, 2)).reshape(grid // blocks // steps, steps * dirs, LANES)


def paired_rows(rows, slabs, steps):
    half = rows.shape[1] // 2
    own = lax.axis_index("vol")
    low = own < slabs // 2
    first = rows[:, :1]
    moved = [(0, slabs // 2)] + [(i, i - 1) for i in range(1, slabs // 2 + 1)]
    other = lax.ppermute(first, "vol", moved)
    tail = jnp.concatenate([rows[:, half + 1 :], other], axis=1)
    sent = jnp.where(low, tail, jnp.flip(rows[:, half:], axis=1))
    sent = lay_out(sent, steps)
    arrived = lax.ppermute(sent, "vol", [(i, slabs - 1 - i) for i in range(slabs)])
    head = jnp.concatenate([jnp.where(own == slabs // 2, other, first), rows[:, 1:half]], axis=1)
    kept = jnp.where(low, rows[:, 1 : half + 1], jnp.flip(head, axis=1))
    return lay_out(kept, steps), arrived


def shards(images, projections, assignment, interp_cells, interp_weights):
    class_count = lax.axis_size("cls")
    slab_count = lax.axis_size("vol")
    local_count, grid = images.shape[0], images.shape[1]
    dirs = projections.shape[1]
    slab = grid // slab_count
    width = 2 * slab
    halves = LANES // width
    capacity = 2 * local_count // class_count
    steps = 16 // capacity
    groups = grid // (halves * steps)

    eye = jnp.asarray(np.eye(grid), BF16)
    order = jnp.asarray(lane_order(grid, slab_count))
    outgoing = route_call(images, assignment, eye, order, class_count, slab_count, width, capacity)
    outgoing, projections = lax.optimization_barrier((outgoing, projections))
    arrived = lax.all_to_all(outgoing, ("cls", "vol"), split_axis=0, concat_axis=0, tiled=True)

    kept, joined = paired_rows(projections[0], slab_count, steps)
    corner_y = (interp_cells[:, 0:1, :] & (grid - 1)).astype(F32)
    weights = jnp.concatenate([interp_weights, corner_y, jnp.zeros((dirs, 3, grid), F32)], axis=1)
    weights = weights.reshape(dirs, 8, halves, groups, steps)
    weights = jnp.transpose(weights, (3, 4, 0, 2, 1)).reshape(groups, steps * dirs, 8 * halves)
    weights = jnp.pad(weights, ((0, 0), (0, 0), (0, LANES - 8 * halves)))
    plan = sorted_points(interp_cells, grid)
    table_y, table_x, table_z, restore = tables(grid, slab_count)

    arrived, kept, joined, weights, plan = lax.optimization_barrier((arrived, kept, joined, weights, plan))
    partial_value = scores_call(arrived, kept, joined, capacity, dirs, slab)
    copies = jnp.broadcast_to(partial_value[None], (slab_count,) + partial_value.shape)
    parts = lax.all_to_all(copies, "vol", split_axis=0, concat_axis=0, tiled=True)
    plane = scatter_call(plan, parts, arrived, weights, capacity, width, grid)
    plane = plane.reshape(grid // LANES, 2, slab, grid + PAD, LANES)
    own = lax.axis_index("vol")
    single = (own == slab_count // 2).astype(jnp.int32).reshape(1)
    flip = (own >= slab_count // 2).astype(jnp.int32).reshape(1)
    sent = planes_call(single, plane, table_y, table_x, slab_count, grid)
    received = lax.all_to_all(sent, "vol", split_axis=0, concat_axis=0, tiled=True)
    return volume_call(flip, received, restore, table_z)[None]


def solution(mesh):
    in_specs = (
        P(("cls", "vol"), None, None, None),
        P("cls", None, "vol", None, None),
        P(("cls", "vol"), None),
        P(),
        P(),
    )
    out_specs = P("cls", "vol", None, None)
    return jax.shard_map(shards, mesh=mesh, in_specs=in_specs, out_specs=out_specs, check_vma=False)
```

```python
import functools
import math

import jax
import jax.numpy as jnp
import numpy as np
from jax import lax
from jax.experimental import pallas as pl
from jax.experimental.pallas import tpu as pltpu
from jax.sharding import PartitionSpec as P

F32 = jnp.float32
BF16 = jnp.bfloat16
LANES = 128
HALF = 64
CHUNK = 128
PAD = 8
UNROLL = 8
VMEM = pltpu.VMEM


def split_table(table):
    high = table.astype(jnp.bfloat16)
    low = (table - high.astype(np.float64)).astype(jnp.bfloat16)
    return high, low


def plane_pairs(grid, slabs):
    slab = grid // slabs
    half = slab // 2
    pairs = []
    for w in range(slabs):
        for i in range(half):
            if w < slabs // 2:
                first = slab * w + 1 + i
            else:
                first = slab * w + half - 1 - i
            if 2 * first == grid:
                pairs.append((0, first))
            else:
                pairs.append((first, grid - first))
    return np.array(pairs).reshape(slabs, half, 2)


def tables(grid, slabs):
    half = grid // 2
    scale = 1.0 / math.sqrt(grid)
    index = np.arange(grid)
    angle = 2.0 * np.pi / grid
    phase = (index[:, None] * np.arange(half)[None, :]) % grid
    cosine = np.cos(phase * angle)
    sine = np.sin(phase * angle)
    sine[:, 0] = np.cos(((index * half) % grid) * angle)
    table_y = np.concatenate([cosine, sine], axis=1) * scale
    rows = half + 8
    phase = (np.arange(rows)[:, None] * index[None, :]) % grid
    live = (np.arange(rows) <= half)[:, None]
    table_x = np.concatenate([np.cos(phase * angle) * live, np.sin(phase * angle) * live], axis=0) * scale
    pairs = plane_pairs(grid, slabs).reshape(-1, 2)
    single = (2 * pairs[:, 1] == grid)[:, None]
    z = np.where(single[:, 0], pairs[:, 1], pairs[:, 0])
    phase = (z[:, None] * index[None, :]) % grid
    for_sum = np.where(single, 1.0, np.cos(phase * angle))
    for_difference = np.where(single, np.cos(phase * angle), -np.sin(phase * angle))
    table_z = np.stack([for_sum, for_difference], axis=1).reshape(grid, grid) * scale
    order = np.concatenate([np.arange(half), [half], np.arange(grid - 1, half, -1)])
    restore = (order[None, :] == index[:, None]).astype(jnp.bfloat16)
    return split_table(table_y), split_table(table_x), split_table(table_z), restore


def lane_order(grid, slabs):
    rows = plane_pairs(grid, slabs).transpose(0, 2, 1).reshape(-1)
    source = (2 * rows[:, None] + np.arange(2)[None, :]).reshape(-1)
    return (np.arange(2 * grid)[:, None] == source[None, :]).astype(jnp.bfloat16)


def dot(a, b):
    return jnp.dot(a, b, preferred_element_type=F32)


def dot_t(a, b):
    return lax.dot_general(a, b, (((1,), (1,)), ((), ())), preferred_element_type=F32)


def two_terms(value):
    high = value.astype(BF16)
    low = (value - high.astype(F32)).astype(BF16)
    return high, low


def route_kernel(cap, slabs, width, classes_ref, images_ref, eye_ref, order_ref, out_ref, lines):
    count, _, _, grid = images_ref.shape
    halves = LANES // width
    piece = grid // halves
    lane = lax.broadcasted_iota(jnp.int32, (piece, LANES), 1)
    lines[...] = jnp.zeros_like(lines)

    def place(p, carry):
        own = classes_ref[p, 0]
        rank = 0
        for q in range(count):
            rank = rank + jnp.where((classes_ref[q, 0] == own) & (q < p), 1, 0)
        image = images_ref[p].reshape(-1, grid)
        turned = dot(dot_t(eye_ref[...], image).astype(BF16), order_ref[...])
        for w in range(slabs):
            tile = w * width // LANES * LANES
            block = jnp.zeros((piece, LANES), F32)
            for h in range(halves):
                part = turned[h * piece : (h + 1) * piece, tile : tile + LANES]
                shift = (h * width - (w * width - tile)) % LANES
                part = part if shift == 0 else pltpu.roll(part, shift, 1)
                block = jnp.where((lane >= h * width) & (lane < (h + 1) * width), part, block)
            lines[own * slabs + w, pl.ds(rank, piece, stride=cap), :] = block
        return carry

    lax.fori_loop(0, count, place, 0, unroll=2)
    out_ref[...] = lines[...].astype(BF16).reshape(out_ref.shape)


def route_call(images, assignment, eye, order, class_count, slabs, width, cap):
    count, grid = images.shape[0], images.shape[1]
    rows = grid // (LANES // width) * cap
    vmem = pl.BlockSpec(memory_space=VMEM)
    return pl.pallas_call(
        functools.partial(route_kernel, cap, slabs, width),
        out_shape=jax.ShapeDtypeStruct((class_count * slabs, rows // 16, 16, LANES), BF16),
        in_specs=[pl.BlockSpec(memory_space=pltpu.SMEM)] + [vmem] * 3,
        out_specs=vmem,
        scratch_shapes=[VMEM((class_count * slabs, rows, LANES), F32)],
        compiler_params=pltpu.CompilerParams(vmem_limit_bytes=48 * 2**20),
        name="route",
    )(assignment, images, eye, order)


def score_kernel(cap, dirs, unit, images_ref, kept_ref, joined_ref, out_ref, sums):
    sources, groups, rows16, _ = images_ref.shape
    rows = sources * rows16
    steps = rows16 // cap
    sums[...] = jnp.zeros_like(sums)
    lane = lax.broadcasted_iota(jnp.int32, (steps * dirs, LANES), 1)
    even = (lane & unit) == 0

    def step(g, carry):
        kept = kept_ref[g].astype(F32)
        joined = joined_ref[g].astype(F32)
        refs = [
            jnp.where(even, kept, pltpu.roll(joined, unit, 1)).astype(BF16),
            jnp.where(even, pltpu.roll(kept, LANES - unit, 1), joined).astype(BF16),
        ]
        blocks = [images_ref[:, pl.ds(g + i * (groups // 2), 1), :, :].reshape(rows, LANES) for i in range(2)]
        sums[...] += dot_t(jnp.concatenate(refs, axis=1), jnp.concatenate(blocks, axis=1))
        return carry

    lax.fori_loop(0, groups // 2, step, 0, unroll=2)
    column = lax.broadcasted_iota(jnp.int32, (dirs, rows), 1)
    part = (column & (rows16 - 1)) // cap
    kept = jnp.zeros((dirs, rows), F32)
    for j in range(steps):
        kept = kept + jnp.where(part == j, sums[j * dirs : (j + 1) * dirs, :], 0.0)
    slots = sources * cap
    row_id = lax.broadcasted_iota(jnp.int32, (rows, slots), 0)
    slot_id = lax.broadcasted_iota(jnp.int32, (rows, slots), 1)
    gather = (row_id // rows16 * cap + row_id % cap) == slot_id
    out_ref[...] = jnp.dot(
        kept, gather.astype(F32), preferred_element_type=F32, precision=lax.Precision.HIGHEST
    )


def scores_call(images, kept, joined, cap, dirs, unit):
    sources, groups, rows16, _ = images.shape
    return pl.pallas_call(
        functools.partial(score_kernel, cap, dirs, unit),
        out_shape=jax.ShapeDtypeStruct((dirs, sources * cap), F32),
        in_specs=[pl.BlockSpec(memory_space=VMEM)] * 3,
        out_specs=pl.BlockSpec(memory_space=VMEM),
        scratch_shapes=[VMEM((kept.shape[1], sources * rows16), F32)],
        compiler_params=pltpu.CompilerParams(vmem_limit_bytes=48 * 2**20),
        name="scores",
    )(images, kept, joined)


def scatter_kernel(
    cap,
    width,
    grid,
    turns_ref,
    chunk_row_ref,
    chunk_start_ref,
    chunk_size_ref,
    point_ref,
    parts_ref,
    images_ref,
    weights_ref,
    out_ref,
    values,
    sums,
    spread,
    *buffers,
):
    sources, groups, rows16, _ = images_ref.shape
    rows = sources * rows16
    steps = rows16 // cap
    dirs, slots = parts_ref.shape[1:]
    joined = steps * dirs
    halves = LANES // width

    total = parts_ref[0]
    for i in range(1, parts_ref.shape[0]):
        total = total + parts_ref[i]
    expo = jnp.exp(total - jnp.max(total, axis=0, keepdims=True))
    posterior = (expo / jnp.sum(expo, axis=0, keepdims=True)).astype(BF16)
    slot_id = lax.broadcasted_iota(jnp.int32, (slots, rows), 0)
    row_id = lax.broadcasted_iota(jnp.int32, (slots, rows), 1)
    repeat = ((row_id // rows16 * cap + row_id % cap) == slot_id).astype(F32).astype(BF16)
    wide = dot(posterior, repeat)
    part = (lax.broadcasted_iota(jnp.int32, (dirs, rows), 1) & (rows16 - 1)) // cap
    for j in range(steps):
        spread[j * dirs : (j + 1) * dirs, :] = jnp.where(part == j, wide, 0.0).astype(BF16)

    lane_j = lax.broadcasted_iota(jnp.int32, (joined, LANES), 1)

    def average(g, carry):
        block = images_ref[:, pl.ds(g, 1), :, :].reshape(rows, LANES)
        mean = dot(spread[...], block)
        weight = weights_ref[g]
        for h in range(halves):
            shifted = mean if h == 0 else pltpu.roll(mean, LANES - h * width, 1)
            behind = pltpu.roll(weight, HALF - 8 * h, 1)
            start = pl.multiple_of((h * groups + g) * joined, joined)
            values[pl.ds(start, joined), :] = jnp.where(lane_j < HALF, shifted, behind)
        return carry

    lax.fori_loop(0, groups, average, 0, unroll=2)

    for buffer in buffers:
        buffer[...] = jnp.zeros_like(buffer)
    sums[...] = jnp.zeros_like(sums)

    place = lax.broadcasted_iota(jnp.int32, (CHUNK, LANES), 0)
    lane = lax.broadcasted_iota(jnp.int32, (CHUNK, grid), 1)
    at_y = lane.astype(F32).astype(BF16)
    at_next = ((lane + (grid - 1)) & (grid - 1)).astype(F32).astype(BF16)
    line_8 = lax.broadcasted_iota(jnp.int32, (8, LANES), 0)
    one = jnp.ones((CHUNK, grid), BF16)
    none = jnp.zeros((CHUNK, grid), BF16)

    def fetch(c, buffer):
        start = chunk_start_ref[c]
        for i in range(0, CHUNK, 8):
            block = jnp.broadcast_to(values[pl.ds(point_ref[start + i], 1), :], (8, LANES))
            for j in range(1, 8):
                line = jnp.broadcast_to(values[pl.ds(point_ref[start + i + j], 1), :], (8, LANES))
                block = jnp.where(line_8 == j, line, block)
            buffer[i : i + 8, :] = block

    def put(x, plane):
        for side in range(grid // LANES):
            out_ref[side, pl.ds(x, width, stride=grid + PAD), :] = plane[:, side * LANES : (side + 1) * LANES]

    def work(c, buffer):
        row = chunk_row_ref[c]
        before = chunk_row_ref[jnp.maximum(c - 1, 0)]
        data = buffer[...]
        y = jnp.broadcast_to(data[:, HALF + 4 : HALF + 5], (CHUNK, LANES))
        y = jnp.where(place < chunk_size_ref[c], y, -1.0).astype(BF16)
        y = jnp.concatenate([y] * (grid // LANES), axis=1)
        hot = jnp.concatenate([jnp.where(at_y == y, one, none), jnp.where(at_next == y, one, none)], axis=0)
        turned = data.T
        mean = turned[:width]
        weight = [jnp.broadcast_to(turned[HALF + j : HALF + j + 1], (width, CHUNK)) for j in range(4)]
        operand = jnp.concatenate(
            [
                jnp.concatenate([mean * weight[0], mean * weight[2]], axis=1),
                jnp.concatenate([mean * weight[1], mean * weight[3]], axis=1),
            ],
            axis=0,
        )
        high, low = two_terms(operand)
        result = dot(jnp.concatenate([high, low], axis=0), hot)
        result = result[: 2 * width] + result[2 * width :]
        same = row == before
        old_low, old_high = sums[:width], sums[width:]
        put((before + (grid - 1)) & (grid - 1), old_low)
        sums[:width] = result[:width] + jnp.where(same, old_low, old_high)
        sums[width:] = result[width:] + jnp.where(same, old_high, 0.0)

    fetch(0, buffers[0])

    def several(m, carry):
        for i in range(UNROLL):
            fetch(UNROLL * m + i + 1, buffers[(i + 1) % UNROLL])
            work(UNROLL * m + i, buffers[i])
        return carry

    lax.fori_loop(0, turns_ref[0], several, 0)
    put(grid - 2, sums[:width])
    for side in range(grid // LANES):
        wrapped = pl.ds(grid - 1, width, stride=grid + PAD)
        cut = slice(side * LANES, (side + 1) * LANES)
        out_ref[side, wrapped, :] = out_ref[side, wrapped, :] + sums[width:, cut]


def scatter_call(plan, parts, images, weights, cap, width, grid):
    sources, groups, rows16, _ = images.shape
    dirs = parts.shape[1]
    points = dirs * grid
    smem = pl.BlockSpec(memory_space=pltpu.SMEM)
    vmem = pl.BlockSpec(memory_space=VMEM)
    return pl.pallas_call(
        functools.partial(scatter_kernel, cap, width, grid),
        out_shape=jax.ShapeDtypeStruct((grid // LANES, width * (grid + PAD), LANES), F32),
        in_specs=[smem] * 5 + [vmem] * 3,
        out_specs=vmem,
        scratch_shapes=[
            VMEM((points, LANES), F32),
            VMEM((2 * width, grid), F32),
            VMEM((weights.shape[1], sources * rows16), BF16),
        ]
        + [VMEM((CHUNK, LANES), F32)] * UNROLL,
        compiler_params=pltpu.CompilerParams(vmem_limit_bytes=60 * 2**20),
        name="scatter",
    )(*plan, parts, images, weights)


def plane_kernel(slabs, grid, flag_ref, data_ref, yh_ref, yl_ref, xh_ref, xl_ref, out_ref, lines):
    pairs = data_ref.shape[2] // 2
    half = grid // 2
    rows = half + 8
    slab = grid // slabs
    count = 2 * pairs
    lane = lax.broadcasted_iota(jnp.int32, (grid, half), 1)
    last = (pl.program_id(0) == pl.num_programs(0) - 1) & (flag_ref[0] == 1)

    def along_y(plane):
        high, low = two_terms(plane)
        both = dot(high, yh_ref[...]) + dot(low, yh_ref[...]) + dot(high, yl_ref[...])
        return both[:, :half], both[:, half:]

    def transformed(real, imag):
        cos_r, sin_r = along_y(real)
        cos_i, sin_i = along_y(imag)
        zero_r = jnp.where(lane == 0, 0.0, sin_r)
        zero_i = jnp.where(lane == 0, 0.0, sin_i)
        real = jnp.concatenate([cos_r - zero_i, jnp.where(lane == 0, sin_r, cos_r + sin_i)], axis=1)
        imag = jnp.concatenate([cos_i + zero_r, jnp.where(lane == 0, sin_i, cos_i - sin_r)], axis=1)
        return real, imag

    def along_x(table, operand):
        high, low = operand
        start = table * rows
        upper, lower = xh_ref[start : start + rows], xl_ref[start : start + rows]
        return dot(upper, high) + dot(upper, low) + dot(lower, high)

    def one(i, carry):
        planes = [
            [
                jnp.concatenate([data_ref[part, side, 2 * i + r][:grid] for part in range(grid // LANES)], axis=1)
                for r in range(2)
            ]
            for side in range(2)
        ]
        (a_r, a_i), (b_r, b_i) = planes
        single = last & (i == pairs - 1)
        sum_r, sum_i = transformed(jnp.where(single, a_r, a_r + b_r), jnp.where(single, a_i, a_i + b_i))
        dif_r, dif_i = transformed(jnp.where(single, -b_i, a_r - b_r), jnp.where(single, b_r, a_i - b_i))
        cosine = along_x(0, two_terms(jnp.concatenate([sum_r, dif_i], axis=1)))
        sine = along_x(1, two_terms(jnp.concatenate([sum_i, dif_r], axis=1)))
        fields = (
            (cosine[:, :grid] - sine[:, :grid], cosine[:, :grid] + sine[:, :grid]),
            (cosine[:, grid:] + sine[:, grid:], cosine[:, grid:] - sine[:, grid:]),
        )
        for c in range(2):
            plus, minus = fields[c]
            for part in range(grid // LANES):
                cut = slice(part * LANES, (part + 1) * LANES)
                place = 2 * i + c
                lines[part, pl.ds(place, half, stride=count), :] = plus[:half, cut]
                lines[part, pl.ds(half * count + place, half, stride=count), :] = minus[1 : half + 1, cut]
        return carry

    lax.fori_loop(0, pairs, one, 0, unroll=2)
    for d in range(slabs):
        if d < slabs // 2:
            start = slab * d
        else:
            start = half + grid - slab * d - slab
        size = slab * count
        for part in range(grid // LANES):
            block = lines[part, start * count : start * count + size, :]
            out_ref[d, :, :, part * LANES : (part + 1) * LANES] = block.astype(BF16).reshape(slab, count, LANES)


def planes_call(flag, data, table_y, table_x, slabs, grid):
    parts, sides, values, pitch, _ = data.shape
    step = min(16, values)
    slab = grid // slabs
    fixed = lambda i, flag_ref: (0, 0)
    return pl.pallas_call(
        functools.partial(plane_kernel, slabs, grid),
        grid_spec=pltpu.PrefetchScalarGridSpec(
            num_scalar_prefetch=1,
            grid=(values // step,),
            in_specs=[
                pl.BlockSpec((parts, sides, step, pitch, LANES), lambda i, flag_ref: (0, 0, i, 0, 0)),
                pl.BlockSpec(table_y[0].shape, fixed),
                pl.BlockSpec(table_y[1].shape, fixed),
                pl.BlockSpec(table_x[0].shape, fixed),
                pl.BlockSpec(table_x[1].shape, fixed),
            ],
            out_specs=pl.BlockSpec((slabs, slab, step, grid), lambda i, flag_ref: (0, 0, i, 0)),
            scratch_shapes=[VMEM((parts, grid * step, LANES), F32)],
        ),
        out_shape=jax.ShapeDtypeStruct((slabs, slab, values, grid), BF16),
        compiler_params=pltpu.CompilerParams(vmem_limit_bytes=56 * 2**20),
        name="planes",
    )(flag, data, *table_y, *table_x)


def volume_kernel(flip_ref, data_ref, restore_ref, zh_ref, zl_ref, out_ref):
    slabs, span, width, grid = data_ref.shape
    for i in range(span):
        block = data_ref[:, i].reshape(slabs * width, grid)
        turned = dot_t(restore_ref[...], block).astype(BF16)
        value = dot(turned, zh_ref[...]) + dot(turned, zl_ref[...])
        out_ref[jnp.where(flip_ref[0] == 1, span - 1 - i, i)] = value


def volume_call(flip, data, restore, table_z):
    slabs, slab, width, grid = data.shape
    span = 4
    steps = slab // span
    fixed = lambda i, flip_ref: (0, 0)
    return pl.pallas_call(
        volume_kernel,
        grid_spec=pltpu.PrefetchScalarGridSpec(
            num_scalar_prefetch=1,
            grid=(steps,),
            in_specs=[
                pl.BlockSpec((slabs, span, width, grid), lambda i, flip_ref: (0, i, 0, 0)),
                pl.BlockSpec(restore.shape, fixed),
                pl.BlockSpec(table_z[0].shape, fixed),
                pl.BlockSpec(table_z[1].shape, fixed),
            ],
            out_specs=pl.BlockSpec(
                (span, grid, grid), lambda i, flip_ref: (jnp.where(flip_ref[0] == 1, steps - 1 - i, i), 0, 0)
            ),
        ),
        out_shape=jax.ShapeDtypeStruct((slab, grid, grid), F32),
        compiler_params=pltpu.CompilerParams(vmem_limit_bytes=48 * 2**20),
        name="volume",
    )(flip, data, restore, *table_z)


def sorted_points(interp_cells, grid):
    dirs = interp_cells.shape[0]
    points = dirs * grid
    base = interp_cells[:, 0, :].T.reshape(-1)
    row = (base // grid + 1) & (grid - 1)
    key = row * points + jnp.arange(points, dtype=jnp.int32)
    key = lax.sort(key, is_stable=False)
    rows = jnp.arange(grid, dtype=jnp.int32)
    count = jnp.sum((row[None, :] == rows[:, None]).astype(jnp.int32), axis=1)
    first = jnp.cumsum(count) - count
    chunks = jnp.maximum((count + (CHUNK - 1)) // CHUNK, 1)
    ends = jnp.cumsum(chunks)
    most = grid + points // CHUNK + UNROLL + 1
    number = jnp.arange(most, dtype=jnp.int32)
    chunk_row = jnp.minimum(jnp.sum((ends[None, :] <= number[:, None]).astype(jnp.int32), axis=1), grid - 1)
    mine = (rows[None, :] == chunk_row[:, None]).astype(jnp.int32)
    shift = first - (ends - chunks) * CHUNK
    chunk_start = jnp.sum(mine * shift[None, :], axis=1) + number * CHUNK
    row_end = jnp.sum(mine * (first + count)[None, :], axis=1)
    used = number < ends[-1]
    chunk_size = jnp.where(used, jnp.clip(row_end - chunk_start, 0, CHUNK), 0)
    chunk_start = jnp.where(used, chunk_start, points)
    turns = ((ends[-1] + (UNROLL - 1)) // UNROLL).reshape(1)
    point = jnp.concatenate([key & (points - 1), jnp.zeros((CHUNK,), jnp.int32)])
    return turns, chunk_row, chunk_start, chunk_size, point


def arrange_kernel(rows_ref, eye_ref, order_ref, kept_ref, sent_ref, *lines):
    dirs, count, _, grid = rows_ref.shape
    blocks = LANES // count
    length = grid // blocks
    lane = lax.broadcasted_iota(jnp.int32, (length, LANES), 1)

    def step(m, carry):
        block = rows_ref[pl.ds(blocks * m, blocks)].reshape(2 * LANES, grid)
        turned = dot(dot_t(eye_ref[...], block).astype(BF16), order_ref[...])
        for side in range(2):
            tile = [turned[q * length : (q + 1) * length, side * LANES : (side + 1) * LANES] for q in range(blocks)]
            for i in range(blocks):
                out = tile[i]
                for q in range(blocks):
                    if q != i:
                        moved = pltpu.roll(tile[q], (q - i) * count % LANES, 1)
                        out = jnp.where((lane >= q * count) & (lane < (q + 1) * count), moved, out)
                lines[side][pl.ds(blocks * m + i, length, stride=dirs), :] = out
        return carry

    lax.fori_loop(0, dirs // blocks, step, 0, unroll=2)
    kept_ref[...] = lines[0][...].astype(BF16).reshape(kept_ref.shape)
    sent_ref[...] = lines[1][...].astype(BF16).reshape(sent_ref.shape)


def arrange_call(rows, eye, order, steps):
    dirs, count, _, grid = rows.shape
    length = grid // (LANES // count)
    vmem = pl.BlockSpec(memory_space=VMEM)
    shape = jax.ShapeDtypeStruct((length // steps, steps * dirs, LANES), BF16)
    return pl.pallas_call(
        arrange_kernel,
        out_shape=(shape, shape),
        in_specs=[vmem] * 3,
        out_specs=(vmem, vmem),
        scratch_shapes=[VMEM((length * dirs, LANES), F32)] * 2,
        compiler_params=pltpu.CompilerParams(vmem_limit_bytes=48 * 2**20),
        name="arrange",
    )(rows, eye, order)


def row_orders(slab):
    half = slab // 2
    blocks = LANES // slab
    orders = []
    for kept, sent in (
        (range(1, half + 1), [*range(half + 1, slab), 0]),
        (range(half - 1, -1, -1), range(slab - 1, half - 1, -1)),
    ):
        order = np.zeros((2 * LANES, 2 * LANES), np.float32)
        for side, rows in enumerate((kept, sent)):
            for k in range(blocks):
                for i, row in enumerate(rows):
                    for r in range(2):
                        order[(k * slab + row) * 2 + r, side * LANES + k * slab + 2 * i + r] = 1.0
        orders.append(order.astype(jnp.bfloat16))
    return orders


def paired_rows(rows, other, eye, slabs, steps):
    own = lax.axis_index("vol")
    rows = jnp.concatenate([jnp.where(own <= slabs // 2, other, rows[:, :1]), rows[:, 1:]], axis=1)
    lower, upper = row_orders(rows.shape[1])
    order = jnp.where(own < slabs // 2, jnp.asarray(lower), jnp.asarray(upper))
    kept, sent = arrange_call(rows, eye, order, steps)
    arrived = lax.ppermute(sent, "vol", [(i, slabs - 1 - i) for i in range(slabs)])
    return kept, arrived


def shards(images, projections, assignment, interp_cells, interp_weights):
    class_count = lax.axis_size("cls")
    slab_count = lax.axis_size("vol")
    local_count, grid = images.shape[0], images.shape[1]
    dirs = projections.shape[1]
    slab = grid // slab_count
    width = 2 * slab
    halves = LANES // width
    capacity = 2 * local_count // class_count
    steps = 16 // capacity
    groups = grid // (halves * steps)

    eye = jnp.asarray(np.eye(grid), BF16)
    order = jnp.asarray(lane_order(grid, slab_count))
    outgoing = route_call(images, assignment, eye, order, class_count, slab_count, width, capacity)
    first = [(0, slab_count // 2)] + [(i, i - 1) for i in range(1, slab_count // 2 + 1)]
    other = lax.ppermute(projections[0, :, :1], "vol", first)
    outgoing, projections, other = lax.optimization_barrier((outgoing, projections, other))
    arrived = lax.all_to_all(outgoing, ("cls", "vol"), split_axis=0, concat_axis=0, tiled=True)

    kept, joined = paired_rows(projections[0], other, eye, slab_count, steps)
    corner_y = (interp_cells[:, 0:1, :] & (grid - 1)).astype(F32)
    weights = jnp.concatenate([interp_weights, corner_y, jnp.zeros((dirs, 3, grid), F32)], axis=1)
    weights = weights.reshape(dirs, 8, halves, groups, steps)
    weights = jnp.transpose(weights, (3, 4, 0, 2, 1)).reshape(groups, steps * dirs, 8 * halves)
    weights = jnp.pad(weights, ((0, 0), (0, 0), (0, LANES - 8 * halves)))
    plan = sorted_points(interp_cells, grid)
    table_y, table_x, table_z, restore = tables(grid, slab_count)

    arrived, kept, joined, weights, plan = lax.optimization_barrier((arrived, kept, joined, weights, plan))
    partial_value = scores_call(arrived, kept, joined, capacity, dirs, slab)
    copies = jnp.broadcast_to(partial_value[None], (slab_count,) + partial_value.shape)
    parts = lax.all_to_all(copies, "vol", split_axis=0, concat_axis=0, tiled=True)
    plane = scatter_call(plan, parts, arrived, weights, capacity, width, grid)
    plane = plane.reshape(grid // LANES, 2, slab, grid + PAD, LANES)
    own = lax.axis_index("vol")
    single = (own == slab_count // 2).astype(jnp.int32).reshape(1)
    flip = (own >= slab_count // 2).astype(jnp.int32).reshape(1)
    sent = planes_call(single, plane, table_y, table_x, slab_count, grid)
    received = lax.all_to_all(sent, "vol", split_axis=0, concat_axis=0, tiled=True)
    return volume_call(flip, received, restore, table_z)[None]


def solution(mesh):
    in_specs = (
        P(("cls", "vol"), None, None, None),
        P("cls", None, "vol", None, None),
        P(("cls", "vol"), None),
        P(),
        P(),
    )
    out_specs = P("cls", "vol", None, None)
    return jax.shard_map(shards, mesh=mesh, in_specs=in_specs, out_specs=out_specs, check_vma=False)
```

```python
import functools
import math

import jax
import jax.numpy as jnp
import numpy as np
from jax import lax
from jax.experimental import pallas as pl
from jax.experimental.pallas import tpu as pltpu
from jax.sharding import PartitionSpec as P

F32 = jnp.float32
BF16 = jnp.bfloat16
LANES = 128
HALF = 64
CHUNK = 128
PAD = 8
UNROLL = 8
STEP = 16
VMEM = pltpu.VMEM


def split_table(table):
    high = table.astype(jnp.bfloat16)
    low = (table - high.astype(np.float64)).astype(jnp.bfloat16)
    return high, low


def plane_pairs(grid, slabs):
    slab = grid // slabs
    half = slab // 2
    pairs = []
    for w in range(slabs):
        for i in range(half):
            if w < slabs // 2:
                first = slab * w + 1 + i
            else:
                first = slab * w + half - 1 - i
            if 2 * first == grid:
                pairs.append((0, first))
            else:
                pairs.append((first, grid - first))
    return np.array(pairs).reshape(slabs, half, 2)


def tables(grid, slabs):
    half = grid // 2
    scale = 1.0 / math.sqrt(grid)
    index = np.arange(grid)
    angle = 2.0 * np.pi / grid
    phase = (index[:, None] * np.arange(half)[None, :]) % grid
    cosine = np.cos(phase * angle)
    sine = np.sin(phase * angle)
    sine[:, 0] = np.cos(((index * half) % grid) * angle)
    table_y = np.concatenate([cosine, sine], axis=1) * scale
    rows = half + 8
    phase = (np.arange(rows)[:, None] * index[None, :]) % grid
    live = (np.arange(rows) <= half)[:, None]
    table_x = np.concatenate([np.cos(phase * angle) * live, np.sin(phase * angle) * live], axis=0) * scale
    pairs = plane_pairs(grid, slabs).reshape(-1, 2)
    single = (2 * pairs[:, 1] == grid)[:, None]
    z = np.where(single[:, 0], pairs[:, 1], pairs[:, 0])
    phase = (z[:, None] * index[None, :]) % grid
    for_sum = np.where(single, 1.0, np.cos(phase * angle))
    for_difference = np.where(single, np.cos(phase * angle), -np.sin(phase * angle))
    table_z = np.stack([for_sum, for_difference], axis=1).reshape(grid, grid) * scale
    order = np.concatenate([np.arange(half), [half], np.arange(grid - 1, half, -1)])
    restore = (order[None, :] == index[:, None]).astype(jnp.bfloat16)
    parts = max(1, grid // slabs // STEP)
    table_z = table_z.reshape(slabs, parts, -1, grid).transpose(1, 0, 2, 3).reshape(grid, grid)
    high, low = split_table(table_y)
    table_y = np.concatenate([high, high, low], axis=0)
    high, low = split_table(table_x)
    table_x = np.concatenate([high, high, low], axis=1)
    table_z = np.concatenate(split_table(table_z), axis=0)
    return table_y, table_x, table_z, restore


def lane_order(grid, slabs):
    rows = plane_pairs(grid, slabs).transpose(0, 2, 1).reshape(-1)
    source = (2 * rows[:, None] + np.arange(2)[None, :]).reshape(-1)
    return (np.arange(2 * grid)[:, None] == source[None, :]).astype(jnp.bfloat16)


def dot(a, b):
    return jnp.dot(a, b, preferred_element_type=F32)


def dot_t(a, b):
    return lax.dot_general(a, b, (((1,), (1,)), ((), ())), preferred_element_type=F32)


def two_terms(value):
    high = value.astype(BF16)
    low = (value - high.astype(F32)).astype(BF16)
    return high, low


def route_kernel(cap, slabs, width, classes_ref, images_ref, eye_ref, order_ref, out_ref, lines):
    count, _, _, grid = images_ref.shape
    halves = LANES // width
    piece = grid // halves
    lane = lax.broadcasted_iota(jnp.int32, (piece, LANES), 1)
    lines[...] = jnp.zeros_like(lines)

    def place(p, carry):
        own = classes_ref[p, 0]
        rank = 0
        for q in range(count):
            rank = rank + jnp.where((classes_ref[q, 0] == own) & (q < p), 1, 0)
        image = images_ref[p].reshape(-1, grid)
        turned = dot(dot_t(eye_ref[...], image).astype(BF16), order_ref[...])
        for w in range(slabs):
            tile = w * width // LANES * LANES
            block = jnp.zeros((piece, LANES), F32)
            for h in range(halves):
                part = turned[h * piece : (h + 1) * piece, tile : tile + LANES]
                shift = (h * width - (w * width - tile)) % LANES
                part = part if shift == 0 else pltpu.roll(part, shift, 1)
                block = jnp.where((lane >= h * width) & (lane < (h + 1) * width), part, block)
            lines[own * slabs + w, pl.ds(rank, piece, stride=cap), :] = block
        return carry

    lax.fori_loop(0, count, place, 0, unroll=2)
    out_ref[...] = lines[...].astype(BF16).reshape(out_ref.shape)


def route_call(images, assignment, eye, order, class_count, slabs, width, cap):
    count, grid = images.shape[0], images.shape[1]
    rows = grid // (LANES // width) * cap
    vmem = pl.BlockSpec(memory_space=VMEM)
    return pl.pallas_call(
        functools.partial(route_kernel, cap, slabs, width),
        out_shape=jax.ShapeDtypeStruct((class_count * slabs, rows // 16, 16, LANES), BF16),
        in_specs=[pl.BlockSpec(memory_space=pltpu.SMEM)] + [vmem] * 3,
        out_specs=vmem,
        scratch_shapes=[VMEM((class_count * slabs, rows, LANES), F32)],
        compiler_params=pltpu.CompilerParams(vmem_limit_bytes=48 * 2**20),
        name="route",
    )(assignment, images, eye, order)


def score_kernel(cap, dirs, unit, images_ref, kept_ref, joined_ref, out_ref, sums):
    sources, groups, rows16, _ = images_ref.shape
    rows = sources * rows16
    steps = rows16 // cap
    sums[...] = jnp.zeros_like(sums)
    lane = lax.broadcasted_iota(jnp.int32, (steps * dirs, LANES), 1)
    even = (lane & unit) == 0

    def step(g, carry):
        kept = kept_ref[g].astype(F32)
        joined = joined_ref[g].astype(F32)
        refs = [
            jnp.where(even, kept, pltpu.roll(joined, unit, 1)).astype(BF16),
            jnp.where(even, pltpu.roll(kept, LANES - unit, 1), joined).astype(BF16),
        ]
        blocks = [images_ref[:, pl.ds(g + i * (groups // 2), 1), :, :].reshape(rows, LANES) for i in range(2)]
        sums[...] += dot_t(jnp.concatenate(refs, axis=1), jnp.concatenate(blocks, axis=1))
        return carry

    lax.fori_loop(0, groups // 2, step, 0, unroll=2)
    column = lax.broadcasted_iota(jnp.int32, (dirs, rows), 1)
    part = (column & (rows16 - 1)) // cap
    kept = jnp.zeros((dirs, rows), F32)
    for j in range(steps):
        kept = kept + jnp.where(part == j, sums[j * dirs : (j + 1) * dirs, :], 0.0)
    slots = sources * cap
    row_id = lax.broadcasted_iota(jnp.int32, (rows, slots), 0)
    slot_id = lax.broadcasted_iota(jnp.int32, (rows, slots), 1)
    gather = (row_id // rows16 * cap + row_id % cap) == slot_id
    out_ref[...] = jnp.dot(
        kept, gather.astype(F32), preferred_element_type=F32, precision=lax.Precision.HIGHEST
    )


def scores_call(images, kept, joined, cap, dirs, unit):
    sources, groups, rows16, _ = images.shape
    return pl.pallas_call(
        functools.partial(score_kernel, cap, dirs, unit),
        out_shape=jax.ShapeDtypeStruct((dirs, sources * cap), F32),
        in_specs=[pl.BlockSpec(memory_space=VMEM)] * 3,
        out_specs=pl.BlockSpec(memory_space=VMEM),
        scratch_shapes=[VMEM((kept.shape[1], sources * rows16), F32)],
        compiler_params=pltpu.CompilerParams(vmem_limit_bytes=48 * 2**20),
        name="scores",
    )(images, kept, joined)


def scatter_kernel(
    cap,
    width,
    grid,
    first_ref,
    point_ref,
    parts_ref,
    images_ref,
    weights_ref,
    out_ref,
    values,
    sums,
    spread,
    *buffers,
):
    sources, groups, rows16, _ = images_ref.shape
    rows = sources * rows16
    steps = rows16 // cap
    dirs, slots = parts_ref.shape[1:]
    joined = steps * dirs
    halves = LANES // width

    total = parts_ref[0]
    for i in range(1, parts_ref.shape[0]):
        total = total + parts_ref[i]
    expo = jnp.exp(total - jnp.max(total, axis=0, keepdims=True))
    posterior = (expo / jnp.sum(expo, axis=0, keepdims=True)).astype(BF16)
    slot_id = lax.broadcasted_iota(jnp.int32, (slots, rows), 0)
    row_id = lax.broadcasted_iota(jnp.int32, (slots, rows), 1)
    repeat = ((row_id // rows16 * cap + row_id % cap) == slot_id).astype(F32).astype(BF16)
    wide = dot(posterior, repeat)
    part = (lax.broadcasted_iota(jnp.int32, (dirs, rows), 1) & (rows16 - 1)) // cap
    for j in range(steps):
        spread[j * dirs : (j + 1) * dirs, :] = jnp.where(part == j, wide, 0.0).astype(BF16)

    lane_j = lax.broadcasted_iota(jnp.int32, (joined, LANES), 1)

    def average(g, carry):
        block = images_ref[:, pl.ds(g, 1), :, :].reshape(rows, LANES)
        mean = dot(spread[...], block)
        weight = weights_ref[g]
        for h in range(halves):
            shifted = mean if h == 0 else pltpu.roll(mean, LANES - h * width, 1)
            behind = pltpu.roll(weight, HALF - 8 * h, 1)
            start = pl.multiple_of((h * groups + g) * joined, joined)
            values[pl.ds(start, joined), :] = jnp.where(lane_j < HALF, shifted, behind)
        return carry

    lax.fori_loop(0, groups, average, 0, unroll=2)

    for buffer in buffers:
        buffer[...] = jnp.zeros_like(buffer)
    sums[...] = jnp.zeros_like(sums)

    place = lax.broadcasted_iota(jnp.int32, (CHUNK, LANES), 0)
    lane = lax.broadcasted_iota(jnp.int32, (CHUNK, grid), 1)
    at_y = lane.astype(F32).astype(BF16)
    at_next = ((lane + (grid - 1)) & (grid - 1)).astype(F32).astype(BF16)
    line_8 = lax.broadcasted_iota(jnp.int32, (8, LANES), 0)
    one = jnp.ones((CHUNK, grid), BF16)
    none = jnp.zeros((CHUNK, grid), BF16)

    lane_1 = lax.broadcasted_iota(jnp.int32, (1, CHUNK), 1)
    points = values.shape[0]

    def fetch(start, buffer):
        for i in range(0, CHUNK, 8):
            block = jnp.broadcast_to(values[pl.ds(point_ref[start + i], 1), :], (8, LANES))
            for j in range(1, 8):
                line = jnp.broadcast_to(values[pl.ds(point_ref[start + i + j], 1), :], (8, LANES))
                block = jnp.where(line_8 == j, line, block)
            buffer[i : i + 8, :] = block

    def put(row, plane):
        x = (row + (grid - 1)) & (grid - 1)
        for side in range(grid // LANES):
            out_ref[side, pl.ds(x, width, stride=grid + PAD), :] = plane[:, side * LANES : (side + 1) * LANES]

    def following(start, row):
        second, third = first_ref[row + 1], first_ref[row + 2]
        end = jnp.minimum(start + CHUNK, third)
        moved = row + jnp.where(end >= second, 1, 0) + jnp.where(end >= third, 1, 0)
        return end, jnp.minimum(moved, grid - 1), end - start, jnp.clip(second - start, 0, end - start)

    def work(row, before, size, size_0, buffer):
        data = buffer[...]
        y = jnp.broadcast_to(data[:, HALF + 4 : HALF + 5], (CHUNK, LANES))
        y = jnp.where(place < size, y, -1.0).astype(BF16)
        y = jnp.concatenate([y] * (grid // LANES), axis=1)
        hot = jnp.concatenate([jnp.where(at_y == y, one, none), jnp.where(at_next == y, one, none)], axis=0)
        turned = data.T
        mean = turned[:width]
        weight = [turned[HALF + j : HALF + j + 1] for j in range(4)]
        here = [jnp.where(lane_1 < size_0, w, 0.0) for w in weight]
        there = [w - h for w, h in zip(weight, here)]
        by_row = (
            (here[0], here[2]),
            (here[1] + there[0], here[3] + there[2]),
            (there[1], there[3]),
        )
        operand = jnp.concatenate(
            [
                jnp.concatenate([mean * jnp.broadcast_to(w, (width, CHUNK)) for w in pair], axis=1)
                for pair in by_row
            ],
            axis=0,
        )
        high, low = two_terms(operand)
        result = dot(jnp.concatenate([high, low], axis=0), hot)
        result = result[: 3 * width] + result[3 * width :]
        old = [sums[i * width : (i + 1) * width] for i in range(3)]
        put(jnp.minimum(before + 1, grid - 1), old[1])
        put(before, old[0])
        stay, by_one = row == before, row == before + 1
        kept = (
            jnp.where(stay, old[0], jnp.where(by_one, old[1], old[2])),
            jnp.where(stay, old[1], jnp.where(by_one, old[2], 0.0)),
            jnp.where(stay, old[2], 0.0),
        )
        for i in range(3):
            sums[i * width : (i + 1) * width] = result[i * width : (i + 1) * width] + kept[i]

    fetch(0, buffers[0])

    def several(state):
        start, row, before = state
        for i in range(UNROLL):
            end, moved, size, size_0 = following(start, row)
            fetch(end, buffers[(i + 1) % UNROLL])
            work(row, before, size, size_0, buffers[i])
            start, row, before = end, moved, row
        return start, row, before

    zero = jnp.int32(0)
    lax.while_loop(lambda state: (state[0] < points) | (state[2] < grid - 1), several, (zero, zero, zero))
    put(grid - 1, sums[:width])
    for side in range(grid // LANES):
        wrapped = pl.ds(grid - 1, width, stride=grid + PAD)
        cut = slice(side * LANES, (side + 1) * LANES)
        out_ref[side, wrapped, :] = out_ref[side, wrapped, :] + sums[width : 2 * width, cut]


def scatter_call(plan, parts, images, weights, cap, width, grid):
    sources, groups, rows16, _ = images.shape
    dirs = parts.shape[1]
    points = dirs * grid
    smem = pl.BlockSpec(memory_space=pltpu.SMEM)
    vmem = pl.BlockSpec(memory_space=VMEM)
    return pl.pallas_call(
        functools.partial(scatter_kernel, cap, width, grid),
        out_shape=jax.ShapeDtypeStruct((grid // LANES, width * (grid + PAD), LANES), F32),
        in_specs=[smem] * 2 + [vmem] * 3,
        out_specs=vmem,
        scratch_shapes=[
            VMEM((points, LANES), F32),
            VMEM((3 * width, grid), F32),
            VMEM((weights.shape[1], sources * rows16), BF16),
        ]
        + [VMEM((CHUNK, LANES), F32)] * UNROLL,
        compiler_params=pltpu.CompilerParams(vmem_limit_bytes=60 * 2**20),
        name="scatter",
    )(*plan, parts, images, weights)


def plane_kernel(slabs, grid, final, flag_ref, data_ref, y_ref, x_ref, out_ref, lines):
    pairs = data_ref.shape[2] // 2
    half = grid // 2
    rows = half + 8
    slab = grid // slabs
    count = 2 * pairs
    lane = lax.broadcasted_iota(jnp.int32, (grid, half), 1)
    last = (flag_ref[0] == 1) & final

    def along_y(plane):
        high, low = two_terms(plane)
        both = dot(jnp.concatenate([high, low, high], axis=1), y_ref[...])
        return both[:, :half], both[:, half:]

    def transformed(real, imag):
        cos_r, sin_r = along_y(real)
        cos_i, sin_i = along_y(imag)
        zero_r = jnp.where(lane == 0, 0.0, sin_r)
        zero_i = jnp.where(lane == 0, 0.0, sin_i)
        real = jnp.concatenate([cos_r - zero_i, jnp.where(lane == 0, sin_r, cos_r + sin_i)], axis=1)
        imag = jnp.concatenate([cos_i + zero_r, jnp.where(lane == 0, sin_i, cos_i - sin_r)], axis=1)
        return real, imag

    def along_x(table, operand):
        high, low = operand
        start = table * rows
        return dot(x_ref[start : start + rows], jnp.concatenate([high, low, high], axis=0))

    def one(i, carry):
        planes = [
            [
                jnp.concatenate([data_ref[part, side, 2 * i + r][:grid] for part in range(grid // LANES)], axis=1)
                for r in range(2)
            ]
            for side in range(2)
        ]
        (a_r, a_i), (b_r, b_i) = planes
        single = last & (i == pairs - 1)
        sum_r, sum_i = transformed(jnp.where(single, a_r, a_r + b_r), jnp.where(single, a_i, a_i + b_i))
        dif_r, dif_i = transformed(jnp.where(single, -b_i, a_r - b_r), jnp.where(single, b_r, a_i - b_i))
        cosine = along_x(0, two_terms(jnp.concatenate([sum_r, dif_i], axis=1)))
        sine = along_x(1, two_terms(jnp.concatenate([sum_i, dif_r], axis=1)))
        fields = (
            (cosine[:, :grid] - sine[:, :grid], cosine[:, :grid] + sine[:, :grid]),
            (cosine[:, grid:] + sine[:, grid:], cosine[:, grid:] - sine[:, grid:]),
        )
        for c in range(2):
            plus, minus = fields[c]
            for part in range(grid // LANES):
                cut = slice(part * LANES, (part + 1) * LANES)
                place = 2 * i + c
                lines[part, pl.ds(place, half, stride=count), :] = plus[:half, cut]
                lines[part, pl.ds(half * count + place, half, stride=count), :] = minus[1 : half + 1, cut]
        return carry

    lax.fori_loop(0, pairs, one, 0, unroll=2)
    for d in range(slabs):
        if d < slabs // 2:
            start = slab * d
        else:
            start = half + grid - slab * d - slab
        size = slab * count
        for part in range(grid // LANES):
            block = lines[part, start * count : start * count + size, :]
            out_ref[d, :, :, part * LANES : (part + 1) * LANES] = block.astype(BF16).reshape(slab, count, LANES)


def planes_call(flag, data, table_y, table_x, slabs, grid, part):
    parts, sides, values, pitch, _ = data.shape
    step = min(STEP, values)
    slab = grid // slabs
    final = part == values // step - 1
    fixed = lambda i, flag_ref: (0, 0)
    return pl.pallas_call(
        functools.partial(plane_kernel, slabs, grid, final),
        grid_spec=pltpu.PrefetchScalarGridSpec(
            num_scalar_prefetch=1,
            grid=(1,),
            in_specs=[
                pl.BlockSpec((parts, sides, step, pitch, LANES), lambda i, flag_ref: (0, 0, part, 0, 0)),
                pl.BlockSpec(table_y.shape, fixed),
                pl.BlockSpec(table_x.shape, fixed),
            ],
            out_specs=pl.BlockSpec((slabs, slab, step, grid), lambda i, flag_ref: (0, 0, 0, 0)),
            scratch_shapes=[VMEM((parts, grid * step, LANES), F32)],
        ),
        out_shape=jax.ShapeDtypeStruct((slabs, slab, step, grid), BF16),
        compiler_params=pltpu.CompilerParams(vmem_limit_bytes=56 * 2**20),
        name="planes",
    )(flag, data, table_y, table_x)


def volume_kernel(flip_ref, restore_ref, z_ref, *refs):
    out_ref = refs[-1]
    slabs, span, width, grid = refs[0].shape
    for i in range(span):
        block = jnp.concatenate([ref[:, i].reshape(slabs * width, grid) for ref in refs[:-1]], axis=0)
        turned = dot_t(restore_ref[...], block).astype(BF16)
        value = dot(jnp.concatenate([turned, turned], axis=1), z_ref[...])
        out_ref[jnp.where(flip_ref[0] == 1, span - 1 - i, i)] = value


def volume_call(flip, parts, restore, table_z):
    slabs, slab, width, grid = parts[0].shape
    span = 4
    steps = slab // span
    fixed = lambda i, flip_ref: (0, 0)
    return pl.pallas_call(
        volume_kernel,
        grid_spec=pltpu.PrefetchScalarGridSpec(
            num_scalar_prefetch=1,
            grid=(steps,),
            in_specs=[pl.BlockSpec(restore.shape, fixed), pl.BlockSpec(table_z.shape, fixed)]
            + [pl.BlockSpec((slabs, span, width, grid), lambda i, flip_ref: (0, i, 0, 0))] * len(parts),
            out_specs=pl.BlockSpec(
                (span, grid, grid), lambda i, flip_ref: (jnp.where(flip_ref[0] == 1, steps - 1 - i, i), 0, 0)
            ),
        ),
        out_shape=jax.ShapeDtypeStruct((slab, grid, grid), F32),
        compiler_params=pltpu.CompilerParams(vmem_limit_bytes=48 * 2**20),
        name="volume",
    )(flip, restore, table_z, *parts)


def sorted_points(interp_cells, grid):
    dirs = interp_cells.shape[0]
    points = dirs * grid
    base = interp_cells[:, 0, :].T.reshape(-1)
    row = (base // grid + 1) & (grid - 1)
    key = row * points + jnp.arange(points, dtype=jnp.int32)
    key = lax.sort(key, is_stable=False)
    rows = jnp.arange(grid + 3, dtype=jnp.int32)
    first = jnp.sum((row[None, :] < rows[:, None]).astype(jnp.int32), axis=1)
    point = jnp.concatenate([key & (points - 1), jnp.zeros((CHUNK,), jnp.int32)])
    return first, point


def arrange_kernel(rows_ref, eye_ref, order_ref, kept_ref, sent_ref, *lines):
    dirs, count, _, grid = rows_ref.shape
    blocks = LANES // count
    length = grid // blocks
    lane = lax.broadcasted_iota(jnp.int32, (length, LANES), 1)

    def step(m, carry):
        block = rows_ref[pl.ds(blocks * m, blocks)].reshape(2 * LANES, grid)
        turned = dot(dot_t(eye_ref[...], block).astype(BF16), order_ref[...])
        for side in range(2):
            tile = [turned[q * length : (q + 1) * length, side * LANES : (side + 1) * LANES] for q in range(blocks)]
            for i in range(blocks):
                out = tile[i]
                for q in range(blocks):
                    if q != i:
                        moved = pltpu.roll(tile[q], (q - i) * count % LANES, 1)
                        out = jnp.where((lane >= q * count) & (lane < (q + 1) * count), moved, out)
                lines[side][pl.ds(blocks * m + i, length, stride=dirs), :] = out
        return carry

    lax.fori_loop(0, dirs // blocks, step, 0, unroll=2)
    kept_ref[...] = lines[0][...].astype(BF16).reshape(kept_ref.shape)
    sent_ref[...] = lines[1][...].astype(BF16).reshape(sent_ref.shape)


def arrange_call(rows, eye, order, steps):
    dirs, count, _, grid = rows.shape
    length = grid // (LANES // count)
    vmem = pl.BlockSpec(memory_space=VMEM)
    shape = jax.ShapeDtypeStruct((length // steps, steps * dirs, LANES), BF16)
    return pl.pallas_call(
        arrange_kernel,
        out_shape=(shape, shape),
        in_specs=[vmem] * 3,
        out_specs=(vmem, vmem),
        scratch_shapes=[VMEM((length * dirs, LANES), F32)] * 2,
        compiler_params=pltpu.CompilerParams(vmem_limit_bytes=48 * 2**20),
        name="arrange",
    )(rows, eye, order)


def row_orders(slab):
    half = slab // 2
    blocks = LANES // slab
    orders = []
    for kept, sent in (
        (range(1, half + 1), [*range(half + 1, slab), 0]),
        (range(half - 1, -1, -1), range(slab - 1, half - 1, -1)),
    ):
        order = np.zeros((2 * LANES, 2 * LANES), np.float32)
        for side, rows in enumerate((kept, sent)):
            for k in range(blocks):
                for i, row in enumerate(rows):
                    for r in range(2):
                        order[(k * slab + row) * 2 + r, side * LANES + k * slab + 2 * i + r] = 1.0
        orders.append(order.astype(jnp.bfloat16))
    return orders


def paired_rows(rows, other, eye, slabs, steps):
    own = lax.axis_index("vol")
    rows = jnp.concatenate([jnp.where(own <= slabs // 2, other, rows[:, :1]), rows[:, 1:]], axis=1)
    lower, upper = row_orders(rows.shape[1])
    order = jnp.where(own < slabs // 2, jnp.asarray(lower), jnp.asarray(upper))
    kept, sent = arrange_call(rows, eye, order, steps)
    arrived = lax.ppermute(sent, "vol", [(i, slabs - 1 - i) for i in range(slabs)])
    return kept, arrived


def shards(images, projections, assignment, interp_cells, interp_weights):
    class_count = lax.axis_size("cls")
    slab_count = lax.axis_size("vol")
    local_count, grid = images.shape[0], images.shape[1]
    dirs = projections.shape[1]
    slab = grid // slab_count
    width = 2 * slab
    halves = LANES // width
    capacity = 2 * local_count // class_count
    steps = 16 // capacity
    groups = grid // (halves * steps)

    eye = jnp.asarray(np.eye(grid), BF16)
    order = jnp.asarray(lane_order(grid, slab_count))
    outgoing = route_call(images, assignment, eye, order, class_count, slab_count, width, capacity)
    first = [(0, slab_count // 2)] + [(i, i - 1) for i in range(1, slab_count // 2 + 1)]
    other = lax.ppermute(projections[0, :, :1], "vol", first)
    outgoing, projections, other = lax.optimization_barrier((outgoing, projections, other))
    arrived = lax.all_to_all(outgoing, ("cls", "vol"), split_axis=0, concat_axis=0, tiled=True)

    kept, joined = paired_rows(projections[0], other, eye, slab_count, steps)
    corner_y = (interp_cells[:, 0:1, :] & (grid - 1)).astype(F32)
    weights = jnp.concatenate([interp_weights, corner_y, jnp.zeros((dirs, 3, grid), F32)], axis=1)
    weights = weights.reshape(dirs, 8, halves, groups, steps)
    weights = jnp.transpose(weights, (3, 4, 0, 2, 1)).reshape(groups, steps * dirs, 8 * halves)
    weights = jnp.pad(weights, ((0, 0), (0, 0), (0, LANES - 8 * halves)))
    plan = sorted_points(interp_cells, grid)
    table_y, table_x, table_z, restore = tables(grid, slab_count)

    arrived, kept, joined, weights, plan = lax.optimization_barrier((arrived, kept, joined, weights, plan))
    partial_value = scores_call(arrived, kept, joined, capacity, dirs, slab)
    copies = jnp.broadcast_to(partial_value[None], (slab_count,) + partial_value.shape)
    parts = lax.all_to_all(copies, "vol", split_axis=0, concat_axis=0, tiled=True)
    plane = scatter_call(plan, parts, arrived, weights, capacity, width, grid)
    plane = plane.reshape(grid // LANES, 2, slab, grid + PAD, LANES)
    own = lax.axis_index("vol")
    single = (own == slab_count // 2).astype(jnp.int32).reshape(1)
    flip = (own >= slab_count // 2).astype(jnp.int32).reshape(1)
    received = []
    for part in range(max(1, slab // STEP)):
        sent = planes_call(single, plane, table_y, table_x, slab_count, grid, part)
        received.append(lax.all_to_all(sent, "vol", split_axis=0, concat_axis=0, tiled=True))
    return volume_call(flip, received, restore, table_z)[None]


def solution(mesh):
    in_specs = (
        P(("cls", "vol"), None, None, None),
        P("cls", None, "vol", None, None),
        P(("cls", "vol"), None),
        P(),
        P(),
    )
    out_specs = P("cls", "vol", None, None)
    return jax.shard_map(shards, mesh=mesh, in_specs=in_specs, out_specs=out_specs, check_vma=False)
```

```python
import functools
import math

import jax
import jax.numpy as jnp
import numpy as np
from jax import lax
from jax.experimental import pallas as pl
from jax.experimental.pallas import tpu as pltpu
from jax.sharding import PartitionSpec as P

F32 = jnp.float32
BF16 = jnp.bfloat16
LANES = 128
HALF = 64
CHUNK = 128
PAD = 8
UNROLL = 8
STEP = 16
VMEM = pltpu.VMEM


def split_table(table):
    high = table.astype(jnp.bfloat16)
    low = (table - high.astype(np.float64)).astype(jnp.bfloat16)
    return high, low


def plane_pairs(grid, slabs):
    slab = grid // slabs
    half = slab // 2
    pairs = []
    for w in range(slabs):
        for i in range(half):
            if w < slabs // 2:
                first = slab * w + 1 + i
            else:
                first = slab * w + half - 1 - i
            if 2 * first == grid:
                pairs.append((0, first))
            else:
                pairs.append((first, grid - first))
    return np.array(pairs).reshape(slabs, half, 2)


def tables(grid, slabs):
    half = grid // 2
    scale = 1.0 / math.sqrt(grid)
    index = np.arange(grid)
    angle = 2.0 * np.pi / grid
    phase = (index[:, None] * np.arange(half)[None, :]) % grid
    cosine = np.cos(phase * angle)
    sine = np.sin(phase * angle)
    sine[:, 0] = np.cos(((index * half) % grid) * angle)
    table_y = np.concatenate([cosine, sine], axis=1) * scale
    rows = half + 8
    phase = (np.arange(rows)[:, None] * index[None, :]) % grid
    live = (np.arange(rows) <= half)[:, None]
    table_x = np.concatenate([np.cos(phase * angle) * live, np.sin(phase * angle) * live], axis=0) * scale
    pairs = plane_pairs(grid, slabs).reshape(-1, 2)
    single = (2 * pairs[:, 1] == grid)[:, None]
    z = np.where(single[:, 0], pairs[:, 1], pairs[:, 0])
    phase = (z[:, None] * index[None, :]) % grid
    for_sum = np.where(single, 1.0, np.cos(phase * angle))
    for_difference = np.where(single, np.cos(phase * angle), -np.sin(phase * angle))
    table_z = np.stack([for_sum, for_difference], axis=1).reshape(grid, grid) * scale
    order = np.concatenate([np.arange(half), [half], np.arange(grid - 1, half, -1)])
    restore = (order[None, :] == index[:, None]).astype(jnp.bfloat16)
    parts = max(1, grid // slabs // STEP)
    table_z = table_z.reshape(slabs, parts, -1, grid).transpose(1, 0, 2, 3).reshape(grid, grid)
    high, low = split_table(table_y)
    table_y = np.concatenate([high, high, low], axis=0)
    high, low = split_table(table_x)
    table_x = np.concatenate([high, high, low], axis=1)
    table_z = np.concatenate(split_table(table_z), axis=0)
    return table_y, table_x, table_z, restore


def lane_order(grid, slabs):
    rows = plane_pairs(grid, slabs).transpose(0, 2, 1).reshape(-1)
    source = (2 * rows[:, None] + np.arange(2)[None, :]).reshape(-1)
    return (np.arange(2 * grid)[:, None] == source[None, :]).astype(jnp.bfloat16)


def dot(a, b):
    return jnp.dot(a, b, preferred_element_type=F32)


def dot_t(a, b):
    return lax.dot_general(a, b, (((1,), (1,)), ((), ())), preferred_element_type=F32)


def two_terms(value):
    high = value.astype(BF16)
    low = (value - high.astype(F32)).astype(BF16)
    return high, low


def route_kernel(cap, slabs, width, classes_ref, images_ref, eye_ref, order_ref, out_ref, lines):
    count, _, _, grid = images_ref.shape
    halves = LANES // width
    piece = grid // halves
    lane = lax.broadcasted_iota(jnp.int32, (piece, LANES), 1)
    lines[...] = jnp.zeros_like(lines)

    def place(p, carry):
        own = classes_ref[p, 0]
        rank = 0
        for q in range(count):
            rank = rank + jnp.where((classes_ref[q, 0] == own) & (q < p), 1, 0)
        image = images_ref[p].reshape(-1, grid)
        turned = dot(dot_t(eye_ref[...], image).astype(BF16), order_ref[...])
        for w in range(slabs):
            tile = w * width // LANES * LANES
            block = jnp.zeros((piece, LANES), F32)
            for h in range(halves):
                part = turned[h * piece : (h + 1) * piece, tile : tile + LANES]
                shift = (h * width - (w * width - tile)) % LANES
                part = part if shift == 0 else pltpu.roll(part, shift, 1)
                block = jnp.where((lane >= h * width) & (lane < (h + 1) * width), part, block)
            lines[own * slabs + w, pl.ds(rank, piece, stride=cap), :] = block
        return carry

    lax.fori_loop(0, count, place, 0, unroll=2)
    out_ref[...] = lines[...].astype(BF16).reshape(out_ref.shape)


def route_call(images, assignment, eye, order, class_count, slabs, width, cap):
    count, grid = images.shape[0], images.shape[1]
    rows = grid // (LANES // width) * cap
    vmem = pl.BlockSpec(memory_space=VMEM)
    return pl.pallas_call(
        functools.partial(route_kernel, cap, slabs, width),
        out_shape=jax.ShapeDtypeStruct((class_count * slabs, rows // 16, 16, LANES), BF16),
        in_specs=[pl.BlockSpec(memory_space=pltpu.SMEM)] + [vmem] * 3,
        out_specs=vmem,
        scratch_shapes=[VMEM((class_count * slabs, rows, LANES), F32)],
        compiler_params=pltpu.CompilerParams(vmem_limit_bytes=48 * 2**20),
        name="route",
    )(assignment, images, eye, order)


def score_kernel(cap, dirs, unit, images_ref, kept_ref, joined_ref, out_ref, sums):
    sources, groups, rows16, _ = images_ref.shape
    rows = sources * rows16
    steps = rows16 // cap
    sums[...] = jnp.zeros_like(sums)
    lane = lax.broadcasted_iota(jnp.int32, (steps * dirs, LANES), 1)
    even = (lane & unit) == 0

    def step(g, carry):
        kept = kept_ref[g].astype(F32)
        joined = joined_ref[g].astype(F32)
        refs = [
            jnp.where(even, kept, pltpu.roll(joined, unit, 1)).astype(BF16),
            jnp.where(even, pltpu.roll(kept, LANES - unit, 1), joined).astype(BF16),
        ]
        blocks = [images_ref[:, pl.ds(g + i * (groups // 2), 1), :, :].reshape(rows, LANES) for i in range(2)]
        sums[...] += dot_t(jnp.concatenate(refs, axis=1), jnp.concatenate(blocks, axis=1))
        return carry

    lax.fori_loop(0, groups // 2, step, 0, unroll=2)
    column = lax.broadcasted_iota(jnp.int32, (dirs, rows), 1)
    part = (column & (rows16 - 1)) // cap
    kept = jnp.zeros((dirs, rows), F32)
    for j in range(steps):
        kept = kept + jnp.where(part == j, sums[j * dirs : (j + 1) * dirs, :], 0.0)
    slots = sources * cap
    row_id = lax.broadcasted_iota(jnp.int32, (rows, slots), 0)
    slot_id = lax.broadcasted_iota(jnp.int32, (rows, slots), 1)
    gather = (row_id // rows16 * cap + row_id % cap) == slot_id
    out_ref[...] = jnp.dot(
        kept, gather.astype(F32), preferred_element_type=F32, precision=lax.Precision.HIGHEST
    )


def scores_call(images, kept, joined, cap, dirs, unit):
    sources, groups, rows16, _ = images.shape
    return pl.pallas_call(
        functools.partial(score_kernel, cap, dirs, unit),
        out_shape=jax.ShapeDtypeStruct((dirs, sources * cap), F32),
        in_specs=[pl.BlockSpec(memory_space=VMEM)] * 3,
        out_specs=pl.BlockSpec(memory_space=VMEM),
        scratch_shapes=[VMEM((kept.shape[1], sources * rows16), F32)],
        compiler_params=pltpu.CompilerParams(vmem_limit_bytes=48 * 2**20),
        name="scores",
    )(images, kept, joined)


def scatter_kernel(
    cap,
    width,
    grid,
    single_ref,
    first_ref,
    point_ref,
    parts_ref,
    images_ref,
    weights_ref,
    out_ref,
    values,
    sums,
    spread,
    *buffers,
):
    sources, groups, rows16, _ = images_ref.shape
    rows = sources * rows16
    steps = rows16 // cap
    dirs, slots = parts_ref.shape[1:]
    joined = steps * dirs
    halves = LANES // width

    total = parts_ref[0]
    for i in range(1, parts_ref.shape[0]):
        total = total + parts_ref[i]
    expo = jnp.exp(total - jnp.max(total, axis=0, keepdims=True))
    posterior = (expo / jnp.sum(expo, axis=0, keepdims=True)).astype(BF16)
    slot_id = lax.broadcasted_iota(jnp.int32, (slots, rows), 0)
    row_id = lax.broadcasted_iota(jnp.int32, (slots, rows), 1)
    repeat = ((row_id // rows16 * cap + row_id % cap) == slot_id).astype(F32).astype(BF16)
    wide = dot(posterior, repeat)
    part = (lax.broadcasted_iota(jnp.int32, (dirs, rows), 1) & (rows16 - 1)) // cap
    for j in range(steps):
        spread[j * dirs : (j + 1) * dirs, :] = jnp.where(part == j, wide, 0.0).astype(BF16)

    lane_j = lax.broadcasted_iota(jnp.int32, (joined, LANES), 1)

    def average(g, carry):
        block = images_ref[:, pl.ds(g, 1), :, :].reshape(rows, LANES)
        mean = dot(spread[...], block)
        weight = weights_ref[g]
        for h in range(halves):
            shifted = mean if h == 0 else pltpu.roll(mean, LANES - h * width, 1)
            behind = pltpu.roll(weight, HALF - 8 * h, 1)
            start = pl.multiple_of((h * groups + g) * joined, joined)
            values[pl.ds(start, joined), :] = jnp.where(lane_j < HALF, shifted, behind)
        return carry

    lax.fori_loop(0, groups, average, 0, unroll=2)

    for buffer in buffers:
        buffer[...] = jnp.zeros_like(buffer)
    sums[...] = jnp.zeros_like(sums)

    place = lax.broadcasted_iota(jnp.int32, (CHUNK, LANES), 0)
    lane = lax.broadcasted_iota(jnp.int32, (CHUNK, grid), 1)
    at_y = lane.astype(F32).astype(BF16)
    at_next = ((lane + (grid - 1)) & (grid - 1)).astype(F32).astype(BF16)
    line_8 = lax.broadcasted_iota(jnp.int32, (8, LANES), 0)
    one = jnp.ones((CHUNK, grid), BF16)
    none = jnp.zeros((CHUNK, grid), BF16)

    lane_1 = lax.broadcasted_iota(jnp.int32, (1, CHUNK), 1)
    points = values.shape[0]

    def fetch(start, buffer):
        for i in range(0, CHUNK, 8):
            block = jnp.broadcast_to(values[pl.ds(point_ref[start + i], 1), :], (8, LANES))
            for j in range(1, 8):
                line = jnp.broadcast_to(values[pl.ds(point_ref[start + i + j], 1), :], (8, LANES))
                block = jnp.where(line_8 == j, line, block)
            buffer[i : i + 8, :] = block

    def put(row, plane):
        x = (row + (grid - 1)) & (grid - 1)
        for side in range(grid // LANES):
            out_ref[side, pl.ds(x, width, stride=grid + PAD), :] = plane[:, side * LANES : (side + 1) * LANES]

    def combined(mean):
        a, b = mean[: width // 2], mean[width // 2 :]
        total, gap = a + b, a - b
        tile = width // 2 - 8
        special = (single_ref[0] == 1) & (line_8 >= 6)
        moved = jnp.where(line_8 == 6, -pltpu.roll(b[tile:], 7, 0), pltpu.roll(b[tile:], 1, 0))
        total = [total[:tile], jnp.where(special, a[tile:], total[tile:])]
        gap = [gap[:tile], jnp.where(special, moved, gap[tile:])]
        return jnp.concatenate([part for part in total + gap if part.shape[0]], axis=0)

    def following(start, row):
        second, third = first_ref[row + 1], first_ref[row + 2]
        end = jnp.minimum(start + CHUNK, third)
        moved = row + jnp.where(end >= second, 1, 0) + jnp.where(end >= third, 1, 0)
        return end, jnp.minimum(moved, grid - 1), end - start, jnp.clip(second - start, 0, end - start)

    def work(row, before, size, size_0, buffer):
        data = buffer[...]
        y = jnp.broadcast_to(data[:, HALF + 4 : HALF + 5], (CHUNK, LANES))
        y = jnp.where(place < size, y, -1.0).astype(BF16)
        y = jnp.concatenate([y] * (grid // LANES), axis=1)
        hot = jnp.concatenate([jnp.where(at_y == y, one, none), jnp.where(at_next == y, one, none)], axis=0)
        turned = data.T
        mean = combined(turned[:width])
        weight = [turned[HALF + j : HALF + j + 1] for j in range(4)]
        here = [jnp.where(lane_1 < size_0, w, 0.0) for w in weight]
        there = [w - h for w, h in zip(weight, here)]
        by_row = (
            (here[0], here[2]),
            (here[1] + there[0], here[3] + there[2]),
            (there[1], there[3]),
        )
        operand = jnp.concatenate(
            [
                jnp.concatenate([mean * jnp.broadcast_to(w, (width, CHUNK)) for w in pair], axis=1)
                for pair in by_row
            ],
            axis=0,
        )
        result = dot(operand.astype(BF16), hot)
        old = [sums[i * width : (i + 1) * width] for i in range(3)]
        put(jnp.minimum(before + 1, grid - 1), old[1])
        put(before, old[0])
        stay, by_one = row == before, row == before + 1
        kept = (
            jnp.where(stay, old[0], jnp.where(by_one, old[1], old[2])),
            jnp.where(stay, old[1], jnp.where(by_one, old[2], 0.0)),
            jnp.where(stay, old[2], 0.0),
        )
        for i in range(3):
            sums[i * width : (i + 1) * width] = result[i * width : (i + 1) * width] + kept[i]

    fetch(0, buffers[0])

    def several(state):
        start, row, before = state
        for i in range(UNROLL):
            end, moved, size, size_0 = following(start, row)
            fetch(end, buffers[(i + 1) % UNROLL])
            work(row, before, size, size_0, buffers[i])
            start, row, before = end, moved, row
        return start, row, before

    zero = jnp.int32(0)
    lax.while_loop(lambda state: (state[0] < points) | (state[2] < grid - 1), several, (zero, zero, zero))
    put(grid - 1, sums[:width])
    for side in range(grid // LANES):
        wrapped = pl.ds(grid - 1, width, stride=grid + PAD)
        cut = slice(side * LANES, (side + 1) * LANES)
        out_ref[side, wrapped, :] = out_ref[side, wrapped, :] + sums[width : 2 * width, cut]


def scatter_call(single, plan, parts, images, weights, cap, width, grid):
    sources, groups, rows16, _ = images.shape
    dirs = parts.shape[1]
    points = dirs * grid
    smem = pl.BlockSpec(memory_space=pltpu.SMEM)
    vmem = pl.BlockSpec(memory_space=VMEM)
    return pl.pallas_call(
        functools.partial(scatter_kernel, cap, width, grid),
        out_shape=jax.ShapeDtypeStruct((grid // LANES, width * (grid + PAD), LANES), F32),
        in_specs=[smem] * 3 + [vmem] * 3,
        out_specs=vmem,
        scratch_shapes=[
            VMEM((points, LANES), F32),
            VMEM((3 * width, grid), F32),
            VMEM((weights.shape[1], sources * rows16), BF16),
        ]
        + [VMEM((CHUNK, LANES), F32)] * UNROLL,
        compiler_params=pltpu.CompilerParams(vmem_limit_bytes=60 * 2**20),
        name="scatter",
    )(single, *plan, parts, images, weights)


def plane_kernel(slabs, grid, data_ref, y_ref, x_ref, out_ref, lines):
    pairs = data_ref.shape[2] // 2
    half = grid // 2
    rows = half + 8
    slab = grid // slabs
    count = 2 * pairs
    lane = lax.broadcasted_iota(jnp.int32, (grid, half), 1)

    def along_y(plane):
        high, low = two_terms(plane)
        both = dot(jnp.concatenate([high, low, high], axis=1), y_ref[...])
        return both[:, :half], both[:, half:]

    def transformed(real, imag):
        cos_r, sin_r = along_y(real)
        cos_i, sin_i = along_y(imag)
        zero_r = jnp.where(lane == 0, 0.0, sin_r)
        zero_i = jnp.where(lane == 0, 0.0, sin_i)
        real = jnp.concatenate([cos_r - zero_i, jnp.where(lane == 0, sin_r, cos_r + sin_i)], axis=1)
        imag = jnp.concatenate([cos_i + zero_r, jnp.where(lane == 0, sin_i, cos_i - sin_r)], axis=1)
        return real, imag

    def along_x(table, operand):
        high, low = operand
        start = table * rows
        return dot(x_ref[start : start + rows], jnp.concatenate([high, low, high], axis=0))

    def one(i, carry):
        planes = [
            [
                jnp.concatenate([data_ref[part, side, 2 * i + r][:grid] for part in range(grid // LANES)], axis=1)
                for r in range(2)
            ]
            for side in range(2)
        ]
        sum_r, sum_i = transformed(*planes[0])
        dif_r, dif_i = transformed(*planes[1])
        cosine = along_x(0, two_terms(jnp.concatenate([sum_r, dif_i], axis=1)))
        sine = along_x(1, two_terms(jnp.concatenate([sum_i, dif_r], axis=1)))
        fields = (
            (cosine[:, :grid] - sine[:, :grid], cosine[:, :grid] + sine[:, :grid]),
            (cosine[:, grid:] + sine[:, grid:], cosine[:, grid:] - sine[:, grid:]),
        )
        for c in range(2):
            plus, minus = fields[c]
            for part in range(grid // LANES):
                cut = slice(part * LANES, (part + 1) * LANES)
                place = 2 * i + c
                lines[part, pl.ds(place, half, stride=count), :] = plus[:half, cut]
                lines[part, pl.ds(half * count + place, half, stride=count), :] = minus[1 : half + 1, cut]
        return carry

    lax.fori_loop(0, pairs, one, 0, unroll=2)
    for d in range(slabs):
        if d < slabs // 2:
            start = slab * d
        else:
            start = half + grid - slab * d - slab
        size = slab * count
        for part in range(grid // LANES):
            block = lines[part, start * count : start * count + size, :]
            out_ref[d, :, :, part * LANES : (part + 1) * LANES] = block.astype(BF16).reshape(slab, count, LANES)


def planes_call(data, table_y, table_x, slabs, grid, part):
    parts, sides, values, pitch, _ = data.shape
    step = min(STEP, values)
    slab = grid // slabs
    fixed = lambda i: (0, 0)
    return pl.pallas_call(
        functools.partial(plane_kernel, slabs, grid),
        grid=(1,),
        in_specs=[
            pl.BlockSpec((parts, sides, step, pitch, LANES), lambda i: (0, 0, part, 0, 0)),
            pl.BlockSpec(table_y.shape, fixed),
            pl.BlockSpec(table_x.shape, fixed),
        ],
        out_specs=pl.BlockSpec((slabs, slab, step, grid), lambda i: (0, 0, 0, 0)),
        scratch_shapes=[VMEM((parts, grid * step, LANES), F32)],
        out_shape=jax.ShapeDtypeStruct((slabs, slab, step, grid), BF16),
        compiler_params=pltpu.CompilerParams(vmem_limit_bytes=56 * 2**20),
        name="planes",
    )(data, table_y, table_x)


def volume_kernel(flip_ref, restore_ref, z_ref, *refs):
    out_ref = refs[-1]
    slabs, span, width, grid = refs[0].shape
    for i in range(span):
        block = jnp.concatenate([ref[:, i].reshape(slabs * width, grid) for ref in refs[:-1]], axis=0)
        turned = dot_t(restore_ref[...], block).astype(BF16)
        value = dot(jnp.concatenate([turned, turned], axis=1), z_ref[...])
        out_ref[jnp.where(flip_ref[0] == 1, span - 1 - i, i)] = value


def volume_call(flip, parts, restore, table_z):
    slabs, slab, width, grid = parts[0].shape
    span = 4
    steps = slab // span
    fixed = lambda i, flip_ref: (0, 0)
    return pl.pallas_call(
        volume_kernel,
        grid_spec=pltpu.PrefetchScalarGridSpec(
            num_scalar_prefetch=1,
            grid=(steps,),
            in_specs=[pl.BlockSpec(restore.shape, fixed), pl.BlockSpec(table_z.shape, fixed)]
            + [pl.BlockSpec((slabs, span, width, grid), lambda i, flip_ref: (0, i, 0, 0))] * len(parts),
            out_specs=pl.BlockSpec(
                (span, grid, grid), lambda i, flip_ref: (jnp.where(flip_ref[0] == 1, steps - 1 - i, i), 0, 0)
            ),
        ),
        out_shape=jax.ShapeDtypeStruct((slab, grid, grid), F32),
        compiler_params=pltpu.CompilerParams(vmem_limit_bytes=48 * 2**20),
        name="volume",
    )(flip, restore, table_z, *parts)


def sorted_points(interp_cells, grid):
    dirs = interp_cells.shape[0]
    points = dirs * grid
    base = interp_cells[:, 0, :].T.reshape(-1)
    row = (base // grid + 1) & (grid - 1)
    key = row * points + jnp.arange(points, dtype=jnp.int32)
    key = lax.sort(key, is_stable=False)
    rows = jnp.arange(grid + 3, dtype=jnp.int32)
    first = jnp.sum((row[None, :] < rows[:, None]).astype(jnp.int32), axis=1)
    point = jnp.concatenate([key & (points - 1), jnp.zeros((CHUNK,), jnp.int32)])
    return first, point


def arrange_kernel(rows_ref, other_ref, eye_ref, order_ref, extra_ref, kept_ref, sent_ref, *lines):
    dirs, count, _, grid = rows_ref.shape
    blocks = LANES // count
    length = grid // blocks
    span = extra_ref.shape[0]
    each = span * blocks
    number = lax.broadcasted_iota(jnp.int32, (length, LANES), 1) // count

    def step(m, carry):
        other = other_ref[pl.ds(pl.multiple_of(2 * each * m, 2 * each), 2 * each), :]
        other = dot_t(eye_ref[...], other).astype(BF16)
        for group in range(span):
            k = each * m + blocks * group
            block = rows_ref[pl.ds(k, blocks)].reshape(2 * LANES, grid)
            turned = dot_t(eye_ref[...], block).astype(BF16)
            turned = dot(turned, order_ref[...]) + dot(other, extra_ref[group])
            for side in range(2):
                tile = [turned[q * length : (q + 1) * length, side * LANES : (side + 1) * LANES] for q in range(blocks)]
                bit = 1
                while bit < blocks:
                    low = (number & bit) == 0
                    swapped = list(tile)
                    for q in range(blocks):
                        if q & bit == 0:
                            swapped[q] = jnp.where(low, tile[q], pltpu.roll(tile[q + bit], bit * count, 1))
                            swapped[q + bit] = jnp.where(low, pltpu.roll(tile[q], LANES - bit * count, 1), tile[q + bit])
                    tile = swapped
                    bit *= 2
                for i in range(blocks):
                    lines[side][pl.ds(k + i, length, stride=dirs + PAD), :] = tile[i]
        return carry

    lax.fori_loop(0, dirs // each, step, 0)
    for side, out_ref in enumerate((kept_ref, sent_ref)):
        steps = out_ref.shape[1] // dirs
        for u in range(length):
            block = lines[side][u * (dirs + PAD) : u * (dirs + PAD) + dirs, :].astype(BF16)
            out_ref[u // steps, u % steps * dirs : (u % steps + 1) * dirs, :] = block


def arrange_call(rows, other, eye, order, extra, steps):
    dirs, count, _, grid = rows.shape
    length = grid // (LANES // count)
    vmem = pl.BlockSpec(memory_space=VMEM)
    shape = jax.ShapeDtypeStruct((length // steps, steps * dirs, LANES), BF16)
    return pl.pallas_call(
        arrange_kernel,
        out_shape=(shape, shape),
        in_specs=[vmem] * 5,
        out_specs=(vmem, vmem),
        scratch_shapes=[VMEM((length * (dirs + PAD), LANES), F32)] * 2,
        compiler_params=pltpu.CompilerParams(vmem_limit_bytes=48 * 2**20),
        name="arrange",
    )(rows, other, eye, order, extra)


def row_orders(slab):
    half = slab // 2
    blocks = LANES // slab
    span = max(1, 8 // blocks)
    down = list(range(half - 1, -1, -1))
    upper = list(range(slab - 1, half - 1, -1))
    orders, extras = [], []
    for kept, sent in (
        (list(range(1, half + 1)), list(range(half + 1, slab)) + [None]),
        (down[:-1] + [None], upper),
        (down, upper),
    ):
        order = np.zeros((2 * LANES, 2 * LANES))
        extra = np.zeros((span, 2 * span * blocks, 2 * LANES))
        for side, rows in enumerate((kept, sent)):
            for k in range(blocks):
                for i, row in enumerate(rows):
                    for r in range(2):
                        lane = side * LANES + k * slab + 2 * i + r
                        if row is not None:
                            order[(k * slab + row) * 2 + r, lane] = 1.0
                        else:
                            for group in range(span):
                                extra[group, (group * blocks + k) * 2 + r, lane] = 1.0
        orders.append(order.astype(jnp.bfloat16))
        extras.append(extra.astype(jnp.bfloat16))
    return np.stack(orders), np.stack(extras)


def paired_rows(rows, eye, slabs, steps):
    own = lax.axis_index("vol")
    dirs, slab, _, grid = rows.shape
    first = [(0, slabs // 2)] + [(i, i - 1) for i in range(1, slabs // 2 + 1)]
    other = lax.ppermute(rows[:, 0], "vol", first).reshape(2 * dirs, grid)
    kind = jnp.where(own < slabs // 2, 0, jnp.where(own == slabs // 2, 1, 2))
    order, extra = (lax.dynamic_index_in_dim(jnp.asarray(t), kind, 0, keepdims=False) for t in row_orders(slab))
    kept, sent = arrange_call(rows, other, eye, order, extra, steps)
    arrived = lax.ppermute(sent, "vol", [(i, slabs - 1 - i) for i in range(slabs)])
    return kept, arrived


def shards(images, projections, assignment, interp_cells, interp_weights):
    class_count = lax.axis_size("cls")
    slab_count = lax.axis_size("vol")
    local_count, grid = images.shape[0], images.shape[1]
    dirs = projections.shape[1]
    slab = grid // slab_count
    width = 2 * slab
    halves = LANES // width
    capacity = 2 * local_count // class_count
    steps = 16 // capacity
    groups = grid // (halves * steps)

    eye = jnp.asarray(np.eye(grid), BF16)
    order = jnp.asarray(lane_order(grid, slab_count))
    outgoing = route_call(images, assignment, eye, order, class_count, slab_count, width, capacity)
    outgoing, projections = lax.optimization_barrier((outgoing, projections))
    arrived = lax.all_to_all(outgoing, ("cls", "vol"), split_axis=0, concat_axis=0, tiled=True)

    kept, joined = paired_rows(projections[0], eye, slab_count, steps)
    corner_y = (interp_cells[:, 0:1, :] & (grid - 1)).astype(F32)
    weights = jnp.concatenate([interp_weights, corner_y, jnp.zeros((dirs, 3, grid), F32)], axis=1)
    weights = weights.reshape(dirs, 8, halves, groups, steps)
    weights = jnp.transpose(weights, (3, 4, 0, 2, 1)).reshape(groups, steps * dirs, 8 * halves)
    weights = jnp.pad(weights, ((0, 0), (0, 0), (0, LANES - 8 * halves)))
    plan = sorted_points(interp_cells, grid)
    table_y, table_x, table_z, restore = tables(grid, slab_count)

    arrived, kept, joined, weights, plan = lax.optimization_barrier((arrived, kept, joined, weights, plan))
    partial_value = scores_call(arrived, kept, joined, capacity, dirs, slab)
    copies = jnp.broadcast_to(partial_value[None], (slab_count,) + partial_value.shape)
    parts = lax.all_to_all(copies, "vol", split_axis=0, concat_axis=0, tiled=True)
    own = lax.axis_index("vol")
    single = (own == slab_count // 2).astype(jnp.int32).reshape(1)
    flip = (own >= slab_count // 2).astype(jnp.int32).reshape(1)
    plane = scatter_call(single, plan, parts, arrived, weights, capacity, width, grid)
    plane = plane.reshape(grid // LANES, 2, slab, grid + PAD, LANES)
    received = []
    for part in range(max(1, slab // STEP)):
        sent = planes_call(plane, table_y, table_x, slab_count, grid, part)
        received.append(lax.all_to_all(sent, "vol", split_axis=0, concat_axis=0, tiled=True))
    return volume_call(flip, received, restore, table_z)[None]


def solution(mesh):
    in_specs = (
        P(("cls", "vol"), None, None, None),
        P("cls", None, "vol", None, None),
        P(("cls", "vol"), None),
        P(),
        P(),
    )
    out_specs = P("cls", "vol", None, None)
    return jax.shard_map(shards, mesh=mesh, in_specs=in_specs, out_specs=out_specs, check_vma=False)
```

```python
import functools
import math

import jax
import jax.numpy as jnp
import numpy as np
from jax import lax
from jax.experimental import pallas as pl
from jax.experimental.pallas import tpu as pltpu
from jax.sharding import PartitionSpec as P

F32 = jnp.float32
BF16 = jnp.bfloat16
LANES = 128
HALF = 64
CHUNK = 128
PAD = 8
UNROLL = 8
STEP = 16
VMEM = pltpu.VMEM


def split_table(table):
    high = table.astype(jnp.bfloat16)
    low = (table - high.astype(np.float64)).astype(jnp.bfloat16)
    return high, low


def plane_pairs(grid, slabs):
    slab = grid // slabs
    half = slab // 2
    pairs = []
    for w in range(slabs):
        for i in range(half):
            if w < slabs // 2:
                first = slab * w + 1 + i
            else:
                first = slab * w + half - 1 - i
            if 2 * first == grid:
                pairs.append((0, first))
            else:
                pairs.append((first, grid - first))
    return np.array(pairs).reshape(slabs, half, 2)


def tables(grid, slabs):
    half = grid // 2
    scale = 1.0 / math.sqrt(grid)
    index = np.arange(grid)
    angle = 2.0 * np.pi / grid
    phase = (index[:, None] * np.arange(half)[None, :]) % grid
    cosine = np.cos(phase * angle)
    sine = np.sin(phase * angle)
    sine[:, 0] = np.cos(((index * half) % grid) * angle)
    table_y = np.concatenate([cosine, sine], axis=1) * scale
    rows = half + 8
    phase = (np.arange(rows)[:, None] * index[None, :]) % grid
    live = (np.arange(rows) <= half)[:, None]
    table_x = np.concatenate([np.cos(phase * angle) * live, np.sin(phase * angle) * live], axis=0) * scale
    pairs = plane_pairs(grid, slabs).reshape(-1, 2)
    single = (2 * pairs[:, 1] == grid)[:, None]
    z = np.where(single[:, 0], pairs[:, 1], pairs[:, 0])
    phase = (z[:, None] * index[None, :]) % grid
    for_sum = np.where(single, 1.0, np.cos(phase * angle))
    for_difference = np.where(single, np.cos(phase * angle), -np.sin(phase * angle))
    table_z = np.stack([for_sum, for_difference], axis=1).reshape(grid, grid) * scale
    order = np.concatenate([np.arange(half), [half], np.arange(grid - 1, half, -1)])
    restore = (order[None, :] == index[:, None]).astype(jnp.bfloat16)
    parts = max(1, grid // slabs // STEP)
    table_z = table_z.reshape(slabs, parts, -1, grid).transpose(1, 0, 2, 3).reshape(grid, grid)
    high, low = split_table(table_y)
    table_y = np.concatenate([high, high, low], axis=0)
    high, low = split_table(table_x)
    table_x = np.concatenate([high, high, low], axis=1)
    table_z = np.concatenate(split_table(table_z), axis=0)
    return table_y, table_x, table_z, restore


def lane_order(grid, slabs):
    rows = plane_pairs(grid, slabs).transpose(0, 2, 1).reshape(-1)
    source = (2 * rows[:, None] + np.arange(2)[None, :]).reshape(-1)
    return (np.arange(2 * grid)[:, None] == source[None, :]).astype(jnp.bfloat16)


def dot(a, b):
    return jnp.dot(a, b, preferred_element_type=F32)


def dot_t(a, b):
    return lax.dot_general(a, b, (((1,), (1,)), ((), ())), preferred_element_type=F32)


def two_terms(value):
    high = value.astype(BF16)
    low = (value - high.astype(F32)).astype(BF16)
    return high, low


def route_kernel(cap, slabs, width, classes_ref, images_ref, eye_ref, order_ref, out_ref, lines):
    count, _, _, grid = images_ref.shape
    halves = LANES // width
    piece = grid // halves
    lane = lax.broadcasted_iota(jnp.int32, (piece, LANES), 1)
    lines[...] = jnp.zeros_like(lines)

    def place(p, carry):
        own = classes_ref[p, 0]
        rank = 0
        for q in range(count):
            rank = rank + jnp.where((classes_ref[q, 0] == own) & (q < p), 1, 0)
        image = images_ref[p].reshape(-1, grid)
        turned = dot(dot_t(eye_ref[...], image).astype(BF16), order_ref[...])
        for w in range(slabs):
            tile = w * width // LANES * LANES
            block = jnp.zeros((piece, LANES), F32)
            for h in range(halves):
                part = turned[h * piece : (h + 1) * piece, tile : tile + LANES]
                shift = (h * width - (w * width - tile)) % LANES
                part = part if shift == 0 else pltpu.roll(part, shift, 1)
                block = jnp.where((lane >= h * width) & (lane < (h + 1) * width), part, block)
            lines[own * slabs + w, pl.ds(rank, piece, stride=cap), :] = block
        return carry

    lax.fori_loop(0, count, place, 0, unroll=2)
    out_ref[...] = lines[...].astype(BF16).reshape(out_ref.shape)


def route_call(images, assignment, eye, order, class_count, slabs, width, cap):
    count, grid = images.shape[0], images.shape[1]
    rows = grid // (LANES // width) * cap
    vmem = pl.BlockSpec(memory_space=VMEM)
    return pl.pallas_call(
        functools.partial(route_kernel, cap, slabs, width),
        out_shape=jax.ShapeDtypeStruct((class_count * slabs, rows // 16, 16, LANES), BF16),
        in_specs=[pl.BlockSpec(memory_space=pltpu.SMEM)] + [vmem] * 3,
        out_specs=vmem,
        scratch_shapes=[VMEM((class_count * slabs, rows, LANES), F32)],
        compiler_params=pltpu.CompilerParams(vmem_limit_bytes=48 * 2**20),
        name="route",
    )(assignment, images, eye, order)


def score_kernel(cap, dirs, unit, images_ref, kept_ref, joined_ref, out_ref, sums):
    sources, groups, rows16, _ = images_ref.shape
    rows = sources * rows16
    steps = rows16 // cap
    sums[...] = jnp.zeros_like(sums)
    lane = lax.broadcasted_iota(jnp.int32, (steps * dirs, LANES), 1)
    even = (lane & unit) == 0

    def step(g, carry):
        kept = kept_ref[g].astype(F32)
        joined = joined_ref[g].astype(F32)
        refs = [
            jnp.where(even, kept, pltpu.roll(joined, unit, 1)).astype(BF16),
            jnp.where(even, pltpu.roll(kept, LANES - unit, 1), joined).astype(BF16),
        ]
        blocks = [images_ref[:, pl.ds(g + i * (groups // 2), 1), :, :].reshape(rows, LANES) for i in range(2)]
        sums[...] += dot_t(jnp.concatenate(refs, axis=1), jnp.concatenate(blocks, axis=1))
        return carry

    lax.fori_loop(0, groups // 2, step, 0, unroll=2)
    column = lax.broadcasted_iota(jnp.int32, (dirs, rows), 1)
    part = (column & (rows16 - 1)) // cap
    kept = jnp.zeros((dirs, rows), F32)
    for j in range(steps):
        kept = kept + jnp.where(part == j, sums[j * dirs : (j + 1) * dirs, :], 0.0)
    slots = sources * cap
    row_id = lax.broadcasted_iota(jnp.int32, (rows, slots), 0)
    slot_id = lax.broadcasted_iota(jnp.int32, (rows, slots), 1)
    gather = (row_id // rows16 * cap + row_id % cap) == slot_id
    out_ref[...] = jnp.dot(
        kept, gather.astype(F32), preferred_element_type=F32, precision=lax.Precision.HIGHEST
    )


def scores_call(images, kept, joined, cap, dirs, unit):
    sources, groups, rows16, _ = images.shape
    return pl.pallas_call(
        functools.partial(score_kernel, cap, dirs, unit),
        out_shape=jax.ShapeDtypeStruct((dirs, sources * cap), F32),
        in_specs=[pl.BlockSpec(memory_space=VMEM)] * 3,
        out_specs=pl.BlockSpec(memory_space=VMEM),
        scratch_shapes=[VMEM((kept.shape[1], sources * rows16), F32)],
        compiler_params=pltpu.CompilerParams(vmem_limit_bytes=48 * 2**20),
        name="scores",
    )(images, kept, joined)


def scatter_kernel(
    cap,
    width,
    grid,
    slabs,
    single_ref,
    first_ref,
    point_ref,
    parts_ref,
    images_hbm,
    weights_hbm,
    y_ref,
    x_ref,
    sent_ref,
    *refs,
):
    rest = width > STEP * 2
    rest_hbm = refs[0] if rest else None
    plane, values, sums, spread, lines, images_ref, weights_ref, image_sem, weight_sem, rest_sem, *buffers = refs[rest:]
    sources, groups, rows16, _ = images_ref.shape
    pieces = weight_sem.shape[0]
    images_copy = pltpu.make_async_copy(images_hbm, images_ref, image_sem)
    images_copy.start()
    weight_copies = []
    for i in range(pieces):
        part = pl.ds(i * (groups // pieces), groups // pieces)
        weight_copies.append(pltpu.make_async_copy(weights_hbm.at[part], weights_ref.at[part], weight_sem.at[i]))
        weight_copies[i].start()
    rows = sources * rows16
    steps = rows16 // cap
    dirs, slots = parts_ref.shape[1:]
    joined = steps * dirs
    halves = LANES // width

    total = parts_ref[0]
    for i in range(1, parts_ref.shape[0]):
        total = total + parts_ref[i]
    expo = jnp.exp(total - jnp.max(total, axis=0, keepdims=True))
    posterior = (expo / jnp.sum(expo, axis=0, keepdims=True)).astype(BF16)
    slot_id = lax.broadcasted_iota(jnp.int32, (slots, rows), 0)
    row_id = lax.broadcasted_iota(jnp.int32, (slots, rows), 1)
    repeat = ((row_id // rows16 * cap + row_id % cap) == slot_id).astype(F32).astype(BF16)
    wide = dot(posterior, repeat)
    part = (lax.broadcasted_iota(jnp.int32, (dirs, rows), 1) & (rows16 - 1)) // cap
    for j in range(steps):
        spread[j * dirs : (j + 1) * dirs, :] = jnp.where(part == j, wide, 0.0).astype(BF16)

    lane_j = lax.broadcasted_iota(jnp.int32, (joined, LANES), 1)

    def average(m, carry):
        blocks = [images_ref[:, pl.ds(2 * m + i, 1), :, :].reshape(rows, LANES) for i in range(2)]
        means = dot(spread[...], jnp.concatenate(blocks, axis=1))
        for i in range(2):
            g = 2 * m + i
            mean = means[:, i * LANES : (i + 1) * LANES]
            weight = weights_ref[g]
            for h in range(halves):
                shifted = mean if h == 0 else pltpu.roll(mean, LANES - h * width, 1)
                behind = pltpu.roll(weight, HALF - 8 * h, 1)
                start = pl.multiple_of((h * groups + g) * joined, joined)
                values[pl.ds(start, joined), :] = jnp.where(lane_j < HALF, shifted, behind)
        return carry

    images_copy.wait()
    for i in range(pieces):
        weight_copies[i].wait()
        begin = groups // pieces // 2
        lax.fori_loop(i * begin, (i + 1) * begin, average, 0)

    for buffer in buffers:
        buffer[...] = jnp.zeros_like(buffer)
    sums[...] = jnp.zeros_like(sums)

    place = lax.broadcasted_iota(jnp.int32, (CHUNK, LANES), 0)
    lane = lax.broadcasted_iota(jnp.int32, (CHUNK, grid), 1)
    at_y = lane.astype(F32).astype(BF16)
    at_next = ((lane + (grid - 1)) & (grid - 1)).astype(F32).astype(BF16)
    line_8 = lax.broadcasted_iota(jnp.int32, (8, LANES), 0)
    one = jnp.ones((CHUNK, grid), BF16)
    none = jnp.zeros((CHUNK, grid), BF16)

    lane_1 = lax.broadcasted_iota(jnp.int32, (1, CHUNK), 1)
    points = values.shape[0]

    def fetch(start, buffer):
        for i in range(0, CHUNK, 8):
            block = jnp.broadcast_to(values[pl.ds(point_ref[start + i], 1), :], (8, LANES))
            for j in range(1, 8):
                line = jnp.broadcast_to(values[pl.ds(point_ref[start + i + j], 1), :], (8, LANES))
                block = jnp.where(line_8 == j, line, block)
            buffer[i : i + 8, :] = block

    def put(row, value):
        x = (row + (grid - 1)) & (grid - 1)
        for side in range(grid // LANES):
            plane[side, pl.ds(x, width, stride=grid + PAD), :] = value[:, side * LANES : (side + 1) * LANES]

    def combined(mean):
        a, b = mean[: width // 2], mean[width // 2 :]
        total, gap = a + b, a - b
        tile = width // 2 - 8
        special = (single_ref[0] == 1) & (line_8 >= 6)
        moved = jnp.where(line_8 == 6, -pltpu.roll(b[tile:], 7, 0), pltpu.roll(b[tile:], 1, 0))
        total = [total[:tile], jnp.where(special, a[tile:], total[tile:])]
        gap = [gap[:tile], jnp.where(special, moved, gap[tile:])]
        return jnp.concatenate([part for part in total + gap if part.shape[0]], axis=0)

    def following(start, row):
        second, third = first_ref[row + 1], first_ref[row + 2]
        end = jnp.minimum(start + CHUNK, third)
        moved = row + jnp.where(end >= second, 1, 0) + jnp.where(end >= third, 1, 0)
        return end, jnp.minimum(moved, grid - 1), end - start, jnp.clip(second - start, 0, end - start)

    def work(row, before, size, size_0, buffer):
        data = buffer[...]
        y = jnp.broadcast_to(data[:, HALF + 4 : HALF + 5], (CHUNK, LANES))
        y = jnp.where(place < size, y, -1.0).astype(BF16)
        y = jnp.concatenate([y] * (grid // LANES), axis=1)
        hot = jnp.concatenate([jnp.where(at_y == y, one, none), jnp.where(at_next == y, one, none)], axis=0)
        turned = data.T
        mean = combined(turned[:width])
        weight = [turned[HALF + j : HALF + j + 1] for j in range(4)]
        here = [jnp.where(lane_1 < size_0, w, 0.0) for w in weight]
        there = [w - h for w, h in zip(weight, here)]
        by_row = (
            (here[0], here[2]),
            (here[1] + there[0], here[3] + there[2]),
            (there[1], there[3]),
        )
        operand = jnp.concatenate(
            [
                jnp.concatenate([mean * jnp.broadcast_to(w, (width, CHUNK)) for w in pair], axis=1)
                for pair in by_row
            ],
            axis=0,
        )
        result = dot(operand.astype(BF16), hot)
        old = [sums[i * width : (i + 1) * width] for i in range(3)]
        put(jnp.minimum(before + 1, grid - 1), old[1])
        put(before, old[0])
        stay, by_one = row == before, row == before + 1
        kept = (
            jnp.where(stay, old[0], jnp.where(by_one, old[1], old[2])),
            jnp.where(stay, old[1], jnp.where(by_one, old[2], 0.0)),
            jnp.where(stay, old[2], 0.0),
        )
        for i in range(3):
            sums[i * width : (i + 1) * width] = result[i * width : (i + 1) * width] + kept[i]

    fetch(0, buffers[0])

    def several(state):
        start, row, before = state
        for i in range(UNROLL):
            end, moved, size, size_0 = following(start, row)
            fetch(end, buffers[(i + 1) % UNROLL])
            work(row, before, size, size_0, buffers[i])
            start, row, before = end, moved, row
        return start, row, before

    zero = jnp.int32(0)
    lax.while_loop(lambda state: (state[0] < points) | (state[2] < grid - 1), several, (zero, zero, zero))
    put(grid - 1, sums[:width])
    for side in range(grid // LANES):
        wrapped = pl.ds(grid - 1, width, stride=grid + PAD)
        cut = slice(side * LANES, (side + 1) * LANES)
        plane[side, wrapped, :] = plane[side, wrapped, :] + sums[width : 2 * width, cut]

    pitch = grid + PAD
    step = min(STEP, width // 2)
    copies = []
    if rest:
        size = (width // 2 - step) * pitch
        for part in range(grid // LANES):
            for side in range(2):
                source = plane.at[part, pl.ds((side * (width // 2) + step) * pitch, size)]
                copies.append(pltpu.make_async_copy(source, rest_hbm.at[part, side], rest_sem.at[2 * part + side]))
                copies[-1].start()

    def load(part, side, value):
        place = pl.multiple_of((side * (width // 2) + value) * pitch, 8)
        return plane[part, pl.ds(place, grid), :]

    transform_pairs(slabs, grid, step // 2, load, y_ref, x_ref, sent_ref, lines)
    for copy in copies:
        copy.wait()


def scatter_call(single, plan, parts, images, weights, table_y, table_x, cap, width, grid, slabs):
    sources, groups, rows16, _ = images.shape
    dirs = parts.shape[1]
    points = dirs * grid
    smem = pl.BlockSpec(memory_space=pltpu.SMEM)
    vmem = pl.BlockSpec(memory_space=VMEM)
    hbm = pl.BlockSpec(memory_space=pl.ANY)
    step = min(STEP, width // 2)
    other = width // 2 - step
    pitch = grid + PAD
    sides = grid // LANES
    pieces = 4
    shapes = [jax.ShapeDtypeStruct((slabs, grid // slabs, step, grid), BF16)]
    if other:
        shapes.append(jax.ShapeDtypeStruct((sides, 2, other * pitch, LANES), F32))
    result = pl.pallas_call(
        functools.partial(scatter_kernel, cap, width, grid, slabs),
        out_shape=shapes,
        in_specs=[smem] * 3 + [vmem, hbm, hbm, vmem, vmem],
        out_specs=[vmem, hbm][: len(shapes)],
        scratch_shapes=[
            VMEM((sides, width * pitch, LANES), F32),
            VMEM((points, LANES), F32),
            VMEM((3 * width, grid), F32),
            VMEM((weights.shape[1], sources * rows16), BF16),
            VMEM((sides, grid * step, LANES), F32),
            VMEM(images.shape, BF16),
            VMEM(weights.shape, F32),
            pltpu.SemaphoreType.DMA,
            pltpu.SemaphoreType.DMA((pieces,)),
            pltpu.SemaphoreType.DMA((2 * sides,)),
        ]
        + [VMEM((CHUNK, LANES), F32)] * UNROLL,
        compiler_params=pltpu.CompilerParams(vmem_limit_bytes=61 * 2**20),
        name="scatter",
    )(single, *plan, parts, images, weights, table_y, table_x)
    if not other:
        return result[0], None
    return result[0], result[1].reshape(sides, 2, other, pitch, LANES)


def transform_pairs(slabs, grid, pairs, load, y_ref, x_ref, out_ref, lines):
    half = grid // 2
    rows = half + 8
    slab = grid // slabs
    count = 2 * pairs
    lane = lax.broadcasted_iota(jnp.int32, (grid, half), 1)

    def transformed(real, imag):
        cos_r, sin_r = real[:, :half], real[:, half:]
        cos_i, sin_i = imag[:, :half], imag[:, half:]
        zero_r = jnp.where(lane == 0, 0.0, sin_r)
        zero_i = jnp.where(lane == 0, 0.0, sin_i)
        real = jnp.concatenate([cos_r - zero_i, jnp.where(lane == 0, sin_r, cos_r + sin_i)], axis=1)
        imag = jnp.concatenate([cos_i + zero_r, jnp.where(lane == 0, sin_i, cos_i - sin_r)], axis=1)
        return real, imag

    def along_x(table, operand):
        high, low = two_terms(operand)
        return dot(x_ref[table * rows : (table + 1) * rows], jnp.concatenate([high, low, high], axis=0))

    def one(i, carry):
        planes = [
            jnp.concatenate([load(part, side, 2 * i + r) for part in range(grid // LANES)], axis=1)
            for side in range(2)
            for r in range(2)
        ]
        high, low = two_terms(jnp.concatenate(planes, axis=0))
        both = dot(jnp.concatenate([high, low, high], axis=1), y_ref[...])
        both = [both[j * grid : (j + 1) * grid] for j in range(4)]
        sum_r, sum_i = transformed(both[0], both[1])
        dif_r, dif_i = transformed(both[2], both[3])
        cosine = along_x(0, jnp.concatenate([sum_r, dif_i], axis=1))
        sine = along_x(1, jnp.concatenate([sum_i, dif_r], axis=1))
        fields = (
            (cosine[:, :grid] - sine[:, :grid], cosine[:, :grid] + sine[:, :grid]),
            (cosine[:, grid:] + sine[:, grid:], cosine[:, grid:] - sine[:, grid:]),
        )
        for c in range(2):
            plus, minus = fields[c]
            for part in range(grid // LANES):
                cut = slice(part * LANES, (part + 1) * LANES)
                place = 2 * i + c
                lines[part, pl.ds(place, half, stride=count), :] = plus[:half, cut]
                lines[part, pl.ds(half * count + place, half, stride=count), :] = minus[1 : half + 1, cut]
        return carry

    lax.fori_loop(0, pairs, one, 0, unroll=2)
    for d in range(slabs):
        if d < slabs // 2:
            start = slab * d
        else:
            start = half + grid - slab * d - slab
        size = slab * count
        for part in range(grid // LANES):
            block = lines[part, start * count : start * count + size, :]
            out_ref[d, :, :, part * LANES : (part + 1) * LANES] = block.astype(BF16).reshape(slab, count, LANES)


def plane_kernel(slabs, grid, data_ref, y_ref, x_ref, out_ref, lines):
    pairs = data_ref.shape[2] // 2

    def load(part, side, value):
        return data_ref[part, side, value][:grid]

    transform_pairs(slabs, grid, pairs, load, y_ref, x_ref, out_ref, lines)


def planes_call(data, table_y, table_x, slabs, grid):
    step = data.shape[2]
    slab = grid // slabs
    vmem = pl.BlockSpec(memory_space=VMEM)
    return pl.pallas_call(
        functools.partial(plane_kernel, slabs, grid),
        in_specs=[vmem] * 3,
        out_specs=vmem,
        scratch_shapes=[VMEM((data.shape[0], grid * step, LANES), F32)],
        out_shape=jax.ShapeDtypeStruct((slabs, slab, step, grid), BF16),
        compiler_params=pltpu.CompilerParams(vmem_limit_bytes=56 * 2**20),
        name="planes",
    )(data, table_y, table_x)


def volume_kernel(flip_ref, restore_ref, z_ref, *refs):
    out_ref = refs[-1]
    slabs, span, width, grid = refs[0].shape
    turned = []
    for i in range(span):
        block = jnp.concatenate([ref[:, i].reshape(slabs * width, grid) for ref in refs[:-1]], axis=0)
        turned.append(dot_t(restore_ref[...], block).astype(BF16))
    turned = jnp.concatenate(turned, axis=0)
    value = dot(jnp.concatenate([turned, turned], axis=1), z_ref[...])
    for i in range(span):
        out_ref[jnp.where(flip_ref[0] == 1, span - 1 - i, i)] = value[i * grid : (i + 1) * grid]


def volume_call(flip, parts, restore, table_z):
    slabs, slab, width, grid = parts[0].shape
    span = 4
    steps = slab // span
    fixed = lambda i, flip_ref: (0, 0)
    return pl.pallas_call(
        volume_kernel,
        grid_spec=pltpu.PrefetchScalarGridSpec(
            num_scalar_prefetch=1,
            grid=(steps,),
            in_specs=[pl.BlockSpec(restore.shape, fixed), pl.BlockSpec(table_z.shape, fixed)]
            + [pl.BlockSpec((slabs, span, width, grid), lambda i, flip_ref: (0, i, 0, 0))] * len(parts),
            out_specs=pl.BlockSpec(
                (span, grid, grid), lambda i, flip_ref: (jnp.where(flip_ref[0] == 1, steps - 1 - i, i), 0, 0)
            ),
        ),
        out_shape=jax.ShapeDtypeStruct((slab, grid, grid), F32),
        compiler_params=pltpu.CompilerParams(vmem_limit_bytes=48 * 2**20),
        name="volume",
    )(flip, restore, table_z, *parts)


def sorted_points(interp_cells, grid):
    dirs = interp_cells.shape[0]
    points = dirs * grid
    base = interp_cells[:, 0, :].T.reshape(-1)
    row = (base // grid + 1) & (grid - 1)
    key = row * points + jnp.arange(points, dtype=jnp.int32)
    key = lax.sort(key, is_stable=False)
    rows = jnp.arange(grid + 3, dtype=jnp.int32)
    first = jnp.sum((row[None, :] < rows[:, None]).astype(jnp.int32), axis=1)
    point = jnp.concatenate([key & (points - 1), jnp.zeros((CHUNK,), jnp.int32)])
    return first, point


def arrange_kernel(rows_ref, other_ref, eye_ref, order_ref, extra_ref, kept_ref, sent_ref, *lines):
    dirs, count, _, grid = rows_ref.shape
    blocks = LANES // count
    length = grid // blocks
    span = extra_ref.shape[0]
    each = span * blocks
    number = lax.broadcasted_iota(jnp.int32, (length, LANES), 1) // count

    def step(m, carry):
        other = other_ref[pl.ds(pl.multiple_of(2 * each * m, 2 * each), 2 * each), :]
        other = dot_t(eye_ref[...], other).astype(BF16)
        for group in range(span):
            k = each * m + blocks * group
            block = rows_ref[pl.ds(k, blocks)].reshape(2 * LANES, grid)
            turned = dot_t(eye_ref[...], block).astype(BF16)
            turned = dot(turned, order_ref[...]) + dot(other, extra_ref[group])
            for side in range(2):
                tile = [turned[q * length : (q + 1) * length, side * LANES : (side + 1) * LANES] for q in range(blocks)]
                bit = 1
                while bit < blocks:
                    low = (number & bit) == 0
                    swapped = list(tile)
                    for q in range(blocks):
                        if q & bit == 0:
                            swapped[q] = jnp.where(low, tile[q], pltpu.roll(tile[q + bit], bit * count, 1))
                            swapped[q + bit] = jnp.where(low, pltpu.roll(tile[q], LANES - bit * count, 1), tile[q + bit])
                    tile = swapped
                    bit *= 2
                for i in range(blocks):
                    lines[side][pl.ds(k + i, length, stride=dirs + PAD), :] = tile[i]
        return carry

    lax.fori_loop(0, dirs // each, step, 0)
    for side, out_ref in enumerate((kept_ref, sent_ref)):
        steps = out_ref.shape[1] // dirs
        for u in range(length):
            block = lines[side][u * (dirs + PAD) : u * (dirs + PAD) + dirs, :].astype(BF16)
            out_ref[u // steps, u % steps * dirs : (u % steps + 1) * dirs, :] = block


def arrange_call(rows, other, eye, order, extra, steps):
    dirs, count, _, grid = rows.shape
    length = grid // (LANES // count)
    vmem = pl.BlockSpec(memory_space=VMEM)
    shape = jax.ShapeDtypeStruct((length // steps, steps * dirs, LANES), BF16)
    return pl.pallas_call(
        arrange_kernel,
        out_shape=(shape, shape),
        in_specs=[vmem] * 5,
        out_specs=(vmem, vmem),
        scratch_shapes=[VMEM((length * (dirs + PAD), LANES), F32)] * 2,
        compiler_params=pltpu.CompilerParams(vmem_limit_bytes=48 * 2**20),
        name="arrange",
    )(rows, other, eye, order, extra)


def row_orders(slab):
    half = slab // 2
    blocks = LANES // slab
    span = max(1, 8 // blocks)
    down = list(range(half - 1, -1, -1))
    upper = list(range(slab - 1, half - 1, -1))
    orders, extras = [], []
    for kept, sent in (
        (list(range(1, half + 1)), list(range(half + 1, slab)) + [None]),
        (down[:-1] + [None], upper),
        (down, upper),
    ):
        order = np.zeros((2 * LANES, 2 * LANES))
        extra = np.zeros((span, 2 * span * blocks, 2 * LANES))
        for side, rows in enumerate((kept, sent)):
            for k in range(blocks):
                for i, row in enumerate(rows):
                    for r in range(2):
                        lane = side * LANES + k * slab + 2 * i + r
                        if row is not None:
                            order[(k * slab + row) * 2 + r, lane] = 1.0
                        else:
                            for group in range(span):
                                extra[group, (group * blocks + k) * 2 + r, lane] = 1.0
        orders.append(order.astype(jnp.bfloat16))
        extras.append(extra.astype(jnp.bfloat16))
    return np.stack(orders), np.stack(extras)


def paired_rows(rows, eye, slabs, steps):
    own = lax.axis_index("vol")
    dirs, slab, _, grid = rows.shape
    first = [(0, slabs // 2)] + [(i, i - 1) for i in range(1, slabs // 2 + 1)]
    other = lax.ppermute(rows[:, 0], "vol", first).reshape(2 * dirs, grid)
    kind = jnp.where(own < slabs // 2, 0, jnp.where(own == slabs // 2, 1, 2))
    order, extra = (lax.dynamic_index_in_dim(jnp.asarray(t), kind, 0, keepdims=False) for t in row_orders(slab))
    kept, sent = arrange_call(rows, other, eye, order, extra, steps)
    arrived = lax.ppermute(sent, "vol", [(i, slabs - 1 - i) for i in range(slabs)])
    return kept, arrived


def shards(images, projections, assignment, interp_cells, interp_weights):
    class_count = lax.axis_size("cls")
    slab_count = lax.axis_size("vol")
    local_count, grid = images.shape[0], images.shape[1]
    dirs = projections.shape[1]
    slab = grid // slab_count
    width = 2 * slab
    halves = LANES // width
    capacity = 2 * local_count // class_count
    steps = 16 // capacity
    groups = grid // (halves * steps)

    eye = jnp.asarray(np.eye(grid), BF16)
    order = jnp.asarray(lane_order(grid, slab_count))
    outgoing = route_call(images, assignment, eye, order, class_count, slab_count, width, capacity)
    outgoing, projections = lax.optimization_barrier((outgoing, projections))
    arrived = lax.all_to_all(outgoing, ("cls", "vol"), split_axis=0, concat_axis=0, tiled=True)

    kept, joined = paired_rows(projections[0], eye, slab_count, steps)
    corner_y = (interp_cells[:, 0:1, :] & (grid - 1)).astype(F32)
    weights = jnp.concatenate([interp_weights, corner_y, jnp.zeros((dirs, 3, grid), F32)], axis=1)
    weights = weights.reshape(dirs, 8, halves, groups, steps)
    weights = jnp.transpose(weights, (3, 4, 0, 2, 1)).reshape(groups, steps * dirs, 8 * halves)
    weights = jnp.pad(weights, ((0, 0), (0, 0), (0, LANES - 8 * halves)))
    plan = sorted_points(interp_cells, grid)
    table_y, table_x, table_z, restore = tables(grid, slab_count)

    arrived, kept, joined, weights, plan = lax.optimization_barrier((arrived, kept, joined, weights, plan))
    partial_value = scores_call(arrived, kept, joined, capacity, dirs, slab)
    copies = jnp.broadcast_to(partial_value[None], (slab_count,) + partial_value.shape)
    parts = lax.all_to_all(copies, "vol", split_axis=0, concat_axis=0, tiled=True)
    own = lax.axis_index("vol")
    single = (own == slab_count // 2).astype(jnp.int32).reshape(1)
    flip = (own >= slab_count // 2).astype(jnp.int32).reshape(1)
    sent, plane = scatter_call(
        single, plan, parts, arrived, weights, table_y, table_x, capacity, width, grid, slab_count
    )
    received = [lax.all_to_all(sent, "vol", split_axis=0, concat_axis=0, tiled=True)]
    if plane is not None:
        sent = planes_call(plane, table_y, table_x, slab_count, grid)
        received.append(lax.all_to_all(sent, "vol", split_axis=0, concat_axis=0, tiled=True))
    return volume_call(flip, received, restore, table_z)[None]


def solution(mesh):
    in_specs = (
        P(("cls", "vol"), None, None, None),
        P("cls", None, "vol", None, None),
        P(("cls", "vol"), None),
        P(),
        P(),
    )
    out_specs = P("cls", "vol", None, None)
    return jax.shard_map(shards, mesh=mesh, in_specs=in_specs, out_specs=out_specs, check_vma=False)
```

```python
import functools
import math

import jax
import jax.numpy as jnp
import numpy as np
from jax import lax
from jax.experimental import pallas as pl
from jax.experimental.pallas import tpu as pltpu
from jax.sharding import PartitionSpec as P

F32 = jnp.float32
BF16 = jnp.bfloat16
LANES = 128
HALF = 64
CHUNK = 128
PAD = 8
UNROLL = 8
STEP = 16
VMEM = pltpu.VMEM


def split_table(table):
    high = table.astype(jnp.bfloat16)
    low = (table - high.astype(np.float64)).astype(jnp.bfloat16)
    return high, low


def plane_pairs(grid, slabs):
    slab = grid // slabs
    half = slab // 2
    pairs = []
    for w in range(slabs):
        for i in range(half):
            if w < slabs // 2:
                first = slab * w + 1 + i
            else:
                first = slab * w + half - 1 - i
            if 2 * first == grid:
                pairs.append((0, first))
            else:
                pairs.append((first, grid - first))
    return np.array(pairs).reshape(slabs, half, 2)


def tables(grid, slabs):
    half = grid // 2
    scale = 1.0 / math.sqrt(grid)
    index = np.arange(grid)
    angle = 2.0 * np.pi / grid
    phase = (index[:, None] * np.arange(half)[None, :]) % grid
    cosine = np.cos(phase * angle)
    sine = np.sin(phase * angle)
    sine[:, 0] = np.cos(((index * half) % grid) * angle)
    table_y = np.concatenate([cosine, sine], axis=1) * scale
    rows = half + 8
    phase = (np.arange(rows)[:, None] * index[None, :]) % grid
    live = (np.arange(rows) <= half)[:, None]
    table_x = np.concatenate([np.cos(phase * angle) * live, np.sin(phase * angle) * live], axis=0) * scale
    pairs = plane_pairs(grid, slabs).reshape(-1, 2)
    single = (2 * pairs[:, 1] == grid)[:, None]
    z = np.where(single[:, 0], pairs[:, 1], pairs[:, 0])
    phase = (z[:, None] * index[None, :]) % grid
    for_sum = np.where(single, 1.0, np.cos(phase * angle))
    for_difference = np.where(single, np.cos(phase * angle), -np.sin(phase * angle))
    table_z = np.stack([for_sum, for_difference], axis=1).reshape(grid, grid) * scale
    order = np.concatenate([np.arange(half), [half], np.arange(grid - 1, half, -1)])
    restore = (order[None, :] == index[:, None]).astype(jnp.bfloat16)
    parts = max(1, grid // slabs // STEP)
    table_z = table_z.reshape(slabs, parts, -1, grid).transpose(1, 0, 2, 3).reshape(grid, grid)
    high, low = split_table(table_y)
    table_y = np.concatenate([high, high, low], axis=0)
    high, low = split_table(table_x)
    table_x = np.concatenate([high, high, low], axis=1)
    table_z = np.concatenate(split_table(table_z), axis=0)
    return table_y, table_x, table_z, restore


def lane_order(grid, slabs):
    rows = plane_pairs(grid, slabs).transpose(0, 2, 1).reshape(-1)
    source = (2 * rows[:, None] + np.arange(2)[None, :]).reshape(-1)
    return (np.arange(2 * grid)[:, None] == source[None, :]).astype(jnp.bfloat16)


def dot(a, b):
    return jnp.dot(a, b, preferred_element_type=F32)


def dot_t(a, b):
    return lax.dot_general(a, b, (((1,), (1,)), ((), ())), preferred_element_type=F32)


def two_terms(value):
    high = value.astype(BF16)
    low = (value - high.astype(F32)).astype(BF16)
    return high, low


def route_kernel(cap, slabs, width, classes_ref, images_ref, eye_ref, order_ref, out_ref, lines):
    count, _, _, grid = images_ref.shape
    halves = LANES // width
    piece = grid // halves
    lane = lax.broadcasted_iota(jnp.int32, (piece, LANES), 1)
    lines[...] = jnp.zeros_like(lines)

    def place(p, carry):
        own = classes_ref[p, 0]
        rank = 0
        for q in range(count):
            rank = rank + jnp.where((classes_ref[q, 0] == own) & (q < p), 1, 0)
        image = images_ref[p].reshape(-1, grid)
        turned = dot(dot_t(eye_ref[...], image).astype(BF16), order_ref[...])
        for w in range(slabs):
            tile = w * width // LANES * LANES
            block = jnp.zeros((piece, LANES), F32)
            for h in range(halves):
                part = turned[h * piece : (h + 1) * piece, tile : tile + LANES]
                shift = (h * width - (w * width - tile)) % LANES
                part = part if shift == 0 else pltpu.roll(part, shift, 1)
                block = jnp.where((lane >= h * width) & (lane < (h + 1) * width), part, block)
            lines[own * slabs + w, pl.ds(rank, piece, stride=cap), :] = block
        return carry

    lax.fori_loop(0, count, place, 0, unroll=2)
    out_ref[...] = lines[...].astype(BF16).reshape(out_ref.shape)


def route_call(images, assignment, eye, order, class_count, slabs, width, cap):
    count, grid = images.shape[0], images.shape[1]
    rows = grid // (LANES // width) * cap
    vmem = pl.BlockSpec(memory_space=VMEM)
    return pl.pallas_call(
        functools.partial(route_kernel, cap, slabs, width),
        out_shape=jax.ShapeDtypeStruct((class_count * slabs, rows // 16, 16, LANES), BF16),
        in_specs=[pl.BlockSpec(memory_space=pltpu.SMEM)] + [vmem] * 3,
        out_specs=vmem,
        scratch_shapes=[VMEM((class_count * slabs, rows, LANES), F32)],
        compiler_params=pltpu.CompilerParams(vmem_limit_bytes=48 * 2**20),
        name="route",
    )(assignment, images, eye, order)


def score_kernel(cap, dirs, unit, first_ref, second_ref, kept_ref, joined_ref, out_ref, sums):
    sources, groups, rows16, _ = first_ref.shape
    rows = sources * rows16
    steps = rows16 // cap
    lane = lax.broadcasted_iota(jnp.int32, (steps * dirs, LANES), 1)
    even = (lane & unit) == 0

    @pl.when(pl.program_id(0) == 0)
    def _():
        sums[...] = jnp.zeros_like(sums)

    for g in range(groups):
        kept = kept_ref[g].astype(F32)
        joined = joined_ref[g].astype(F32)
        refs = [
            jnp.where(even, kept, pltpu.roll(joined, unit, 1)).astype(BF16),
            jnp.where(even, pltpu.roll(kept, LANES - unit, 1), joined).astype(BF16),
        ]
        blocks = [ref[:, g].reshape(rows, LANES) for ref in (first_ref, second_ref)]
        sums[...] += dot_t(jnp.concatenate(refs, axis=1), jnp.concatenate(blocks, axis=1))

    @pl.when(pl.program_id(0) == pl.num_programs(0) - 1)
    def _():
        column = lax.broadcasted_iota(jnp.int32, (dirs, rows), 1)
        part = (column & (rows16 - 1)) // cap
        kept = jnp.zeros((dirs, rows), F32)
        for j in range(steps):
            kept = kept + jnp.where(part == j, sums[j * dirs : (j + 1) * dirs, :], 0.0)
        slots = sources * cap
        row_id = lax.broadcasted_iota(jnp.int32, (rows, slots), 0)
        slot_id = lax.broadcasted_iota(jnp.int32, (rows, slots), 1)
        gather = (row_id // rows16 * cap + row_id % cap) == slot_id
        value = jnp.dot(
            kept, gather.astype(F32), preferred_element_type=F32, precision=lax.Precision.HIGHEST
        )
        for copy in range(out_ref.shape[0]):
            out_ref[copy] = value


def scores_call(images, kept, joined, cap, dirs, unit, slabs):
    sources, groups, rows16, _ = images.shape
    joint = kept.shape[1]
    span = min(4, groups // 2)
    turns = groups // 2 // span
    return pl.pallas_call(
        functools.partial(score_kernel, cap, dirs, unit),
        grid=(turns,),
        out_shape=jax.ShapeDtypeStruct((slabs, dirs, sources * cap), F32),
        in_specs=[
            pl.BlockSpec((sources, span, rows16, LANES), lambda i: (0, i, 0, 0)),
            pl.BlockSpec((sources, span, rows16, LANES), lambda i: (0, i + turns, 0, 0)),
            pl.BlockSpec((span, joint, LANES), lambda i: (i, 0, 0)),
            pl.BlockSpec((span, joint, LANES), lambda i: (i, 0, 0)),
        ],
        out_specs=pl.BlockSpec((slabs, dirs, sources * cap), lambda i: (0, 0, 0)),
        scratch_shapes=[VMEM((joint, sources * rows16), F32)],
        compiler_params=pltpu.CompilerParams(vmem_limit_bytes=48 * 2**20),
        name="scores",
    )(images, images, kept, joined)


def scatter_kernel(
    cap,
    width,
    grid,
    slabs,
    single_ref,
    first_ref,
    point_ref,
    parts_ref,
    images_hbm,
    weights_hbm,
    y_ref,
    x_ref,
    sent_ref,
    *refs,
):
    rest = width > STEP * 2
    rest_hbm = refs[0] if rest else None
    plane, values, sums, spread, lines, images_ref, weights_ref, image_sem, weight_sem, rest_sem, *buffers = refs[rest:]
    sources, groups, rows16, _ = images_ref.shape
    pieces = weight_sem.shape[0]
    images_copy = pltpu.make_async_copy(images_hbm, images_ref, image_sem)
    images_copy.start()
    weight_copies = []
    for i in range(pieces):
        part = pl.ds(i * (groups // pieces), groups // pieces)
        weight_copies.append(pltpu.make_async_copy(weights_hbm.at[part], weights_ref.at[part], weight_sem.at[i]))
        weight_copies[i].start()
    rows = sources * rows16
    steps = rows16 // cap
    dirs, slots = parts_ref.shape[1:]
    joined = steps * dirs
    halves = LANES // width

    total = parts_ref[0]
    for i in range(1, parts_ref.shape[0]):
        total = total + parts_ref[i]
    expo = jnp.exp(total - jnp.max(total, axis=0, keepdims=True))
    posterior = (expo / jnp.sum(expo, axis=0, keepdims=True)).astype(BF16)
    slot_id = lax.broadcasted_iota(jnp.int32, (slots, rows), 0)
    row_id = lax.broadcasted_iota(jnp.int32, (slots, rows), 1)
    repeat = ((row_id // rows16 * cap + row_id % cap) == slot_id).astype(F32).astype(BF16)
    wide = dot(posterior, repeat)
    part = (lax.broadcasted_iota(jnp.int32, (dirs, rows), 1) & (rows16 - 1)) // cap
    for j in range(steps):
        spread[j * dirs : (j + 1) * dirs, :] = jnp.where(part == j, wide, 0.0).astype(BF16)

    lane_j = lax.broadcasted_iota(jnp.int32, (joined, LANES), 1)

    def average(m, carry):
        blocks = [images_ref[:, pl.ds(2 * m + i, 1), :, :].reshape(rows, LANES) for i in range(2)]
        means = dot(spread[...], jnp.concatenate(blocks, axis=1))
        for i in range(2):
            g = 2 * m + i
            mean = means[:, i * LANES : (i + 1) * LANES]
            weight = weights_ref[g]
            for h in range(halves):
                shifted = mean if h == 0 else pltpu.roll(mean, LANES - h * width, 1)
                behind = pltpu.roll(weight, HALF - 8 * h, 1)
                start = pl.multiple_of((h * groups + g) * joined, joined)
                values[pl.ds(start, joined), :] = jnp.where(lane_j < HALF, shifted, behind)
        return carry

    images_copy.wait()
    for i in range(pieces):
        weight_copies[i].wait()
        begin = groups // pieces // 2
        lax.fori_loop(i * begin, (i + 1) * begin, average, 0)

    for buffer in buffers:
        buffer[...] = jnp.zeros_like(buffer)
    sums[...] = jnp.zeros_like(sums)

    place = lax.broadcasted_iota(jnp.int32, (CHUNK, LANES), 0)
    lane = lax.broadcasted_iota(jnp.int32, (CHUNK, grid), 1)
    at_y = lane.astype(F32).astype(BF16)
    at_next = ((lane + (grid - 1)) & (grid - 1)).astype(F32).astype(BF16)
    line_8 = lax.broadcasted_iota(jnp.int32, (8, LANES), 0)
    one = jnp.ones((CHUNK, grid), BF16)
    none = jnp.zeros((CHUNK, grid), BF16)

    lane_1 = lax.broadcasted_iota(jnp.int32, (1, CHUNK), 1)
    points = values.shape[0]

    lines_of = values.reshape(points, 1, LANES)

    def fetch(start, buffer):
        chosen = point_ref.at[pl.ds(start, CHUNK)]
        for i in range(0, CHUNK, 8):
            block = jnp.broadcast_to(lines_of[chosen[i]], (8, LANES))
            for j in range(1, 8):
                block = jnp.where(line_8 == j, jnp.broadcast_to(lines_of[chosen[i + j]], (8, LANES)), block)
            buffer[i : i + 8, :] = block

    def put(row, value):
        x = (row + (grid - 1)) & (grid - 1)
        for side in range(grid // LANES):
            plane[side, pl.ds(x, width, stride=grid + PAD), :] = value[:, side * LANES : (side + 1) * LANES]

    def combined(mean):
        a, b = mean[: width // 2], mean[width // 2 :]
        total, gap = a + b, a - b
        tile = width // 2 - 8
        special = (single_ref[0] == 1) & (line_8 >= 6)
        moved = jnp.where(line_8 == 6, -pltpu.roll(b[tile:], 7, 0), pltpu.roll(b[tile:], 1, 0))
        total = [total[:tile], jnp.where(special, a[tile:], total[tile:])]
        gap = [gap[:tile], jnp.where(special, moved, gap[tile:])]
        return jnp.concatenate([part for part in total + gap if part.shape[0]], axis=0)

    def following(start, row):
        second, third = first_ref[row + 1], first_ref[row + 2]
        end = jnp.minimum(start + CHUNK, third)
        moved = row + jnp.where(end >= second, 1, 0) + jnp.where(end >= third, 1, 0)
        return end, jnp.minimum(moved, grid - 1), end - start, jnp.clip(second - start, 0, end - start)

    def work(row, before, size, size_0, buffer):
        data = buffer[...]
        y = jnp.broadcast_to(data[:, HALF + 4 : HALF + 5], (CHUNK, LANES))
        y = jnp.where(place < size, y, -1.0).astype(BF16)
        y = jnp.concatenate([y] * (grid // LANES), axis=1)
        hot = jnp.concatenate([jnp.where(at_y == y, one, none), jnp.where(at_next == y, one, none)], axis=0)
        turned = data.T
        mean = combined(turned[:width])
        weight = [turned[HALF + j : HALF + j + 1] for j in range(4)]
        here = [jnp.where(lane_1 < size_0, w, 0.0) for w in weight]
        there = [w - h for w, h in zip(weight, here)]
        by_row = (
            (here[0], here[2]),
            (here[1] + there[0], here[3] + there[2]),
            (there[1], there[3]),
        )
        operand = jnp.concatenate(
            [
                jnp.concatenate([mean * jnp.broadcast_to(w, (width, CHUNK)) for w in pair], axis=1)
                for pair in by_row
            ],
            axis=0,
        )
        result = dot(operand.astype(BF16), hot)
        old = [sums[i * width : (i + 1) * width] for i in range(3)]
        put(jnp.minimum(before + 1, grid - 1), old[1])
        put(before, old[0])
        stay, by_one = row == before, row == before + 1
        kept = (
            jnp.where(stay, old[0], jnp.where(by_one, old[1], old[2])),
            jnp.where(stay, old[1], jnp.where(by_one, old[2], 0.0)),
            jnp.where(stay, old[2], 0.0),
        )
        for i in range(3):
            sums[i * width : (i + 1) * width] = result[i * width : (i + 1) * width] + kept[i]

    fetch(0, buffers[0])

    def several(state):
        start, row, before = state
        for i in range(UNROLL):
            end, moved, size, size_0 = following(start, row)
            fetch(end, buffers[(i + 1) % UNROLL])
            work(row, before, size, size_0, buffers[i])
            start, row, before = end, moved, row
        return start, row, before

    zero = jnp.int32(0)
    lax.while_loop(lambda state: (state[0] < points) | (state[2] < grid - 1), several, (zero, zero, zero))
    put(grid - 1, sums[:width])
    for side in range(grid // LANES):
        wrapped = pl.ds(grid - 1, width, stride=grid + PAD)
        cut = slice(side * LANES, (side + 1) * LANES)
        plane[side, wrapped, :] = plane[side, wrapped, :] + sums[width : 2 * width, cut]

    pitch = grid + PAD
    step = min(STEP, width // 2)
    copies = []
    if rest:
        size = (width // 2 - step) * pitch
        for part in range(grid // LANES):
            for side in range(2):
                source = plane.at[part, pl.ds((side * (width // 2) + step) * pitch, size)]
                copies.append(pltpu.make_async_copy(source, rest_hbm.at[part, side], rest_sem.at[2 * part + side]))
                copies[-1].start()

    def load(part, side, value):
        place = pl.multiple_of((side * (width // 2) + value) * pitch, 8)
        return plane[part, pl.ds(place, grid), :]

    transform_pairs(slabs, grid, step // 2, load, y_ref, x_ref, sent_ref, lines)
    for copy in copies:
        copy.wait()


def scatter_call(single, plan, parts, images, weights, table_y, table_x, cap, width, grid, slabs):
    sources, groups, rows16, _ = images.shape
    dirs = parts.shape[1]
    points = dirs * grid
    smem = pl.BlockSpec(memory_space=pltpu.SMEM)
    vmem = pl.BlockSpec(memory_space=VMEM)
    hbm = pl.BlockSpec(memory_space=pl.ANY)
    step = min(STEP, width // 2)
    other = width // 2 - step
    pitch = grid + PAD
    sides = grid // LANES
    pieces = 4
    shapes = [jax.ShapeDtypeStruct((slabs, grid // slabs, step, grid), BF16)]
    if other:
        shapes.append(jax.ShapeDtypeStruct((sides, 2, other * pitch, LANES), F32))
    result = pl.pallas_call(
        functools.partial(scatter_kernel, cap, width, grid, slabs),
        out_shape=shapes,
        in_specs=[smem] * 3 + [vmem, hbm, hbm, vmem, vmem],
        out_specs=[vmem, hbm][: len(shapes)],
        scratch_shapes=[
            VMEM((sides, width * pitch, LANES), F32),
            VMEM((points, LANES), F32),
            VMEM((3 * width, grid), F32),
            VMEM((weights.shape[1], sources * rows16), BF16),
            VMEM((sides, grid * step, LANES), F32),
            VMEM(images.shape, BF16),
            VMEM(weights.shape, F32),
            pltpu.SemaphoreType.DMA,
            pltpu.SemaphoreType.DMA((pieces,)),
            pltpu.SemaphoreType.DMA((2 * sides,)),
        ]
        + [VMEM((CHUNK, LANES), F32)] * UNROLL,
        compiler_params=pltpu.CompilerParams(vmem_limit_bytes=61 * 2**20),
        name="scatter",
    )(single, *plan, parts, images, weights, table_y, table_x)
    if not other:
        return result[0], None
    return result[0], result[1].reshape(sides, 2, other, pitch, LANES)


def transform_pairs(slabs, grid, pairs, load, y_ref, x_ref, out_ref, lines):
    half = grid // 2
    rows = half + 8
    slab = grid // slabs
    count = 2 * pairs
    lane = lax.broadcasted_iota(jnp.int32, (grid, half), 1)

    def transformed(real, imag):
        cos_r, sin_r = real[:, :half], real[:, half:]
        cos_i, sin_i = imag[:, :half], imag[:, half:]
        zero_r = jnp.where(lane == 0, 0.0, sin_r)
        zero_i = jnp.where(lane == 0, 0.0, sin_i)
        real = jnp.concatenate([cos_r - zero_i, jnp.where(lane == 0, sin_r, cos_r + sin_i)], axis=1)
        imag = jnp.concatenate([cos_i + zero_r, jnp.where(lane == 0, sin_i, cos_i - sin_r)], axis=1)
        return real, imag

    def along_x(table, operand):
        high, low = two_terms(operand)
        return dot(x_ref[table * rows : (table + 1) * rows], jnp.concatenate([high, low, high], axis=0))

    def one(i, carry):
        planes = [
            jnp.concatenate([load(part, side, 2 * i + r) for part in range(grid // LANES)], axis=1)
            for side in range(2)
            for r in range(2)
        ]
        both = []
        for value in planes:
            high, low = two_terms(value)
            both.append(dot(jnp.concatenate([high, low, high], axis=1), y_ref[...]))
        sum_r, sum_i = transformed(both[0], both[1])
        dif_r, dif_i = transformed(both[2], both[3])
        cosine = along_x(0, jnp.concatenate([sum_r, dif_i], axis=1))
        sine = along_x(1, jnp.concatenate([sum_i, dif_r], axis=1))
        fields = (
            (cosine[:, :grid] - sine[:, :grid], cosine[:, :grid] + sine[:, :grid]),
            (cosine[:, grid:] + sine[:, grid:], cosine[:, grid:] - sine[:, grid:]),
        )
        for c in range(2):
            plus, minus = fields[c]
            for part in range(grid // LANES):
                cut = slice(part * LANES, (part + 1) * LANES)
                place = 2 * i + c
                lines[part, pl.ds(place, half, stride=count), :] = plus[:half, cut]
                lines[part, pl.ds(half * count + place, half, stride=count), :] = minus[1 : half + 1, cut]
        return carry

    lax.fori_loop(0, pairs, one, 0, unroll=2)
    for d in range(slabs):
        if d < slabs // 2:
            start = slab * d
        else:
            start = half + grid - slab * d - slab
        size = slab * count
        for part in range(grid // LANES):
            block = lines[part, start * count : start * count + size, :]
            out_ref[d, :, :, part * LANES : (part + 1) * LANES] = block.astype(BF16).reshape(slab, count, LANES)


def plane_kernel(slabs, grid, data_ref, y_ref, x_ref, out_ref, lines):
    pairs = data_ref.shape[2] // 2

    def load(part, side, value):
        return data_ref[part, side, value][:grid]

    transform_pairs(slabs, grid, pairs, load, y_ref, x_ref, out_ref, lines)


def planes_call(data, table_y, table_x, slabs, grid):
    step = data.shape[2]
    slab = grid // slabs
    vmem = pl.BlockSpec(memory_space=VMEM)
    return pl.pallas_call(
        functools.partial(plane_kernel, slabs, grid),
        in_specs=[vmem] * 3,
        out_specs=vmem,
        scratch_shapes=[VMEM((data.shape[0], grid * step, LANES), F32)],
        out_shape=jax.ShapeDtypeStruct((slabs, slab, step, grid), BF16),
        compiler_params=pltpu.CompilerParams(vmem_limit_bytes=56 * 2**20),
        name="planes",
    )(data, table_y, table_x)


def volume_kernel(flip_ref, restore_ref, z_ref, *refs):
    out_ref = refs[-1]
    slabs, span, width, grid = refs[0].shape
    turned = []
    for i in range(span):
        block = jnp.concatenate([ref[:, i].reshape(slabs * width, grid) for ref in refs[:-1]], axis=0)
        turned.append(dot_t(restore_ref[...], block).astype(BF16))
    turned = jnp.concatenate(turned, axis=0)
    value = dot(jnp.concatenate([turned, turned], axis=1), z_ref[...])
    for i in range(span):
        out_ref[jnp.where(flip_ref[0] == 1, span - 1 - i, i)] = value[i * grid : (i + 1) * grid]


def volume_call(flip, parts, restore, table_z):
    slabs, slab, width, grid = parts[0].shape
    span = 4
    steps = slab // span
    fixed = lambda i, flip_ref: (0, 0)
    return pl.pallas_call(
        volume_kernel,
        grid_spec=pltpu.PrefetchScalarGridSpec(
            num_scalar_prefetch=1,
            grid=(steps,),
            in_specs=[pl.BlockSpec(restore.shape, fixed), pl.BlockSpec(table_z.shape, fixed)]
            + [pl.BlockSpec((slabs, span, width, grid), lambda i, flip_ref: (0, i, 0, 0))] * len(parts),
            out_specs=pl.BlockSpec(
                (span, grid, grid), lambda i, flip_ref: (jnp.where(flip_ref[0] == 1, steps - 1 - i, i), 0, 0)
            ),
        ),
        out_shape=jax.ShapeDtypeStruct((slab, grid, grid), F32),
        compiler_params=pltpu.CompilerParams(vmem_limit_bytes=48 * 2**20),
        name="volume",
    )(flip, restore, table_z, *parts)


def sorted_points(interp_cells, grid):
    dirs = interp_cells.shape[0]
    points = dirs * grid
    base = interp_cells[:, 0, :].T.reshape(-1)
    row = (base // grid + 1) & (grid - 1)
    key = row * points + jnp.arange(points, dtype=jnp.int32)
    key = lax.sort(key, is_stable=False)
    rows = jnp.arange(grid + 3, dtype=jnp.int32)
    first = jnp.sum((row[None, :] < rows[:, None]).astype(jnp.int32), axis=1)
    point = jnp.concatenate([key & (points - 1), jnp.zeros((CHUNK,), jnp.int32)])
    return first, point


def arrange_kernel(rows_ref, other_ref, eye_ref, order_ref, extra_ref, kept_ref, sent_ref, *lines):
    dirs, count, _, grid = rows_ref.shape
    blocks = LANES // count
    length = grid // blocks
    span = extra_ref.shape[0]
    each = span * blocks
    number = lax.broadcasted_iota(jnp.int32, (length, LANES), 1) // count

    def step(m, carry):
        other = other_ref[pl.ds(pl.multiple_of(2 * each * m, 2 * each), 2 * each), :]
        other = dot_t(eye_ref[...], other).astype(BF16)
        for group in range(span):
            k = each * m + blocks * group
            block = rows_ref[pl.ds(k, blocks)].reshape(2 * LANES, grid)
            turned = dot_t(eye_ref[...], block).astype(BF16)
            turned = dot(turned, order_ref[...]) + dot(other, extra_ref[group])
            for side in range(2):
                tile = [turned[q * length : (q + 1) * length, side * LANES : (side + 1) * LANES] for q in range(blocks)]
                bit = 1
                while bit < blocks:
                    low = (number & bit) == 0
                    swapped = list(tile)
                    for q in range(blocks):
                        if q & bit == 0:
                            swapped[q] = jnp.where(low, tile[q], pltpu.roll(tile[q + bit], bit * count, 1))
                            swapped[q + bit] = jnp.where(low, pltpu.roll(tile[q], LANES - bit * count, 1), tile[q + bit])
                    tile = swapped
                    bit *= 2
                for i in range(blocks):
                    lines[side][pl.ds(k + i, length, stride=dirs + PAD), :] = tile[i]
        return carry

    lax.fori_loop(0, dirs // each, step, 0)
    for side, out_ref in enumerate((kept_ref, sent_ref)):
        steps = out_ref.shape[1] // dirs
        for u in range(length):
            block = lines[side][u * (dirs + PAD) : u * (dirs + PAD) + dirs, :].astype(BF16)
            out_ref[u // steps, u % steps * dirs : (u % steps + 1) * dirs, :] = block


def arrange_call(rows, other, eye, order, extra, steps):
    dirs, count, _, grid = rows.shape
    length = grid // (LANES // count)
    vmem = pl.BlockSpec(memory_space=VMEM)
    shape = jax.ShapeDtypeStruct((length // steps, steps * dirs, LANES), BF16)
    return pl.pallas_call(
        arrange_kernel,
        out_shape=(shape, shape),
        in_specs=[vmem] * 5,
        out_specs=(vmem, vmem),
        scratch_shapes=[VMEM((length * (dirs + PAD), LANES), F32)] * 2,
        compiler_params=pltpu.CompilerParams(vmem_limit_bytes=48 * 2**20),
        name="arrange",
    )(rows, other, eye, order, extra)


def row_orders(slab):
    half = slab // 2
    blocks = LANES // slab
    span = max(1, 8 // blocks)
    down = list(range(half - 1, -1, -1))
    upper = list(range(slab - 1, half - 1, -1))
    orders, extras = [], []
    for kept, sent in (
        (list(range(1, half + 1)), list(range(half + 1, slab)) + [None]),
        (down[:-1] + [None], upper),
        (down, upper),
    ):
        order = np.zeros((2 * LANES, 2 * LANES))
        extra = np.zeros((span, 2 * span * blocks, 2 * LANES))
        for side, rows in enumerate((kept, sent)):
            for k in range(blocks):
                for i, row in enumerate(rows):
                    for r in range(2):
                        lane = side * LANES + k * slab + 2 * i + r
                        if row is not None:
                            order[(k * slab + row) * 2 + r, lane] = 1.0
                        else:
                            for group in range(span):
                                extra[group, (group * blocks + k) * 2 + r, lane] = 1.0
        orders.append(order.astype(jnp.bfloat16))
        extras.append(extra.astype(jnp.bfloat16))
    return np.stack(orders), np.stack(extras)


def paired_rows(rows, eye, slabs, steps):
    own = lax.axis_index("vol")
    dirs, slab, _, grid = rows.shape
    first = [(0, slabs // 2)] + [(i, i - 1) for i in range(1, slabs // 2 + 1)]
    other = lax.ppermute(rows[:, 0], "vol", first).reshape(2 * dirs, grid)
    kind = jnp.where(own < slabs // 2, 0, jnp.where(own == slabs // 2, 1, 2))
    order, extra = (lax.dynamic_index_in_dim(jnp.asarray(t), kind, 0, keepdims=False) for t in row_orders(slab))
    kept, sent = arrange_call(rows, other, eye, order, extra, steps)
    arrived = lax.ppermute(sent, "vol", [(i, slabs - 1 - i) for i in range(slabs)])
    return kept, arrived


def shards(images, projections, assignment, interp_cells, interp_weights):
    class_count = lax.axis_size("cls")
    slab_count = lax.axis_size("vol")
    local_count, grid = images.shape[0], images.shape[1]
    dirs = projections.shape[1]
    slab = grid // slab_count
    width = 2 * slab
    halves = LANES // width
    capacity = 2 * local_count // class_count
    steps = 16 // capacity
    groups = grid // (halves * steps)

    eye = jnp.asarray(np.eye(grid), BF16)
    order = jnp.asarray(lane_order(grid, slab_count))
    outgoing = route_call(images, assignment, eye, order, class_count, slab_count, width, capacity)
    outgoing, projections = lax.optimization_barrier((outgoing, projections))
    arrived = lax.all_to_all(outgoing, ("cls", "vol"), split_axis=0, concat_axis=0, tiled=True)

    kept, joined = paired_rows(projections[0], eye, slab_count, steps)
    corner_y = (interp_cells[:, 0:1, :] & (grid - 1)).astype(F32)
    weights = jnp.concatenate([interp_weights, corner_y, jnp.zeros((dirs, 3, grid), F32)], axis=1)
    weights = weights.reshape(dirs, 8, halves, groups, steps)
    weights = jnp.transpose(weights, (3, 4, 0, 2, 1)).reshape(groups, steps * dirs, 8 * halves)
    weights = jnp.pad(weights, ((0, 0), (0, 0), (0, LANES - 8 * halves)))
    plan = sorted_points(interp_cells, grid)
    table_y, table_x, table_z, restore = tables(grid, slab_count)

    arrived, kept, joined, weights, plan = lax.optimization_barrier((arrived, kept, joined, weights, plan))
    partial_value = scores_call(arrived, kept, joined, capacity, dirs, slab, slab_count)
    parts = lax.all_to_all(partial_value, "vol", split_axis=0, concat_axis=0, tiled=True)
    own = lax.axis_index("vol")
    single = (own == slab_count // 2).astype(jnp.int32).reshape(1)
    flip = (own >= slab_count // 2).astype(jnp.int32).reshape(1)
    sent, plane = scatter_call(
        single, plan, parts, arrived, weights, table_y, table_x, capacity, width, grid, slab_count
    )
    received = [lax.all_to_all(sent, "vol", split_axis=0, concat_axis=0, tiled=True)]
    if plane is not None:
        sent = planes_call(plane, table_y, table_x, slab_count, grid)
        received.append(lax.all_to_all(sent, "vol", split_axis=0, concat_axis=0, tiled=True))
    return volume_call(flip, received, restore, table_z)[None]


def solution(mesh):
    in_specs = (
        P(("cls", "vol"), None, None, None),
        P("cls", None, "vol", None, None),
        P(("cls", "vol"), None),
        P(),
        P(),
    )
    out_specs = P("cls", "vol", None, None)
    return jax.shard_map(shards, mesh=mesh, in_specs=in_specs, out_specs=out_specs, check_vma=False)
```

```python
import functools
import math

import jax
import jax.numpy as jnp
import numpy as np
from jax import lax
from jax.experimental import pallas as pl
from jax.experimental.pallas import tpu as pltpu
from jax.sharding import PartitionSpec as P

F32 = jnp.float32
BF16 = jnp.bfloat16
LANES = 128
HALF = 64
CHUNK = 128
PAD = 8
UNROLL = 16
STEP = 16
VMEM = pltpu.VMEM


def split_table(table):
    high = table.astype(jnp.bfloat16)
    low = (table - high.astype(np.float64)).astype(jnp.bfloat16)
    return high, low


def plane_pairs(grid, slabs):
    slab = grid // slabs
    half = slab // 2
    pairs = []
    for w in range(slabs):
        for i in range(half):
            if w < slabs // 2:
                first = slab * w + 1 + i
            else:
                first = slab * w + half - 1 - i
            if 2 * first == grid:
                pairs.append((0, first))
            else:
                pairs.append((first, grid - first))
    return np.array(pairs).reshape(slabs, half, 2)


def tables(grid, slabs):
    half = grid // 2
    scale = 1.0 / math.sqrt(grid)
    index = np.arange(grid)
    angle = 2.0 * np.pi / grid
    phase = (index[:, None] * np.arange(half)[None, :]) % grid
    cosine = np.cos(phase * angle)
    sine = np.sin(phase * angle)
    sine[:, 0] = np.cos(((index * half) % grid) * angle)
    table_y = np.concatenate([cosine, sine], axis=1) * scale
    rows = half + 8
    phase = (np.arange(rows)[:, None] * index[None, :]) % grid
    live = (np.arange(rows) <= half)[:, None]
    table_x = np.concatenate([np.cos(phase * angle) * live, np.sin(phase * angle) * live], axis=0) * scale
    pairs = plane_pairs(grid, slabs).reshape(-1, 2)
    single = (2 * pairs[:, 1] == grid)[:, None]
    z = np.where(single[:, 0], pairs[:, 1], pairs[:, 0])
    phase = (z[:, None] * index[None, :]) % grid
    for_sum = np.where(single, 1.0, np.cos(phase * angle))
    for_difference = np.where(single, np.cos(phase * angle), -np.sin(phase * angle))
    table_z = np.stack([for_sum, for_difference], axis=1).reshape(grid, grid) * scale
    order = np.concatenate([np.arange(half), [half], np.arange(grid - 1, half, -1)])
    restore = (order[None, :] == index[:, None]).astype(jnp.bfloat16)
    parts = max(1, grid // slabs // STEP)
    table_z = table_z.reshape(slabs, parts, -1, grid).transpose(1, 0, 2, 3).reshape(grid, grid)
    high, low = split_table(table_y)
    table_y = np.concatenate([high, high, low], axis=0)
    high, low = split_table(table_x)
    table_x = np.concatenate([high, high, low], axis=1)
    table_z = [np.concatenate(split_table(part), axis=0) for part in np.split(table_z, parts)]
    return table_y, table_x, table_z, restore


def lane_order(grid, slabs):
    rows = plane_pairs(grid, slabs).transpose(0, 2, 1).reshape(-1)
    source = (2 * rows[:, None] + np.arange(2)[None, :]).reshape(-1)
    return (np.arange(2 * grid)[:, None] == source[None, :]).astype(jnp.bfloat16)


def dot(a, b):
    return jnp.dot(a, b, preferred_element_type=F32)


def dot_t(a, b):
    return lax.dot_general(a, b, (((1,), (1,)), ((), ())), preferred_element_type=F32)


def two_terms(value):
    high = value.astype(BF16)
    low = (value - high.astype(F32)).astype(BF16)
    return high, low


def route_kernel(cap, slabs, width, classes_ref, images_ref, eye_ref, order_ref, out_ref, lines):
    count, _, _, grid = images_ref.shape
    halves = LANES // width
    piece = grid // halves
    lane = lax.broadcasted_iota(jnp.int32, (piece, LANES), 1)
    lines[...] = jnp.zeros_like(lines)

    def place(p, carry):
        own = classes_ref[p, 0]
        rank = 0
        for q in range(count):
            rank = rank + jnp.where((classes_ref[q, 0] == own) & (q < p), 1, 0)
        image = images_ref[p].reshape(-1, grid)
        turned = dot(dot_t(eye_ref[...], image).astype(BF16), order_ref[...])
        for w in range(slabs):
            tile = w * width // LANES * LANES
            block = jnp.zeros((piece, LANES), F32)
            for h in range(halves):
                part = turned[h * piece : (h + 1) * piece, tile : tile + LANES]
                shift = (h * width - (w * width - tile)) % LANES
                part = part if shift == 0 else pltpu.roll(part, shift, 1)
                block = jnp.where((lane >= h * width) & (lane < (h + 1) * width), part, block)
            lines[own * slabs + w, pl.ds(rank, piece, stride=cap), :] = block
        return carry

    lax.fori_loop(0, count, place, 0, unroll=2)
    out_ref[...] = lines[...].astype(BF16).reshape(out_ref.shape)


def route_call(images, assignment, eye, order, class_count, slabs, width, cap):
    count, grid = images.shape[0], images.shape[1]
    rows = grid // (LANES // width) * cap
    vmem = pl.BlockSpec(memory_space=VMEM)
    return pl.pallas_call(
        functools.partial(route_kernel, cap, slabs, width),
        out_shape=jax.ShapeDtypeStruct((class_count * slabs, rows // 16, 16, LANES), BF16),
        in_specs=[pl.BlockSpec(memory_space=pltpu.SMEM)] + [vmem] * 3,
        out_specs=vmem,
        scratch_shapes=[VMEM((class_count * slabs, rows, LANES), F32)],
        compiler_params=pltpu.CompilerParams(vmem_limit_bytes=48 * 2**20),
        name="route",
    )(assignment, images, eye, order)


def score_kernel(cap, dirs, unit, first_ref, second_ref, kept_ref, joined_ref, out_ref, sums):
    sources, groups, rows16, _ = first_ref.shape
    rows = sources * rows16
    steps = rows16 // cap
    lane = lax.broadcasted_iota(jnp.int32, (steps * dirs, LANES), 1)
    even = (lane & unit) == 0

    @pl.when(pl.program_id(0) == 0)
    def _():
        sums[...] = jnp.zeros_like(sums)

    for g in range(groups):
        kept = kept_ref[g].astype(F32)
        joined = joined_ref[g].astype(F32)
        refs = [
            jnp.where(even, kept, pltpu.roll(joined, unit, 1)).astype(BF16),
            jnp.where(even, pltpu.roll(kept, LANES - unit, 1), joined).astype(BF16),
        ]
        blocks = [ref[:, g].reshape(rows, LANES) for ref in (first_ref, second_ref)]
        sums[...] += dot_t(jnp.concatenate(refs, axis=1), jnp.concatenate(blocks, axis=1))

    @pl.when(pl.program_id(0) == pl.num_programs(0) - 1)
    def _():
        column = lax.broadcasted_iota(jnp.int32, (dirs, rows), 1)
        part = (column & (rows16 - 1)) // cap
        kept = jnp.zeros((dirs, rows), F32)
        for j in range(steps):
            kept = kept + jnp.where(part == j, sums[j * dirs : (j + 1) * dirs, :], 0.0)
        slots = sources * cap
        row_id = lax.broadcasted_iota(jnp.int32, (rows, slots), 0)
        slot_id = lax.broadcasted_iota(jnp.int32, (rows, slots), 1)
        gather = (row_id // rows16 * cap + row_id % cap) == slot_id
        value = jnp.dot(
            kept, gather.astype(F32), preferred_element_type=F32, precision=lax.Precision.HIGHEST
        )
        for copy in range(out_ref.shape[0]):
            out_ref[copy] = value


def scores_call(images, kept, joined, cap, dirs, unit, slabs):
    sources, groups, rows16, _ = images.shape
    joint = kept.shape[1]
    span = min(4, groups // 2)
    turns = groups // 2 // span
    return pl.pallas_call(
        functools.partial(score_kernel, cap, dirs, unit),
        grid=(turns,),
        out_shape=jax.ShapeDtypeStruct((slabs, dirs, sources * cap), F32),
        in_specs=[
            pl.BlockSpec((sources, span, rows16, LANES), lambda i: (0, i, 0, 0)),
            pl.BlockSpec((sources, span, rows16, LANES), lambda i: (0, i + turns, 0, 0)),
            pl.BlockSpec((span, joint, LANES), lambda i: (i, 0, 0)),
            pl.BlockSpec((span, joint, LANES), lambda i: (i, 0, 0)),
        ],
        out_specs=pl.BlockSpec((slabs, dirs, sources * cap), lambda i: (0, 0, 0)),
        scratch_shapes=[VMEM((joint, sources * rows16), F32)],
        compiler_params=pltpu.CompilerParams(vmem_limit_bytes=48 * 2**20),
        name="scores",
    )(images, images, kept, joined)


def scatter_kernel(
    cap,
    width,
    grid,
    slabs,
    single_ref,
    first_ref,
    point_ref,
    parts_ref,
    images_hbm,
    weights_hbm,
    y_ref,
    x_ref,
    sent_ref,
    *refs,
):
    rest = width > STEP * 2
    rest_hbm = refs[0] if rest else None
    plane, values, sums, spread, lines, images_ref, weights_ref, image_sem, weight_sem, rest_sem, *buffers = refs[rest:]
    sources, groups, rows16, _ = images_ref.shape
    pieces = weight_sem.shape[0]
    images_copy = pltpu.make_async_copy(images_hbm, images_ref, image_sem)
    images_copy.start()
    weight_copies = []
    for i in range(pieces):
        part = pl.ds(i * (groups // pieces), groups // pieces)
        weight_copies.append(pltpu.make_async_copy(weights_hbm.at[part], weights_ref.at[part], weight_sem.at[i]))
        weight_copies[i].start()
    rows = sources * rows16
    steps = rows16 // cap
    dirs, slots = parts_ref.shape[1:]
    joined = steps * dirs
    halves = LANES // width

    total = parts_ref[0]
    for i in range(1, parts_ref.shape[0]):
        total = total + parts_ref[i]
    expo = jnp.exp(total - jnp.max(total, axis=0, keepdims=True))
    posterior = (expo / jnp.sum(expo, axis=0, keepdims=True)).astype(BF16)
    slot_id = lax.broadcasted_iota(jnp.int32, (slots, rows), 0)
    row_id = lax.broadcasted_iota(jnp.int32, (slots, rows), 1)
    repeat = ((row_id // rows16 * cap + row_id % cap) == slot_id).astype(F32).astype(BF16)
    wide = dot(posterior, repeat)
    part = (lax.broadcasted_iota(jnp.int32, (dirs, rows), 1) & (rows16 - 1)) // cap
    for j in range(steps):
        spread[j * dirs : (j + 1) * dirs, :] = jnp.where(part == j, wide, 0.0).astype(BF16)

    lane_j = lax.broadcasted_iota(jnp.int32, (joined, LANES), 1)

    def average(m, carry):
        blocks = [images_ref[:, pl.ds(2 * m + i, 1), :, :].reshape(rows, LANES) for i in range(2)]
        means = dot(spread[...], jnp.concatenate(blocks, axis=1))
        for i in range(2):
            g = 2 * m + i
            mean = means[:, i * LANES : (i + 1) * LANES]
            weight = weights_ref[g]
            for h in range(halves):
                shifted = mean if h == 0 else pltpu.roll(mean, LANES - h * width, 1)
                behind = pltpu.roll(weight, HALF - 8 * h, 1)
                start = pl.multiple_of((h * groups + g) * joined, joined)
                values[pl.ds(start, joined), :] = jnp.where(lane_j < HALF, shifted, behind)
        return carry

    images_copy.wait()
    for i in range(pieces):
        weight_copies[i].wait()
        begin = groups // pieces // 2
        lax.fori_loop(i * begin, (i + 1) * begin, average, 0)

    for buffer in buffers:
        buffer[...] = jnp.zeros_like(buffer)
    sums[...] = jnp.zeros_like(sums)

    place = lax.broadcasted_iota(jnp.int32, (CHUNK, LANES), 0)
    lane = lax.broadcasted_iota(jnp.int32, (CHUNK, grid), 1)
    at_y = lane.astype(F32).astype(BF16)
    at_next = ((lane + (grid - 1)) & (grid - 1)).astype(F32).astype(BF16)
    line_8 = lax.broadcasted_iota(jnp.int32, (8, LANES), 0)
    one = jnp.ones((CHUNK, grid), BF16)
    none = jnp.zeros((CHUNK, grid), BF16)

    lane_1 = lax.broadcasted_iota(jnp.int32, (1, CHUNK), 1)
    points = values.shape[0]

    def fetch(start, buffer):
        for i in range(0, CHUNK, 8):
            block = jnp.broadcast_to(values[pl.ds(point_ref[start + i], 1), :], (8, LANES))
            for j in range(1, 8):
                line = jnp.broadcast_to(values[pl.ds(point_ref[start + i + j], 1), :], (8, LANES))
                block = jnp.where(line_8 == j, line, block)
            buffer[i : i + 8, :] = block

    def put(row, value):
        x = (row + (grid - 1)) & (grid - 1)
        for side in range(grid // LANES):
            plane[side, pl.ds(x, width, stride=grid + PAD), :] = value[:, side * LANES : (side + 1) * LANES]

    def combined(mean):
        a, b = mean[: width // 2], mean[width // 2 :]
        total, gap = a + b, a - b
        tile = width // 2 - 8
        special = (single_ref[0] == 1) & (line_8 >= 6)
        moved = jnp.where(line_8 == 6, -pltpu.roll(b[tile:], 7, 0), pltpu.roll(b[tile:], 1, 0))
        total = [total[:tile], jnp.where(special, a[tile:], total[tile:])]
        gap = [gap[:tile], jnp.where(special, moved, gap[tile:])]
        return jnp.concatenate([part for part in total + gap if part.shape[0]], axis=0)

    def following(start, row):
        second, third = first_ref[row + 1], first_ref[row + 2]
        end = jnp.minimum(start + CHUNK, third)
        moved = row + jnp.where(end >= second, 1, 0) + jnp.where(end >= third, 1, 0)
        return end, jnp.minimum(moved, grid - 1), end - start, jnp.clip(second - start, 0, end - start)

    def work(row, before, size, size_0, buffer):
        data = buffer[...]
        y = jnp.broadcast_to(data[:, HALF + 4 : HALF + 5], (CHUNK, LANES))
        y = jnp.where(place < size, y, -1.0).astype(BF16)
        y = jnp.concatenate([y] * (grid // LANES), axis=1)
        hot = jnp.concatenate([jnp.where(at_y == y, one, none), jnp.where(at_next == y, one, none)], axis=0)
        turned = data.T
        mean = combined(turned[:width])
        weight = [turned[HALF + j : HALF + j + 1] for j in range(4)]
        here = [jnp.where(lane_1 < size_0, w, 0.0) for w in weight]
        there = [w - h for w, h in zip(weight, here)]
        by_row = (
            (here[0], here[2]),
            (here[1] + there[0], here[3] + there[2]),
            (there[1], there[3]),
        )
        operand = jnp.concatenate(
            [
                jnp.concatenate([mean * jnp.broadcast_to(w, (width, CHUNK)) for w in pair], axis=1)
                for pair in by_row
            ],
            axis=0,
        )
        result = dot(operand.astype(BF16), hot)
        old = [sums[i * width : (i + 1) * width] for i in range(3)]
        put(jnp.minimum(before + 1, grid - 1), old[1])
        put(before, old[0])
        stay, by_one = row == before, row == before + 1
        kept = (
            jnp.where(stay, old[0], jnp.where(by_one, old[1], old[2])),
            jnp.where(stay, old[1], jnp.where(by_one, old[2], 0.0)),
            jnp.where(stay, old[2], 0.0),
        )
        for i in range(3):
            sums[i * width : (i + 1) * width] = result[i * width : (i + 1) * width] + kept[i]

    fetch(0, buffers[0])

    def several(state):
        start, row, before = state
        for i in range(UNROLL):
            end, moved, size, size_0 = following(start, row)
            fetch(end, buffers[(i + 1) % UNROLL])
            work(row, before, size, size_0, buffers[i])
            start, row, before = end, moved, row
        return start, row, before

    zero = jnp.int32(0)
    lax.while_loop(lambda state: (state[0] < points) | (state[2] < grid - 1), several, (zero, zero, zero))
    put(grid - 1, sums[:width])
    for side in range(grid // LANES):
        wrapped = pl.ds(grid - 1, width, stride=grid + PAD)
        cut = slice(side * LANES, (side + 1) * LANES)
        plane[side, wrapped, :] = plane[side, wrapped, :] + sums[width : 2 * width, cut]

    pitch = grid + PAD
    step = min(STEP, width // 2)
    copies = []
    if rest:
        size = (width // 2 - step) * pitch
        for part in range(grid // LANES):
            for side in range(2):
                source = plane.at[part, pl.ds((side * (width // 2) + step) * pitch, size)]
                copies.append(pltpu.make_async_copy(source, rest_hbm.at[part, side], rest_sem.at[2 * part + side]))
                copies[-1].start()

    def load(part, side, value):
        place = pl.multiple_of((side * (width // 2) + value) * pitch, 8)
        return plane[part, pl.ds(place, grid), :]

    transform_pairs(slabs, grid, step // 2, load, y_ref, x_ref, sent_ref, lines)
    for copy in copies:
        copy.wait()


def scatter_call(single, plan, parts, images, weights, table_y, table_x, cap, width, grid, slabs):
    sources, groups, rows16, _ = images.shape
    dirs = parts.shape[1]
    points = dirs * grid
    smem = pl.BlockSpec(memory_space=pltpu.SMEM)
    vmem = pl.BlockSpec(memory_space=VMEM)
    hbm = pl.BlockSpec(memory_space=pl.ANY)
    step = min(STEP, width // 2)
    other = width // 2 - step
    pitch = grid + PAD
    sides = grid // LANES
    pieces = 4
    shapes = [jax.ShapeDtypeStruct((slabs, grid // slabs, step, grid), BF16)]
    if other:
        shapes.append(jax.ShapeDtypeStruct((sides, 2, other * pitch, LANES), F32))
    result = pl.pallas_call(
        functools.partial(scatter_kernel, cap, width, grid, slabs),
        out_shape=shapes,
        in_specs=[smem] * 3 + [vmem, hbm, hbm, vmem, vmem],
        out_specs=[vmem, hbm][: len(shapes)],
        scratch_shapes=[
            VMEM((sides, width * pitch, LANES), F32),
            VMEM((points, LANES), F32),
            VMEM((3 * width, grid), F32),
            VMEM((weights.shape[1], sources * rows16), BF16),
            VMEM((sides, grid * step, LANES), F32),
            VMEM(images.shape, BF16),
            VMEM(weights.shape, F32),
            pltpu.SemaphoreType.DMA,
            pltpu.SemaphoreType.DMA((pieces,)),
            pltpu.SemaphoreType.DMA((2 * sides,)),
        ]
        + [VMEM((CHUNK, LANES), F32)] * UNROLL,
        compiler_params=pltpu.CompilerParams(vmem_limit_bytes=61 * 2**20),
        name="scatter",
    )(single, *plan, parts, images, weights, table_y, table_x)
    if not other:
        return result[0], None
    return result[0], result[1].reshape(sides, 2, other, pitch, LANES)


def transform_pairs(slabs, grid, pairs, load, y_ref, x_ref, out_ref, lines):
    half = grid // 2
    rows = half + 8
    slab = grid // slabs
    count = 2 * pairs
    lane = lax.broadcasted_iota(jnp.int32, (grid, half), 1)

    def transformed(real, imag):
        cos_r, sin_r = real[:, :half], real[:, half:]
        cos_i, sin_i = imag[:, :half], imag[:, half:]
        zero_r = jnp.where(lane == 0, 0.0, sin_r)
        zero_i = jnp.where(lane == 0, 0.0, sin_i)
        real = jnp.concatenate([cos_r - zero_i, jnp.where(lane == 0, sin_r, cos_r + sin_i)], axis=1)
        imag = jnp.concatenate([cos_i + zero_r, jnp.where(lane == 0, sin_i, cos_i - sin_r)], axis=1)
        return real, imag

    def along_x(table, operand):
        high, low = two_terms(operand)
        return dot(x_ref[table * rows : (table + 1) * rows], jnp.concatenate([high, low, high], axis=0))

    def one(i, carry):
        planes = [
            jnp.concatenate([load(part, side, 2 * i + r) for part in range(grid // LANES)], axis=1)
            for side in range(2)
            for r in range(2)
        ]
        both = []
        for value in planes:
            high, low = two_terms(value)
            both.append(dot(jnp.concatenate([high, low, high], axis=1), y_ref[...]))
        sum_r, sum_i = transformed(both[0], both[1])
        dif_r, dif_i = transformed(both[2], both[3])
        cosine = along_x(0, jnp.concatenate([sum_r, dif_i], axis=1))
        sine = along_x(1, jnp.concatenate([sum_i, dif_r], axis=1))
        fields = (
            (cosine[:, :grid] - sine[:, :grid], cosine[:, :grid] + sine[:, :grid]),
            (cosine[:, grid:] + sine[:, grid:], cosine[:, grid:] - sine[:, grid:]),
        )
        for c in range(2):
            plus, minus = fields[c]
            for part in range(grid // LANES):
                cut = slice(part * LANES, (part + 1) * LANES)
                place = 2 * i + c
                lines[part, pl.ds(place, half, stride=count), :] = plus[:half, cut]
                lines[part, pl.ds(half * count + place, half, stride=count), :] = minus[1 : half + 1, cut]
        return carry

    lax.fori_loop(0, pairs, one, 0, unroll=2)
    for d in range(slabs):
        if d < slabs // 2:
            start = slab * d
        else:
            start = half + grid - slab * d - slab
        size = slab * count
        for part in range(grid // LANES):
            block = lines[part, start * count : start * count + size, :]
            out_ref[d, :, :, part * LANES : (part + 1) * LANES] = block.astype(BF16).reshape(slab, count, LANES)


def plane_kernel(slabs, grid, data_ref, y_ref, x_ref, out_ref, lines):
    pairs = data_ref.shape[2] // 2

    def load(part, side, value):
        return data_ref[part, side, value][:grid]

    transform_pairs(slabs, grid, pairs, load, y_ref, x_ref, out_ref, lines)


def planes_call(data, table_y, table_x, slabs, grid):
    step = data.shape[2]
    slab = grid // slabs
    vmem = pl.BlockSpec(memory_space=VMEM)
    return pl.pallas_call(
        functools.partial(plane_kernel, slabs, grid),
        in_specs=[vmem] * 3,
        out_specs=vmem,
        scratch_shapes=[VMEM((data.shape[0], grid * step, LANES), F32)],
        out_shape=jax.ShapeDtypeStruct((slabs, slab, step, grid), BF16),
        compiler_params=pltpu.CompilerParams(vmem_limit_bytes=56 * 2**20),
        name="planes",
    )(data, table_y, table_x)


def volume_kernel(flip_ref, restore_ref, z_ref, data_ref, *refs):
    out_ref = refs[-1]
    slabs, span, width, grid = data_ref.shape
    turned = []
    for i in range(span):
        turned.append(dot_t(restore_ref[...], data_ref[:, i].reshape(slabs * width, grid)).astype(BF16))
    turned = jnp.concatenate(turned, axis=0)
    value = dot(jnp.concatenate([turned, turned], axis=1), z_ref[...])
    for i in range(span):
        place = jnp.where(flip_ref[0] == 1, span - 1 - i, i)
        term = value[i * grid : (i + 1) * grid]
        out_ref[place] = term if len(refs) == 1 else term + refs[0][place]


def volume_call(flip, data, restore, table_z, before):
    slabs, slab, width, grid = data.shape
    span = 4
    steps = slab // span
    fixed = lambda i, flip_ref: (0, 0)
    place = lambda i, flip_ref: (jnp.where(flip_ref[0] == 1, steps - 1 - i, i), 0, 0)
    whole = [] if before is None else [before]
    return pl.pallas_call(
        volume_kernel,
        grid_spec=pltpu.PrefetchScalarGridSpec(
            num_scalar_prefetch=1,
            grid=(steps,),
            in_specs=[
                pl.BlockSpec(restore.shape, fixed),
                pl.BlockSpec(table_z.shape, fixed),
                pl.BlockSpec((slabs, span, width, grid), lambda i, flip_ref: (0, i, 0, 0)),
            ]
            + [pl.BlockSpec((span, grid, grid), place)] * len(whole),
            out_specs=pl.BlockSpec((span, grid, grid), place),
        ),
        out_shape=jax.ShapeDtypeStruct((slab, grid, grid), F32),
        compiler_params=pltpu.CompilerParams(vmem_limit_bytes=48 * 2**20),
        name="volume",
    )(flip, restore, table_z, data, *whole)


def sorted_points(interp_cells, grid):
    dirs = interp_cells.shape[0]
    points = dirs * grid
    base = interp_cells[:, 0, :].T.reshape(-1)
    row = (base // grid + 1) & (grid - 1)
    key = row * points + jnp.arange(points, dtype=jnp.int32)
    key = lax.sort(key, is_stable=False)
    rows = jnp.arange(grid + 3, dtype=jnp.int32)
    first = jnp.sum((row[None, :] < rows[:, None]).astype(jnp.int32), axis=1)
    point = jnp.concatenate([key & (points - 1), jnp.zeros((CHUNK,), jnp.int32)])
    return first, point


def arrange_kernel(rows_ref, other_ref, eye_ref, order_ref, extra_ref, kept_ref, sent_ref, *lines):
    dirs, count, _, grid = rows_ref.shape
    blocks = LANES // count
    length = grid // blocks
    span = extra_ref.shape[0]
    each = span * blocks
    number = lax.broadcasted_iota(jnp.int32, (length, LANES), 1) // count

    def step(m, carry):
        other = other_ref[pl.ds(pl.multiple_of(2 * each * m, 2 * each), 2 * each), :]
        other = dot_t(eye_ref[...], other).astype(BF16)
        for group in range(span):
            k = each * m + blocks * group
            block = rows_ref[pl.ds(k, blocks)].reshape(2 * LANES, grid)
            turned = dot_t(eye_ref[...], block).astype(BF16)
            turned = dot(turned, order_ref[...]) + dot(other, extra_ref[group])
            for side in range(2):
                tile = [turned[q * length : (q + 1) * length, side * LANES : (side + 1) * LANES] for q in range(blocks)]
                bit = 1
                while bit < blocks:
                    low = (number & bit) == 0
                    swapped = list(tile)
                    for q in range(blocks):
                        if q & bit == 0:
                            swapped[q] = jnp.where(low, tile[q], pltpu.roll(tile[q + bit], bit * count, 1))
                            swapped[q + bit] = jnp.where(low, pltpu.roll(tile[q], LANES - bit * count, 1), tile[q + bit])
                    tile = swapped
                    bit *= 2
                for i in range(blocks):
                    lines[side][pl.ds(k + i, length, stride=dirs + PAD), :] = tile[i]
        return carry

    lax.fori_loop(0, dirs // each, step, 0)
    for side, out_ref in enumerate((kept_ref, sent_ref)):
        steps = out_ref.shape[1] // dirs
        for u in range(length):
            block = lines[side][u * (dirs + PAD) : u * (dirs + PAD) + dirs, :].astype(BF16)
            out_ref[u // steps, u % steps * dirs : (u % steps + 1) * dirs, :] = block


def arrange_call(rows, other, eye, order, extra, steps):
    dirs, count, _, grid = rows.shape
    length = grid // (LANES // count)
    vmem = pl.BlockSpec(memory_space=VMEM)
    shape = jax.ShapeDtypeStruct((length // steps, steps * dirs, LANES), BF16)
    return pl.pallas_call(
        arrange_kernel,
        out_shape=(shape, shape),
        in_specs=[vmem] * 5,
        out_specs=(vmem, vmem),
        scratch_shapes=[VMEM((length * (dirs + PAD), LANES), F32)] * 2,
        compiler_params=pltpu.CompilerParams(vmem_limit_bytes=48 * 2**20),
        name="arrange",
    )(rows, other, eye, order, extra)


def row_orders(slab):
    half = slab // 2
    blocks = LANES // slab
    span = max(1, 8 // blocks)
    down = list(range(half - 1, -1, -1))
    upper = list(range(slab - 1, half - 1, -1))
    orders, extras = [], []
    for kept, sent in (
        (list(range(1, half + 1)), list(range(half + 1, slab)) + [None]),
        (down[:-1] + [None], upper),
        (down, upper),
    ):
        order = np.zeros((2 * LANES, 2 * LANES))
        extra = np.zeros((span, 2 * span * blocks, 2 * LANES))
        for side, rows in enumerate((kept, sent)):
            for k in range(blocks):
                for i, row in enumerate(rows):
                    for r in range(2):
                        lane = side * LANES + k * slab + 2 * i + r
                        if row is not None:
                            order[(k * slab + row) * 2 + r, lane] = 1.0
                        else:
                            for group in range(span):
                                extra[group, (group * blocks + k) * 2 + r, lane] = 1.0
        orders.append(order.astype(jnp.bfloat16))
        extras.append(extra.astype(jnp.bfloat16))
    return np.stack(orders), np.stack(extras)


def paired_rows(rows, eye, slabs, steps):
    own = lax.axis_index("vol")
    dirs, slab, _, grid = rows.shape
    first = [(0, slabs // 2)] + [(i, i - 1) for i in range(1, slabs // 2 + 1)]
    other = lax.ppermute(rows[:, 0], "vol", first).reshape(2 * dirs, grid)
    kind = jnp.where(own < slabs // 2, 0, jnp.where(own == slabs // 2, 1, 2))
    order, extra = (lax.dynamic_index_in_dim(jnp.asarray(t), kind, 0, keepdims=False) for t in row_orders(slab))
    kept, sent = arrange_call(rows, other, eye, order, extra, steps)
    arrived = lax.ppermute(sent, "vol", [(i, slabs - 1 - i) for i in range(slabs)])
    return kept, arrived


def shards(images, projections, assignment, interp_cells, interp_weights):
    class_count = lax.axis_size("cls")
    slab_count = lax.axis_size("vol")
    local_count, grid = images.shape[0], images.shape[1]
    dirs = projections.shape[1]
    slab = grid // slab_count
    width = 2 * slab
    halves = LANES // width
    capacity = 2 * local_count // class_count
    steps = 16 // capacity
    groups = grid // (halves * steps)

    eye = jnp.asarray(np.eye(grid), BF16)
    order = jnp.asarray(lane_order(grid, slab_count))
    outgoing = route_call(images, assignment, eye, order, class_count, slab_count, width, capacity)
    outgoing, projections = lax.optimization_barrier((outgoing, projections))
    arrived = lax.all_to_all(outgoing, ("cls", "vol"), split_axis=0, concat_axis=0, tiled=True)

    kept, joined = paired_rows(projections[0], eye, slab_count, steps)
    corner_y = (interp_cells[:, 0:1, :] & (grid - 1)).astype(F32)
    weights = jnp.concatenate([interp_weights, corner_y, jnp.zeros((dirs, 3, grid), F32)], axis=1)
    weights = weights.reshape(dirs, 8, halves, groups, steps)
    weights = jnp.transpose(weights, (3, 4, 0, 2, 1)).reshape(groups, steps * dirs, 8 * halves)
    weights = jnp.pad(weights, ((0, 0), (0, 0), (0, LANES - 8 * halves)))
    plan = sorted_points(interp_cells, grid)
    table_y, table_x, table_z, restore = tables(grid, slab_count)

    arrived, kept, joined, weights, plan = lax.optimization_barrier((arrived, kept, joined, weights, plan))
    partial_value = scores_call(arrived, kept, joined, capacity, dirs, slab, slab_count)
    parts = lax.all_to_all(partial_value, "vol", split_axis=0, concat_axis=0, tiled=True)
    own = lax.axis_index("vol")
    single = (own == slab_count // 2).astype(jnp.int32).reshape(1)
    flip = (own >= slab_count // 2).astype(jnp.int32).reshape(1)
    sent, plane = scatter_call(
        single, plan, parts, arrived, weights, table_y, table_x, capacity, width, grid, slab_count
    )
    received = [lax.all_to_all(sent, "vol", split_axis=0, concat_axis=0, tiled=True)]
    if plane is not None:
        sent = planes_call(plane, table_y, table_x, slab_count, grid)
        received.append(lax.all_to_all(sent, "vol", split_axis=0, concat_axis=0, tiled=True))
    volume = None
    for data, table in zip(received, table_z):
        volume = volume_call(flip, data, restore, table, volume)
    return volume[None]


def solution(mesh):
    in_specs = (
        P(("cls", "vol"), None, None, None),
        P("cls", None, "vol", None, None),
        P(("cls", "vol"), None),
        P(),
        P(),
    )
    out_specs = P("cls", "vol", None, None)
    return jax.shard_map(shards, mesh=mesh, in_specs=in_specs, out_specs=out_specs, check_vma=False)
```

```python
import functools
import math

import jax
import jax.numpy as jnp
import numpy as np
from jax import lax
from jax.experimental import pallas as pl
from jax.experimental.pallas import tpu as pltpu
from jax.sharding import PartitionSpec as P

F32 = jnp.float32
BF16 = jnp.bfloat16
LANES = 128
HALF = 64
CHUNK = 128
PAD = 8
UNROLL = 16
STEP = 16
VMEM = pltpu.VMEM


def split_table(table):
    high = table.astype(jnp.bfloat16)
    low = (table - high.astype(np.float64)).astype(jnp.bfloat16)
    return high, low


def plane_pairs(grid, slabs):
    slab = grid // slabs
    half = slab // 2
    pairs = []
    for w in range(slabs):
        for i in range(half):
            if w < slabs // 2:
                first = slab * w + 1 + i
            else:
                first = slab * w + half - 1 - i
            if 2 * first == grid:
                pairs.append((0, first))
            else:
                pairs.append((first, grid - first))
    return np.array(pairs).reshape(slabs, half, 2)


def tables(grid, slabs):
    half = grid // 2
    scale = 1.0 / math.sqrt(grid)
    index = np.arange(grid)
    angle = 2.0 * np.pi / grid
    phase = (index[:, None] * np.arange(half)[None, :]) % grid
    cosine = np.cos(phase * angle)
    sine = np.sin(phase * angle)
    sine[:, 0] = np.cos(((index * half) % grid) * angle)
    table_y = np.concatenate([cosine, sine], axis=1) * scale
    rows = half + 8
    phase = (np.arange(rows)[:, None] * index[None, :]) % grid
    live = (np.arange(rows) <= half)[:, None]
    table_x = np.concatenate([np.cos(phase * angle) * live, np.sin(phase * angle) * live], axis=0) * scale
    pairs = plane_pairs(grid, slabs).reshape(-1, 2)
    single = (2 * pairs[:, 1] == grid)[:, None]
    z = np.where(single[:, 0], pairs[:, 1], pairs[:, 0])
    phase = (z[:, None] * index[None, :]) % grid
    for_sum = np.where(single, 1.0, np.cos(phase * angle))
    for_difference = np.where(single, np.cos(phase * angle), -np.sin(phase * angle))
    table_z = np.stack([for_sum, for_difference], axis=1).reshape(grid, grid) * scale
    order = np.concatenate([np.arange(half), [half], np.arange(grid - 1, half, -1)])
    restore = (order[None, :] == index[:, None]).astype(jnp.bfloat16)
    parts = max(1, grid // slabs // STEP)
    table_z = table_z.reshape(slabs, parts, -1, grid).transpose(1, 0, 2, 3).reshape(grid, grid)
    high, low = split_table(table_y)
    table_y = np.concatenate([high, high, low], axis=0)
    high, low = split_table(table_x)
    table_x = np.concatenate([high, high, low], axis=1)
    table_z = np.concatenate(split_table(table_z), axis=0)
    return table_y, table_x, table_z, restore


def lane_order(grid, slabs):
    rows = plane_pairs(grid, slabs).transpose(0, 2, 1).reshape(-1)
    source = (2 * rows[:, None] + np.arange(2)[None, :]).reshape(-1)
    return (np.arange(2 * grid)[:, None] == source[None, :]).astype(jnp.bfloat16)


def dot(a, b):
    return jnp.dot(a, b, preferred_element_type=F32)


def dot_t(a, b):
    return lax.dot_general(a, b, (((1,), (1,)), ((), ())), preferred_element_type=F32)


def two_terms(value):
    high = value.astype(BF16)
    low = (value - high.astype(F32)).astype(BF16)
    return high, low


def route_kernel(cap, slabs, width, classes_ref, images_ref, eye_ref, order_ref, out_ref, lines):
    count, _, _, grid = images_ref.shape
    halves = LANES // width
    piece = grid // halves
    lane = lax.broadcasted_iota(jnp.int32, (piece, LANES), 1)
    lines[...] = jnp.zeros_like(lines)

    def place(p, carry):
        own = classes_ref[p, 0]
        rank = 0
        for q in range(count):
            rank = rank + jnp.where((classes_ref[q, 0] == own) & (q < p), 1, 0)
        image = images_ref[p].reshape(-1, grid)
        turned = dot(dot_t(eye_ref[...], image).astype(BF16), order_ref[...])
        for w in range(slabs):
            tile = w * width // LANES * LANES
            block = jnp.zeros((piece, LANES), F32)
            for h in range(halves):
                part = turned[h * piece : (h + 1) * piece, tile : tile + LANES]
                shift = (h * width - (w * width - tile)) % LANES
                part = part if shift == 0 else pltpu.roll(part, shift, 1)
                block = jnp.where((lane >= h * width) & (lane < (h + 1) * width), part, block)
            lines[own * slabs + w, pl.ds(rank, piece, stride=cap), :] = block
        return carry

    lax.fori_loop(0, count, place, 0, unroll=2)
    out_ref[...] = lines[...].astype(BF16).reshape(out_ref.shape)


def route_call(images, assignment, eye, order, class_count, slabs, width, cap):
    count, grid = images.shape[0], images.shape[1]
    rows = grid // (LANES // width) * cap
    vmem = pl.BlockSpec(memory_space=VMEM)
    return pl.pallas_call(
        functools.partial(route_kernel, cap, slabs, width),
        out_shape=jax.ShapeDtypeStruct((class_count * slabs, rows // 16, 16, LANES), BF16),
        in_specs=[pl.BlockSpec(memory_space=pltpu.SMEM)] + [vmem] * 3,
        out_specs=vmem,
        scratch_shapes=[VMEM((class_count * slabs, rows, LANES), F32)],
        compiler_params=pltpu.CompilerParams(vmem_limit_bytes=48 * 2**20),
        name="route",
    )(assignment, images, eye, order)


def score_kernel(cap, dirs, unit, first_ref, second_ref, kept_ref, joined_ref, out_ref, sums):
    sources, groups, rows16, _ = first_ref.shape
    rows = sources * rows16
    steps = rows16 // cap
    lane = lax.broadcasted_iota(jnp.int32, (steps * dirs, LANES), 1)
    even = (lane & unit) == 0

    @pl.when(pl.program_id(0) == 0)
    def _():
        sums[...] = jnp.zeros_like(sums)

    for g in range(groups):
        kept = kept_ref[g].astype(F32)
        joined = joined_ref[g].astype(F32)
        refs = [
            jnp.where(even, kept, pltpu.roll(joined, unit, 1)).astype(BF16),
            jnp.where(even, pltpu.roll(kept, LANES - unit, 1), joined).astype(BF16),
        ]
        blocks = [ref[:, g].reshape(rows, LANES) for ref in (first_ref, second_ref)]
        sums[...] += dot_t(jnp.concatenate(refs, axis=1), jnp.concatenate(blocks, axis=1))

    @pl.when(pl.program_id(0) == pl.num_programs(0) - 1)
    def _():
        column = lax.broadcasted_iota(jnp.int32, (dirs, rows), 1)
        part = (column & (rows16 - 1)) // cap
        kept = jnp.zeros((dirs, rows), F32)
        for j in range(steps):
            kept = kept + jnp.where(part == j, sums[j * dirs : (j + 1) * dirs, :], 0.0)
        slots = sources * cap
        row_id = lax.broadcasted_iota(jnp.int32, (rows, slots), 0)
        slot_id = lax.broadcasted_iota(jnp.int32, (rows, slots), 1)
        gather = (row_id // rows16 * cap + row_id % cap) == slot_id
        value = jnp.dot(
            kept, gather.astype(F32), preferred_element_type=F32, precision=lax.Precision.HIGHEST
        )
        for copy in range(out_ref.shape[0]):
            out_ref[copy] = value


def scores_call(images, kept, joined, cap, dirs, unit, slabs):
    sources, groups, rows16, _ = images.shape
    joint = kept.shape[1]
    span = min(4, groups // 2)
    turns = groups // 2 // span
    return pl.pallas_call(
        functools.partial(score_kernel, cap, dirs, unit),
        grid=(turns,),
        out_shape=jax.ShapeDtypeStruct((slabs, dirs, sources * cap), F32),
        in_specs=[
            pl.BlockSpec((sources, span, rows16, LANES), lambda i: (0, i, 0, 0)),
            pl.BlockSpec((sources, span, rows16, LANES), lambda i: (0, i + turns, 0, 0)),
            pl.BlockSpec((span, joint, LANES), lambda i: (i, 0, 0)),
            pl.BlockSpec((span, joint, LANES), lambda i: (i, 0, 0)),
        ],
        out_specs=pl.BlockSpec((slabs, dirs, sources * cap), lambda i: (0, 0, 0)),
        scratch_shapes=[VMEM((joint, sources * rows16), F32)],
        compiler_params=pltpu.CompilerParams(vmem_limit_bytes=48 * 2**20),
        name="scores",
    )(images, images, kept, joined)


def scatter_kernel(
    cap,
    width,
    grid,
    slabs,
    single_ref,
    first_ref,
    point_ref,
    parts_ref,
    images_hbm,
    weights_hbm,
    y_ref,
    x_ref,
    sent_ref,
    *refs,
):
    rest = width > STEP * 2
    rest_hbm = refs[0] if rest else None
    plane, values, sums, spread, lines, images_ref, weights_ref, image_sem, weight_sem, rest_sem, *buffers = refs[rest:]
    sources, groups, rows16, _ = images_ref.shape
    pieces = weight_sem.shape[0]
    images_copy = pltpu.make_async_copy(images_hbm, images_ref, image_sem)
    images_copy.start()
    weight_copies = []
    for i in range(pieces):
        part = pl.ds(i * (groups // pieces), groups // pieces)
        weight_copies.append(pltpu.make_async_copy(weights_hbm.at[part], weights_ref.at[part], weight_sem.at[i]))
        weight_copies[i].start()
    rows = sources * rows16
    steps = rows16 // cap
    dirs, slots = parts_ref.shape[1:]
    joined = steps * dirs
    halves = LANES // width

    total = parts_ref[0]
    for i in range(1, parts_ref.shape[0]):
        total = total + parts_ref[i]
    expo = jnp.exp(total - jnp.max(total, axis=0, keepdims=True))
    posterior = (expo / jnp.sum(expo, axis=0, keepdims=True)).astype(BF16)
    slot_id = lax.broadcasted_iota(jnp.int32, (slots, rows), 0)
    row_id = lax.broadcasted_iota(jnp.int32, (slots, rows), 1)
    repeat = ((row_id // rows16 * cap + row_id % cap) == slot_id).astype(F32).astype(BF16)
    wide = dot(posterior, repeat)
    part = (lax.broadcasted_iota(jnp.int32, (dirs, rows), 1) & (rows16 - 1)) // cap
    for j in range(steps):
        spread[j * dirs : (j + 1) * dirs, :] = jnp.where(part == j, wide, 0.0).astype(BF16)

    lane_j = lax.broadcasted_iota(jnp.int32, (joined, LANES), 1)

    def average(m, carry):
        blocks = [images_ref[:, pl.ds(2 * m + i, 1), :, :].reshape(rows, LANES) for i in range(2)]
        means = dot(spread[...], jnp.concatenate(blocks, axis=1))
        for i in range(2):
            g = 2 * m + i
            mean = means[:, i * LANES : (i + 1) * LANES]
            weight = weights_ref[g]
            for h in range(halves):
                shifted = mean if h == 0 else pltpu.roll(mean, LANES - h * width, 1)
                behind = pltpu.roll(weight, HALF - 8 * h, 1)
                start = pl.multiple_of((h * groups + g) * joined, joined)
                values[pl.ds(start, joined), :] = jnp.where(lane_j < HALF, shifted, behind)
        return carry

    images_copy.wait()
    for i in range(pieces):
        weight_copies[i].wait()
        begin = groups // pieces // 2
        lax.fori_loop(i * begin, (i + 1) * begin, average, 0)

    for buffer in buffers:
        buffer[...] = jnp.zeros_like(buffer)
    sums[...] = jnp.zeros_like(sums)

    place = lax.broadcasted_iota(jnp.int32, (CHUNK, LANES), 0)
    lane = lax.broadcasted_iota(jnp.int32, (CHUNK, grid), 1)
    at_y = lane.astype(F32).astype(BF16)
    at_next = ((lane + (grid - 1)) & (grid - 1)).astype(F32).astype(BF16)
    line_8 = lax.broadcasted_iota(jnp.int32, (8, LANES), 0)
    one = jnp.ones((CHUNK, grid), BF16)
    none = jnp.zeros((CHUNK, grid), BF16)

    lane_1 = lax.broadcasted_iota(jnp.int32, (1, CHUNK), 1)
    points = values.shape[0]

    def fetch(start, buffer):
        for i in range(0, CHUNK, 8):
            block = jnp.broadcast_to(values[pl.ds(point_ref[start + i], 1), :], (8, LANES))
            for j in range(1, 8):
                line = jnp.broadcast_to(values[pl.ds(point_ref[start + i + j], 1), :], (8, LANES))
                block = jnp.where(line_8 == j, line, block)
            buffer[i : i + 8, :] = block

    def put(row, value):
        x = (row + (grid - 1)) & (grid - 1)
        for side in range(grid // LANES):
            plane[side, x, :width, :] = value[:, side * LANES : (side + 1) * LANES]

    def combined(mean):
        a, b = mean[: width // 2], mean[width // 2 :]
        total, gap = a + b, a - b
        tile = width // 2 - 8
        special = (single_ref[0] == 1) & (line_8 >= 6)
        moved = jnp.where(line_8 == 6, -pltpu.roll(b[tile:], 7, 0), pltpu.roll(b[tile:], 1, 0))
        total = [total[:tile], jnp.where(special, a[tile:], total[tile:])]
        gap = [gap[:tile], jnp.where(special, moved, gap[tile:])]
        return jnp.concatenate([part for part in total + gap if part.shape[0]], axis=0)

    def following(start, row):
        second, third = first_ref[row + 1], first_ref[row + 2]
        end = jnp.minimum(start + CHUNK, third)
        moved = row + jnp.where(end >= second, 1, 0) + jnp.where(end >= third, 1, 0)
        return end, jnp.minimum(moved, grid - 1), end - start, jnp.clip(second - start, 0, end - start)

    def work(row, before, size, size_0, buffer):
        data = buffer[...]
        y = jnp.broadcast_to(data[:, HALF + 4 : HALF + 5], (CHUNK, LANES))
        y = jnp.where(place < size, y, -1.0).astype(BF16)
        y = jnp.concatenate([y] * (grid // LANES), axis=1)
        hot = jnp.concatenate([jnp.where(at_y == y, one, none), jnp.where(at_next == y, one, none)], axis=0)
        turned = data.T
        mean = combined(turned[:width])
        weight = [turned[HALF + j : HALF + j + 1] for j in range(4)]
        here = [jnp.where(lane_1 < size_0, w, 0.0) for w in weight]
        there = [w - h for w, h in zip(weight, here)]
        by_row = (
            (here[0], here[2]),
            (here[1] + there[0], here[3] + there[2]),
            (there[1], there[3]),
        )
        operand = jnp.concatenate(
            [
                jnp.concatenate([mean * jnp.broadcast_to(w, (width, CHUNK)) for w in pair], axis=1)
                for pair in by_row
            ],
            axis=0,
        )
        result = dot(operand.astype(BF16), hot)
        old = [sums[i * width : (i + 1) * width] for i in range(3)]
        put(jnp.minimum(before + 1, grid - 1), old[1])
        put(before, old[0])
        stay, by_one = row == before, row == before + 1
        kept = (
            jnp.where(stay, old[0], jnp.where(by_one, old[1], old[2])),
            jnp.where(stay, old[1], jnp.where(by_one, old[2], 0.0)),
            jnp.where(stay, old[2], 0.0),
        )
        for i in range(3):
            sums[i * width : (i + 1) * width] = result[i * width : (i + 1) * width] + kept[i]

    fetch(0, buffers[0])

    def several(state):
        start, row, before = state
        for i in range(UNROLL):
            end, moved, size, size_0 = following(start, row)
            fetch(end, buffers[(i + 1) % UNROLL])
            work(row, before, size, size_0, buffers[i])
            start, row, before = end, moved, row
        return start, row, before

    zero = jnp.int32(0)
    lax.while_loop(lambda state: (state[0] < points) | (state[2] < grid - 1), several, (zero, zero, zero))
    put(grid - 1, sums[:width])
    for side in range(grid // LANES):
        cut = slice(side * LANES, (side + 1) * LANES)
        plane[side, grid - 1, :width, :] = plane[side, grid - 1, :width, :] + sums[width : 2 * width, cut]

    step = min(STEP, width // 2)
    copies = []
    if rest:
        for part in range(grid // LANES):
            for side in range(2):
                source = plane.at[part, :, pl.ds(side * (width // 2) + step, width // 2 - step)]
                copies.append(pltpu.make_async_copy(source, rest_hbm.at[part, side], rest_sem.at[2 * part + side]))
                copies[-1].start()

    pitch = width + PAD
    flat = plane.reshape(grid // LANES, grid * pitch, LANES)

    def load(part, side, value):
        return flat[part, pl.ds(side * (width // 2) + value, grid, stride=pitch), :]

    transform_pairs(slabs, grid, step // 2, load, y_ref, x_ref, sent_ref, lines)
    for copy in copies:
        copy.wait()


def scatter_call(single, plan, parts, images, weights, table_y, table_x, cap, width, grid, slabs):
    sources, groups, rows16, _ = images.shape
    dirs = parts.shape[1]
    points = dirs * grid
    smem = pl.BlockSpec(memory_space=pltpu.SMEM)
    vmem = pl.BlockSpec(memory_space=VMEM)
    hbm = pl.BlockSpec(memory_space=pl.ANY)
    step = min(STEP, width // 2)
    other = width // 2 - step
    sides = grid // LANES
    pieces = 4
    shapes = [jax.ShapeDtypeStruct((slabs, grid // slabs, step, grid), BF16)]
    if other:
        shapes.append(jax.ShapeDtypeStruct((sides, 2, grid, other, LANES), F32))
    result = pl.pallas_call(
        functools.partial(scatter_kernel, cap, width, grid, slabs),
        out_shape=shapes,
        in_specs=[smem] * 3 + [vmem, hbm, hbm, vmem, vmem],
        out_specs=[vmem, hbm][: len(shapes)],
        scratch_shapes=[
            VMEM((sides, grid, width + PAD, LANES), F32),
            VMEM((points, LANES), F32),
            VMEM((3 * width, grid), F32),
            VMEM((weights.shape[1], sources * rows16), BF16),
            VMEM((sides, grid * step, LANES), F32),
            VMEM(images.shape, BF16),
            VMEM(weights.shape, F32),
            pltpu.SemaphoreType.DMA,
            pltpu.SemaphoreType.DMA((pieces,)),
            pltpu.SemaphoreType.DMA((2 * sides,)),
        ]
        + [VMEM((CHUNK, LANES), F32)] * UNROLL,
        compiler_params=pltpu.CompilerParams(vmem_limit_bytes=61 * 2**20),
        name="scatter",
    )(single, *plan, parts, images, weights, table_y, table_x)
    if not other:
        return result[0], None
    return result[0], result[1].reshape(sides, 2, grid * other, LANES)


def transform_pairs(slabs, grid, pairs, load, y_ref, x_ref, out_ref, lines):
    half = grid // 2
    rows = half + 8
    slab = grid // slabs
    count = 2 * pairs
    lane = lax.broadcasted_iota(jnp.int32, (grid, half), 1)

    def transformed(real, imag):
        cos_r, sin_r = real[:, :half], real[:, half:]
        cos_i, sin_i = imag[:, :half], imag[:, half:]
        zero_r = jnp.where(lane == 0, 0.0, sin_r)
        zero_i = jnp.where(lane == 0, 0.0, sin_i)
        real = jnp.concatenate([cos_r - zero_i, jnp.where(lane == 0, sin_r, cos_r + sin_i)], axis=1)
        imag = jnp.concatenate([cos_i + zero_r, jnp.where(lane == 0, sin_i, cos_i - sin_r)], axis=1)
        return real, imag

    def along_x(table, operand):
        high, low = two_terms(operand)
        return dot(x_ref[table * rows : (table + 1) * rows], jnp.concatenate([high, low, high], axis=0))

    def one(i, carry):
        planes = [
            jnp.concatenate([load(part, side, 2 * i + r) for part in range(grid // LANES)], axis=1)
            for side in range(2)
            for r in range(2)
        ]
        both = []
        for value in planes:
            high, low = two_terms(value)
            both.append(dot(jnp.concatenate([high, low, high], axis=1), y_ref[...]))
        sum_r, sum_i = transformed(both[0], both[1])
        dif_r, dif_i = transformed(both[2], both[3])
        cosine = along_x(0, jnp.concatenate([sum_r, dif_i], axis=1))
        sine = along_x(1, jnp.concatenate([sum_i, dif_r], axis=1))
        fields = (
            (cosine[:, :grid] - sine[:, :grid], cosine[:, :grid] + sine[:, :grid]),
            (cosine[:, grid:] + sine[:, grid:], cosine[:, grid:] - sine[:, grid:]),
        )
        for c in range(2):
            plus, minus = fields[c]
            for part in range(grid // LANES):
                cut = slice(part * LANES, (part + 1) * LANES)
                place = 2 * i + c
                lines[part, pl.ds(place, half, stride=count), :] = plus[:half, cut]
                lines[part, pl.ds(half * count + place, half, stride=count), :] = minus[1 : half + 1, cut]
        return carry

    lax.fori_loop(0, pairs, one, 0, unroll=2)
    for d in range(slabs):
        if d < slabs // 2:
            start = slab * d
        else:
            start = half + grid - slab * d - slab
        size = slab * count
        for part in range(grid // LANES):
            block = lines[part, start * count : start * count + size, :]
            out_ref[d, :, :, part * LANES : (part + 1) * LANES] = block.astype(BF16).reshape(slab, count, LANES)


def plane_kernel(slabs, grid, data_ref, y_ref, x_ref, out_ref, lines):
    pitch = data_ref.shape[2] // grid
    pairs = pitch // 2

    def load(part, side, value):
        return data_ref[part, side, pl.ds(value, grid, stride=pitch), :]

    transform_pairs(slabs, grid, pairs, load, y_ref, x_ref, out_ref, lines)


def planes_call(data, table_y, table_x, slabs, grid):
    step = data.shape[2] // grid
    slab = grid // slabs
    vmem = pl.BlockSpec(memory_space=VMEM)
    return pl.pallas_call(
        functools.partial(plane_kernel, slabs, grid),
        in_specs=[vmem] * 3,
        out_specs=vmem,
        scratch_shapes=[VMEM((data.shape[0], grid * step, LANES), F32)],
        out_shape=jax.ShapeDtypeStruct((slabs, slab, step, grid), BF16),
        compiler_params=pltpu.CompilerParams(vmem_limit_bytes=56 * 2**20),
        name="planes",
    )(data, table_y, table_x)


def volume_kernel(flip_ref, restore_ref, z_ref, *refs):
    out_ref = refs[-1]
    slabs, span, width, grid = refs[0].shape
    turned = []
    for i in range(span):
        block = jnp.concatenate([ref[:, i].reshape(slabs * width, grid) for ref in refs[:-1]], axis=0)
        turned.append(dot_t(restore_ref[...], block).astype(BF16))
    turned = jnp.concatenate(turned, axis=0)
    value = dot(jnp.concatenate([turned, turned], axis=1), z_ref[...])
    for i in range(span):
        out_ref[jnp.where(flip_ref[0] == 1, span - 1 - i, i)] = value[i * grid : (i + 1) * grid]


def volume_call(flip, parts, restore, table_z):
    slabs, slab, width, grid = parts[0].shape
    span = 4
    steps = slab // span
    fixed = lambda i, flip_ref: (0, 0)
    return pl.pallas_call(
        volume_kernel,
        grid_spec=pltpu.PrefetchScalarGridSpec(
            num_scalar_prefetch=1,
            grid=(steps,),
            in_specs=[pl.BlockSpec(restore.shape, fixed), pl.BlockSpec(table_z.shape, fixed)]
            + [pl.BlockSpec((slabs, span, width, grid), lambda i, flip_ref: (0, i, 0, 0))] * len(parts),
            out_specs=pl.BlockSpec(
                (span, grid, grid), lambda i, flip_ref: (jnp.where(flip_ref[0] == 1, steps - 1 - i, i), 0, 0)
            ),
        ),
        out_shape=jax.ShapeDtypeStruct((slab, grid, grid), F32),
        compiler_params=pltpu.CompilerParams(vmem_limit_bytes=48 * 2**20),
        name="volume",
    )(flip, restore, table_z, *parts)


def sorted_points(interp_cells, grid):
    dirs = interp_cells.shape[0]
    points = dirs * grid
    base = interp_cells[:, 0, :].T.reshape(-1)
    row = (base // grid + 1) & (grid - 1)
    key = row * points + jnp.arange(points, dtype=jnp.int32)
    key = lax.sort(key, is_stable=False)
    rows = jnp.arange(grid + 3, dtype=jnp.int32)
    first = jnp.sum((row[None, :] < rows[:, None]).astype(jnp.int32), axis=1)
    point = jnp.concatenate([key & (points - 1), jnp.zeros((CHUNK,), jnp.int32)])
    return first, point


def arrange_kernel(rows_ref, other_ref, eye_ref, order_ref, extra_ref, kept_ref, sent_ref, *lines):
    dirs, count, _, grid = rows_ref.shape
    blocks = LANES // count
    length = grid // blocks
    span = extra_ref.shape[0]
    each = span * blocks
    number = lax.broadcasted_iota(jnp.int32, (length, LANES), 1) // count

    def step(m, carry):
        other = other_ref[pl.ds(pl.multiple_of(2 * each * m, 2 * each), 2 * each), :]
        other = dot_t(eye_ref[...], other).astype(BF16)
        for group in range(span):
            k = each * m + blocks * group
            block = rows_ref[pl.ds(k, blocks)].reshape(2 * LANES, grid)
            turned = dot_t(eye_ref[...], block).astype(BF16)
            turned = dot(turned, order_ref[...]) + dot(other, extra_ref[group])
            for side in range(2):
                tile = [turned[q * length : (q + 1) * length, side * LANES : (side + 1) * LANES] for q in range(blocks)]
                bit = 1
                while bit < blocks:
                    low = (number & bit) == 0
                    swapped = list(tile)
                    for q in range(blocks):
                        if q & bit == 0:
                            swapped[q] = jnp.where(low, tile[q], pltpu.roll(tile[q + bit], bit * count, 1))
                            swapped[q + bit] = jnp.where(low, pltpu.roll(tile[q], LANES - bit * count, 1), tile[q + bit])
                    tile = swapped
                    bit *= 2
                for i in range(blocks):
                    lines[side][pl.ds(k + i, length, stride=dirs + PAD), :] = tile[i]
        return carry

    lax.fori_loop(0, dirs // each, step, 0)
    for side, out_ref in enumerate((kept_ref, sent_ref)):
        steps = out_ref.shape[1] // dirs
        for u in range(length):
            block = lines[side][u * (dirs + PAD) : u * (dirs + PAD) + dirs, :].astype(BF16)
            out_ref[u // steps, u % steps * dirs : (u % steps + 1) * dirs, :] = block


def arrange_call(rows, other, eye, order, extra, steps):
    dirs, count, _, grid = rows.shape
    length = grid // (LANES // count)
    vmem = pl.BlockSpec(memory_space=VMEM)
    shape = jax.ShapeDtypeStruct((length // steps, steps * dirs, LANES), BF16)
    return pl.pallas_call(
        arrange_kernel,
        out_shape=(shape, shape),
        in_specs=[vmem] * 5,
        out_specs=(vmem, vmem),
        scratch_shapes=[VMEM((length * (dirs + PAD), LANES), F32)] * 2,
        compiler_params=pltpu.CompilerParams(vmem_limit_bytes=48 * 2**20),
        name="arrange",
    )(rows, other, eye, order, extra)


def row_orders(slab):
    half = slab // 2
    blocks = LANES // slab
    span = max(1, 8 // blocks)
    down = list(range(half - 1, -1, -1))
    upper = list(range(slab - 1, half - 1, -1))
    orders, extras = [], []
    for kept, sent in (
        (list(range(1, half + 1)), list(range(half + 1, slab)) + [None]),
        (down[:-1] + [None], upper),
        (down, upper),
    ):
        order = np.zeros((2 * LANES, 2 * LANES))
        extra = np.zeros((span, 2 * span * blocks, 2 * LANES))
        for side, rows in enumerate((kept, sent)):
            for k in range(blocks):
                for i, row in enumerate(rows):
                    for r in range(2):
                        lane = side * LANES + k * slab + 2 * i + r
                        if row is not None:
                            order[(k * slab + row) * 2 + r, lane] = 1.0
                        else:
                            for group in range(span):
                                extra[group, (group * blocks + k) * 2 + r, lane] = 1.0
        orders.append(order.astype(jnp.bfloat16))
        extras.append(extra.astype(jnp.bfloat16))
    return np.stack(orders), np.stack(extras)


def paired_rows(rows, eye, slabs, steps):
    own = lax.axis_index("vol")
    dirs, slab, _, grid = rows.shape
    first = [(0, slabs // 2)] + [(i, i - 1) for i in range(1, slabs // 2 + 1)]
    other = lax.ppermute(rows[:, 0], "vol", first).reshape(2 * dirs, grid)
    kind = jnp.where(own < slabs // 2, 0, jnp.where(own == slabs // 2, 1, 2))
    order, extra = (lax.dynamic_index_in_dim(jnp.asarray(t), kind, 0, keepdims=False) for t in row_orders(slab))
    kept, sent = arrange_call(rows, other, eye, order, extra, steps)
    arrived = lax.ppermute(sent, "vol", [(i, slabs - 1 - i) for i in range(slabs)])
    return kept, arrived


def shards(images, projections, assignment, interp_cells, interp_weights):
    class_count = lax.axis_size("cls")
    slab_count = lax.axis_size("vol")
    local_count, grid = images.shape[0], images.shape[1]
    dirs = projections.shape[1]
    slab = grid // slab_count
    width = 2 * slab
    halves = LANES // width
    capacity = 2 * local_count // class_count
    steps = 16 // capacity
    groups = grid // (halves * steps)

    eye = jnp.asarray(np.eye(grid), BF16)
    order = jnp.asarray(lane_order(grid, slab_count))
    outgoing = route_call(images, assignment, eye, order, class_count, slab_count, width, capacity)
    outgoing, projections = lax.optimization_barrier((outgoing, projections))
    arrived = lax.all_to_all(outgoing, ("cls", "vol"), split_axis=0, concat_axis=0, tiled=True)

    kept, joined = paired_rows(projections[0], eye, slab_count, steps)
    corner_y = (interp_cells[:, 0:1, :] & (grid - 1)).astype(F32)
    weights = jnp.concatenate([interp_weights, corner_y, jnp.zeros((dirs, 3, grid), F32)], axis=1)
    weights = weights.reshape(dirs, 8, halves, groups, steps)
    weights = jnp.transpose(weights, (3, 4, 0, 2, 1)).reshape(groups, steps * dirs, 8 * halves)
    weights = jnp.pad(weights, ((0, 0), (0, 0), (0, LANES - 8 * halves)))
    plan = sorted_points(interp_cells, grid)
    table_y, table_x, table_z, restore = tables(grid, slab_count)

    arrived, kept, joined, weights, plan = lax.optimization_barrier((arrived, kept, joined, weights, plan))
    partial_value = scores_call(arrived, kept, joined, capacity, dirs, slab, slab_count)
    parts = lax.all_to_all(partial_value, "vol", split_axis=0, concat_axis=0, tiled=True)
    own = lax.axis_index("vol")
    single = (own == slab_count // 2).astype(jnp.int32).reshape(1)
    flip = (own >= slab_count // 2).astype(jnp.int32).reshape(1)
    sent, plane = scatter_call(
        single, plan, parts, arrived, weights, table_y, table_x, capacity, width, grid, slab_count
    )
    received = [lax.all_to_all(sent, "vol", split_axis=0, concat_axis=0, tiled=True)]
    if plane is not None:
        sent = planes_call(plane, table_y, table_x, slab_count, grid)
        received.append(lax.all_to_all(sent, "vol", split_axis=0, concat_axis=0, tiled=True))
    return volume_call(flip, received, restore, table_z)[None]


def solution(mesh):
    in_specs = (
        P(("cls", "vol"), None, None, None),
        P("cls", None, "vol", None, None),
        P(("cls", "vol"), None),
        P(),
        P(),
    )
    out_specs = P("cls", "vol", None, None)
    return jax.shard_map(shards, mesh=mesh, in_specs=in_specs, out_specs=out_specs, check_vma=False)
```

```python
import functools
import math

import jax
import jax.numpy as jnp
import numpy as np
from jax import lax
from jax.experimental import pallas as pl
from jax.experimental.pallas import tpu as pltpu
from jax.sharding import PartitionSpec as P

F32 = jnp.float32
BF16 = jnp.bfloat16
LANES = 128
HALF = 64
CHUNK = 128
PAD = 8
UNROLL = 16
STEP = 16
VMEM = pltpu.VMEM


def split_table(table):
    high = table.astype(jnp.bfloat16)
    low = (table - high.astype(np.float64)).astype(jnp.bfloat16)
    return high, low


def plane_pairs(grid, slabs):
    slab = grid // slabs
    half = slab // 2
    pairs = []
    for w in range(slabs):
        for i in range(half):
            if w < slabs // 2:
                first = slab * w + 1 + i
            else:
                first = slab * w + half - 1 - i
            if 2 * first == grid:
                pairs.append((0, first))
            else:
                pairs.append((first, grid - first))
    return np.array(pairs).reshape(slabs, half, 2)


def tables(grid, slabs):
    half = grid // 2
    scale = 1.0 / math.sqrt(grid)
    index = np.arange(grid)
    angle = 2.0 * np.pi / grid
    phase = (index[:, None] * np.arange(half)[None, :]) % grid
    cosine = np.cos(phase * angle)
    sine = np.sin(phase * angle)
    sine[:, 0] = np.cos(((index * half) % grid) * angle)
    table_y = np.concatenate([cosine, sine], axis=1) * scale
    rows = half + 8
    phase = (np.arange(rows)[:, None] * index[None, :]) % grid
    live = (np.arange(rows) <= half)[:, None]
    table_x = np.concatenate([np.cos(phase * angle) * live, np.sin(phase * angle) * live], axis=0) * scale
    pairs = plane_pairs(grid, slabs).reshape(-1, 2)
    single = (2 * pairs[:, 1] == grid)[:, None]
    z = np.where(single[:, 0], pairs[:, 1], pairs[:, 0])
    phase = (z[:, None] * index[None, :]) % grid
    for_sum = np.where(single, 1.0, np.cos(phase * angle))
    for_difference = np.where(single, np.cos(phase * angle), -np.sin(phase * angle))
    table_z = np.stack([for_sum, for_difference], axis=1).reshape(grid, grid) * scale
    order = np.concatenate([np.arange(half), [half], np.arange(grid - 1, half, -1)])
    restore = (order[None, :] == index[:, None]).astype(jnp.bfloat16)
    parts = max(1, grid // slabs // STEP)
    table_z = table_z.reshape(slabs, parts, -1, grid).transpose(1, 0, 2, 3).reshape(grid, grid)
    high, low = split_table(table_y)
    table_y = np.concatenate([high, high, low], axis=0)
    high, low = split_table(table_x)
    table_x = np.concatenate([high, high, low], axis=1)
    table_z = np.concatenate(split_table(table_z), axis=0)
    return table_y, table_x, table_z, restore


def dot(a, b):
    return jnp.dot(a, b, preferred_element_type=F32)


def dot_t(a, b):
    return lax.dot_general(a, b, (((1,), (1,)), ((), ())), preferred_element_type=F32)


def two_terms(value):
    high = value.astype(BF16)
    low = (value - high.astype(F32)).astype(BF16)
    return high, low


def route_kernel(cap, slabs, width, classes_ref, images_ref, out_ref, lines, eye_ref, order_ref):
    count, _, _, grid = images_ref.shape
    eye = lax.broadcasted_iota(jnp.int32, (grid, grid), 0) == lax.broadcasted_iota(jnp.int32, (grid, grid), 1)
    eye_ref[...] = eye.astype(F32).astype(BF16)
    half = width // 4
    bits = width.bit_length() - 1
    value = lax.broadcasted_iota(jnp.int32, (8, 2 * grid), 1)
    slab, pair = value >> bits, (value >> 1) & (half - 1)
    first = 2 * half * slab + jnp.where(slab < slabs // 2, 1 + pair, half - 1 - pair)
    both = jnp.where(2 * first == grid, 0, first)
    row = jnp.where(value & (2 * half) == 0, both, jnp.where(2 * first == grid, first, grid - first))
    source = (2 * row + (value & 1))[0:1, :]
    order = lax.broadcasted_iota(jnp.int32, (2 * grid, 2 * grid), 0) == source
    order_ref[...] = order.astype(F32).astype(BF16)
    halves = LANES // width
    piece = grid // halves
    lane = lax.broadcasted_iota(jnp.int32, (piece, LANES), 1)
    lines[...] = jnp.zeros_like(lines)

    def place(p, carry):
        own = classes_ref[p, 0]
        rank = 0
        for q in range(count):
            rank = rank + jnp.where((classes_ref[q, 0] == own) & (q < p), 1, 0)
        image = images_ref[p].reshape(-1, grid)
        turned = dot(dot_t(eye_ref[...], image).astype(BF16), order_ref[...])
        for w in range(slabs):
            tile = w * width // LANES * LANES
            block = jnp.zeros((piece, LANES), F32)
            for h in range(halves):
                part = turned[h * piece : (h + 1) * piece, tile : tile + LANES]
                shift = (h * width - (w * width - tile)) % LANES
                part = part if shift == 0 else pltpu.roll(part, shift, 1)
                block = jnp.where((lane >= h * width) & (lane < (h + 1) * width), part, block)
            lines[own * slabs + w, pl.ds(rank, piece, stride=cap), :] = block
        return carry

    lax.fori_loop(0, count, place, 0, unroll=2)
    out_ref[...] = lines[...].astype(BF16).reshape(out_ref.shape)


def route_call(images, assignment, class_count, slabs, width, cap):
    count, grid = images.shape[0], images.shape[1]
    rows = grid // (LANES // width) * cap
    vmem = pl.BlockSpec(memory_space=VMEM)
    return pl.pallas_call(
        functools.partial(route_kernel, cap, slabs, width),
        out_shape=jax.ShapeDtypeStruct((class_count * slabs, rows // 16, 16, LANES), BF16),
        in_specs=[pl.BlockSpec(memory_space=pltpu.SMEM), vmem],
        out_specs=vmem,
        scratch_shapes=[
            VMEM((class_count * slabs, rows, LANES), F32),
            VMEM((grid, grid), BF16),
            VMEM((2 * grid, 2 * grid), BF16),
        ],
        compiler_params=pltpu.CompilerParams(vmem_limit_bytes=48 * 2**20),
        name="route",
    )(assignment, images)


def score_kernel(cap, dirs, unit, first_ref, second_ref, kept_ref, joined_ref, out_ref, sums):
    sources, groups, rows16, _ = first_ref.shape
    rows = sources * rows16
    steps = rows16 // cap
    lane = lax.broadcasted_iota(jnp.int32, (steps * dirs, LANES), 1)
    even = (lane & unit) == 0

    @pl.when(pl.program_id(0) == 0)
    def _():
        sums[...] = jnp.zeros_like(sums)

    for g in range(groups):
        kept = kept_ref[g].astype(F32)
        joined = joined_ref[g].astype(F32)
        refs = [
            jnp.where(even, kept, pltpu.roll(joined, unit, 1)).astype(BF16),
            jnp.where(even, pltpu.roll(kept, LANES - unit, 1), joined).astype(BF16),
        ]
        blocks = [ref[:, g].reshape(rows, LANES) for ref in (first_ref, second_ref)]
        sums[...] += dot_t(jnp.concatenate(refs, axis=1), jnp.concatenate(blocks, axis=1))

    @pl.when(pl.program_id(0) == pl.num_programs(0) - 1)
    def _():
        column = lax.broadcasted_iota(jnp.int32, (dirs, rows), 1)
        part = (column & (rows16 - 1)) // cap
        kept = jnp.zeros((dirs, rows), F32)
        for j in range(steps):
            kept = kept + jnp.where(part == j, sums[j * dirs : (j + 1) * dirs, :], 0.0)
        slots = sources * cap
        row_id = lax.broadcasted_iota(jnp.int32, (rows, slots), 0)
        slot_id = lax.broadcasted_iota(jnp.int32, (rows, slots), 1)
        gather = (row_id // rows16 * cap + row_id % cap) == slot_id
        value = jnp.dot(
            kept, gather.astype(F32), preferred_element_type=F32, precision=lax.Precision.HIGHEST
        )
        for copy in range(out_ref.shape[0]):
            out_ref[copy] = value


def scores_call(images, kept, joined, cap, dirs, unit, slabs):
    sources, groups, rows16, _ = images.shape
    joint = kept.shape[1]
    span = min(4, groups // 2)
    turns = groups // 2 // span
    return pl.pallas_call(
        functools.partial(score_kernel, cap, dirs, unit),
        grid=(turns,),
        out_shape=jax.ShapeDtypeStruct((slabs, dirs, sources * cap), F32),
        in_specs=[
            pl.BlockSpec((sources, span, rows16, LANES), lambda i: (0, i, 0, 0)),
            pl.BlockSpec((sources, span, rows16, LANES), lambda i: (0, i + turns, 0, 0)),
            pl.BlockSpec((span, joint, LANES), lambda i: (i, 0, 0)),
            pl.BlockSpec((span, joint, LANES), lambda i: (i, 0, 0)),
        ],
        out_specs=pl.BlockSpec((slabs, dirs, sources * cap), lambda i: (0, 0, 0)),
        scratch_shapes=[VMEM((joint, sources * rows16), F32)],
        compiler_params=pltpu.CompilerParams(vmem_limit_bytes=48 * 2**20),
        name="scores",
    )(images, images, kept, joined)


def scatter_kernel(
    cap,
    width,
    grid,
    slabs,
    single_ref,
    first_ref,
    point_ref,
    parts_ref,
    images_hbm,
    weights_hbm,
    y_ref,
    x_ref,
    sent_ref,
    *refs,
):
    rest = width > STEP * 2
    rest_hbm = refs[0] if rest else None
    plane, values, sums, spread, lines, images_ref, weights_ref, image_sem, weight_sem, rest_sem, *buffers = refs[rest:]
    sources, groups, rows16, _ = images_ref.shape
    pieces = weight_sem.shape[0]
    images_copy = pltpu.make_async_copy(images_hbm, images_ref, image_sem)
    images_copy.start()
    weight_copies = []
    for i in range(pieces):
        part = pl.ds(i * (groups // pieces), groups // pieces)
        weight_copies.append(pltpu.make_async_copy(weights_hbm.at[part], weights_ref.at[part], weight_sem.at[i]))
        weight_copies[i].start()
    rows = sources * rows16
    steps = rows16 // cap
    dirs, slots = parts_ref.shape[1:]
    joined = steps * dirs
    halves = LANES // width

    total = parts_ref[0]
    for i in range(1, parts_ref.shape[0]):
        total = total + parts_ref[i]
    expo = jnp.exp(total - jnp.max(total, axis=0, keepdims=True))
    posterior = (expo / jnp.sum(expo, axis=0, keepdims=True)).astype(BF16)
    slot_id = lax.broadcasted_iota(jnp.int32, (slots, rows), 0)
    row_id = lax.broadcasted_iota(jnp.int32, (slots, rows), 1)
    repeat = ((row_id // rows16 * cap + row_id % cap) == slot_id).astype(F32).astype(BF16)
    wide = dot(posterior, repeat)
    part = (lax.broadcasted_iota(jnp.int32, (dirs, rows), 1) & (rows16 - 1)) // cap
    for j in range(steps):
        spread[j * dirs : (j + 1) * dirs, :] = jnp.where(part == j, wide, 0.0).astype(BF16)

    lane_j = lax.broadcasted_iota(jnp.int32, (joined, LANES), 1)

    def average(m, carry):
        blocks = [images_ref[:, pl.ds(2 * m + i, 1), :, :].reshape(rows, LANES) for i in range(2)]
        means = dot(spread[...], jnp.concatenate(blocks, axis=1))
        for i in range(2):
            g = 2 * m + i
            mean = means[:, i * LANES : (i + 1) * LANES]
            weight = weights_ref[g]
            for h in range(halves):
                shifted = mean if h == 0 else pltpu.roll(mean, LANES - h * width, 1)
                behind = pltpu.roll(weight, HALF - 8 * h, 1)
                start = pl.multiple_of((h * groups + g) * joined, joined)
                values[pl.ds(start, joined), :] = jnp.where(lane_j < HALF, shifted, behind)
        return carry

    images_copy.wait()
    for i in range(pieces):
        weight_copies[i].wait()
        begin = groups // pieces // 2
        lax.fori_loop(i * begin, (i + 1) * begin, average, 0)

    for buffer in buffers:
        buffer[...] = jnp.zeros_like(buffer)
    sums[...] = jnp.zeros_like(sums)

    place = lax.broadcasted_iota(jnp.int32, (CHUNK, LANES), 0)
    lane = lax.broadcasted_iota(jnp.int32, (CHUNK, grid), 1)
    at_y = lane.astype(F32).astype(BF16)
    at_next = ((lane + (grid - 1)) & (grid - 1)).astype(F32).astype(BF16)
    line_8 = lax.broadcasted_iota(jnp.int32, (8, LANES), 0)
    one = jnp.ones((CHUNK, grid), BF16)
    none = jnp.zeros((CHUNK, grid), BF16)

    lane_1 = lax.broadcasted_iota(jnp.int32, (1, CHUNK), 1)
    points = values.shape[0]

    def fetch(start, buffer):
        for i in range(0, CHUNK, 8):
            block = jnp.broadcast_to(values[pl.ds(point_ref[start + i], 1), :], (8, LANES))
            for j in range(1, 8):
                line = jnp.broadcast_to(values[pl.ds(point_ref[start + i + j], 1), :], (8, LANES))
                block = jnp.where(line_8 == j, line, block)
            buffer[i : i + 8, :] = block

    def put(row, value):
        x = (row + (grid - 1)) & (grid - 1)
        for side in range(grid // LANES):
            plane[side, x, :width, :] = value[:, side * LANES : (side + 1) * LANES]

    def combined(mean):
        a, b = mean[: width // 2], mean[width // 2 :]
        total, gap = a + b, a - b
        tile = width // 2 - 8
        special = (single_ref[0] == 1) & (line_8 >= 6)
        moved = jnp.where(line_8 == 6, -pltpu.roll(b[tile:], 7, 0), pltpu.roll(b[tile:], 1, 0))
        total = [total[:tile], jnp.where(special, a[tile:], total[tile:])]
        gap = [gap[:tile], jnp.where(special, moved, gap[tile:])]
        return jnp.concatenate([part for part in total + gap if part.shape[0]], axis=0)

    def following(start, row):
        second, third = first_ref[row + 1], first_ref[row + 2]
        end = jnp.minimum(start + CHUNK, third)
        moved = row + jnp.where(end >= second, 1, 0) + jnp.where(end >= third, 1, 0)
        return end, jnp.minimum(moved, grid - 1), end - start, jnp.clip(second - start, 0, end - start)

    def work(row, before, size, size_0, buffer):
        data = buffer[...]
        y = jnp.broadcast_to(data[:, HALF + 4 : HALF + 5], (CHUNK, LANES))
        y = jnp.where(place < size, y, -1.0).astype(BF16)
        y = jnp.concatenate([y] * (grid // LANES), axis=1)
        hot = jnp.concatenate([jnp.where(at_y == y, one, none), jnp.where(at_next == y, one, none)], axis=0)
        turned = data.T
        mean = combined(turned[:width])
        weight = [turned[HALF + j : HALF + j + 1] for j in range(4)]
        here = [jnp.where(lane_1 < size_0, w, 0.0) for w in weight]
        there = [w - h for w, h in zip(weight, here)]
        by_row = (
            (here[0], here[2]),
            (here[1] + there[0], here[3] + there[2]),
            (there[1], there[3]),
        )
        operand = jnp.concatenate(
            [
                jnp.concatenate([mean * jnp.broadcast_to(w, (width, CHUNK)) for w in pair], axis=1)
                for pair in by_row
            ],
            axis=0,
        )
        result = dot(operand.astype(BF16), hot)
        old = [sums[i * width : (i + 1) * width] for i in range(3)]
        put(jnp.minimum(before + 1, grid - 1), old[1])
        put(before, old[0])
        stay, by_one = row == before, row == before + 1
        kept = (
            jnp.where(stay, old[0], jnp.where(by_one, old[1], old[2])),
            jnp.where(stay, old[1], jnp.where(by_one, old[2], 0.0)),
            jnp.where(stay, old[2], 0.0),
        )
        for i in range(3):
            sums[i * width : (i + 1) * width] = result[i * width : (i + 1) * width] + kept[i]

    fetch(0, buffers[0])

    def several(state):
        start, row, before = state
        for i in range(UNROLL):
            end, moved, size, size_0 = following(start, row)
            fetch(end, buffers[(i + 1) % UNROLL])
            work(row, before, size, size_0, buffers[i])
            start, row, before = end, moved, row
        return start, row, before

    zero = jnp.int32(0)
    lax.while_loop(lambda state: (state[0] < points) | (state[2] < grid - 1), several, (zero, zero, zero))
    put(grid - 1, sums[:width])
    for side in range(grid // LANES):
        cut = slice(side * LANES, (side + 1) * LANES)
        plane[side, grid - 1, :width, :] = plane[side, grid - 1, :width, :] + sums[width : 2 * width, cut]

    step = min(STEP, width // 2)
    copies = []
    if rest:
        for part in range(grid // LANES):
            for side in range(2):
                source = plane.at[part, :, pl.ds(side * (width // 2) + step, width // 2 - step)]
                copies.append(pltpu.make_async_copy(source, rest_hbm.at[part, side], rest_sem.at[2 * part + side]))
                copies[-1].start()

    pitch = width + PAD
    flat = plane.reshape(grid // LANES, grid * pitch, LANES)

    def load(part, side, value):
        return flat[part, pl.ds(side * (width // 2) + value, grid, stride=pitch), :]

    transform_pairs(slabs, grid, step // 2, load, y_ref, x_ref, sent_ref, lines)
    for copy in copies:
        copy.wait()


def scatter_call(single, plan, parts, images, weights, table_y, table_x, cap, width, grid, slabs):
    sources, groups, rows16, _ = images.shape
    dirs = parts.shape[1]
    points = dirs * grid
    smem = pl.BlockSpec(memory_space=pltpu.SMEM)
    vmem = pl.BlockSpec(memory_space=VMEM)
    hbm = pl.BlockSpec(memory_space=pl.ANY)
    step = min(STEP, width // 2)
    other = width // 2 - step
    sides = grid // LANES
    pieces = 4
    shapes = [jax.ShapeDtypeStruct((slabs, grid // slabs, step, grid), BF16)]
    if other:
        shapes.append(jax.ShapeDtypeStruct((sides, 2, grid, other, LANES), F32))
    result = pl.pallas_call(
        functools.partial(scatter_kernel, cap, width, grid, slabs),
        out_shape=shapes,
        in_specs=[smem] * 3 + [vmem, hbm, hbm, vmem, vmem],
        out_specs=[vmem, hbm][: len(shapes)],
        scratch_shapes=[
            VMEM((sides, grid, width + PAD, LANES), F32),
            VMEM((points, LANES), F32),
            VMEM((3 * width, grid), F32),
            VMEM((weights.shape[1], sources * rows16), BF16),
            VMEM((sides, grid, step + PAD, LANES), F32),
            VMEM(images.shape, BF16),
            VMEM(weights.shape, F32),
            pltpu.SemaphoreType.DMA,
            pltpu.SemaphoreType.DMA((pieces,)),
            pltpu.SemaphoreType.DMA((2 * sides,)),
        ]
        + [VMEM((CHUNK, LANES), F32)] * UNROLL,
        compiler_params=pltpu.CompilerParams(vmem_limit_bytes=61 * 2**20),
        name="scatter",
    )(single, *plan, parts, images, weights, table_y, table_x)
    if not other:
        return result[0], None
    return result[0], result[1].reshape(sides, 2, grid * other, LANES)


def transform_pairs(slabs, grid, pairs, load, y_ref, x_ref, out_ref, lines):
    half = grid // 2
    rows = half + 8
    slab = grid // slabs
    count = 2 * pairs
    pitch = count + PAD
    flat = lines.reshape(grid // LANES, grid * pitch, LANES)
    lane = lax.broadcasted_iota(jnp.int32, (grid, half), 1)

    def transformed(real, imag):
        cos_r, sin_r = real[:, :half], real[:, half:]
        cos_i, sin_i = imag[:, :half], imag[:, half:]
        zero_r = jnp.where(lane == 0, 0.0, sin_r)
        zero_i = jnp.where(lane == 0, 0.0, sin_i)
        real = jnp.concatenate([cos_r - zero_i, jnp.where(lane == 0, sin_r, cos_r + sin_i)], axis=1)
        imag = jnp.concatenate([cos_i + zero_r, jnp.where(lane == 0, sin_i, cos_i - sin_r)], axis=1)
        return real, imag

    def along_x(table, operand):
        high, low = two_terms(operand)
        return dot(x_ref[table * rows : (table + 1) * rows], jnp.concatenate([high, low, high], axis=0))

    def one(i, carry):
        planes = [
            jnp.concatenate([load(part, side, 2 * i + r) for part in range(grid // LANES)], axis=1)
            for side in range(2)
            for r in range(2)
        ]
        both = []
        for value in planes:
            high, low = two_terms(value)
            both.append(dot(jnp.concatenate([high, low, high], axis=1), y_ref[...]))
        sum_r, sum_i = transformed(both[0], both[1])
        dif_r, dif_i = transformed(both[2], both[3])
        cosine = along_x(0, jnp.concatenate([sum_r, dif_i], axis=1))
        sine = along_x(1, jnp.concatenate([sum_i, dif_r], axis=1))
        fields = (
            (cosine[:, :grid] - sine[:, :grid], cosine[:, :grid] + sine[:, :grid]),
            (cosine[:, grid:] + sine[:, grid:], cosine[:, grid:] - sine[:, grid:]),
        )
        for c in range(2):
            plus, minus = fields[c]
            for part in range(grid // LANES):
                cut = slice(part * LANES, (part + 1) * LANES)
                place = 2 * i + c
                flat[part, pl.ds(place, half, stride=pitch), :] = plus[:half, cut]
                flat[part, pl.ds(half * pitch + place, half, stride=pitch), :] = minus[1 : half + 1, cut]
        return carry

    lax.fori_loop(0, pairs, one, 0, unroll=2)
    for d in range(slabs):
        if d < slabs // 2:
            start = slab * d
        else:
            start = half + grid - slab * d - slab
        for part in range(grid // LANES):
            block = lines[part, start : start + slab, :count, :]
            out_ref[d, :, :, part * LANES : (part + 1) * LANES] = block.astype(BF16)


def plane_kernel(slabs, grid, data_ref, y_ref, x_ref, out_ref, lines):
    pitch = data_ref.shape[2] // grid
    pairs = pitch // 2

    def load(part, side, value):
        return data_ref[part, side, pl.ds(value, grid, stride=pitch), :]

    transform_pairs(slabs, grid, pairs, load, y_ref, x_ref, out_ref, lines)


def planes_call(data, table_y, table_x, slabs, grid):
    step = data.shape[2] // grid
    slab = grid // slabs
    vmem = pl.BlockSpec(memory_space=VMEM)
    return pl.pallas_call(
        functools.partial(plane_kernel, slabs, grid),
        in_specs=[vmem] * 3,
        out_specs=vmem,
        scratch_shapes=[VMEM((data.shape[0], grid, step + PAD, LANES), F32)],
        out_shape=jax.ShapeDtypeStruct((slabs, slab, step, grid), BF16),
        compiler_params=pltpu.CompilerParams(vmem_limit_bytes=56 * 2**20),
        name="planes",
    )(data, table_y, table_x)


def volume_kernel(flip_ref, restore_ref, z_ref, *refs):
    out_ref = refs[-1]
    slabs, span, width, grid = refs[0].shape
    turned = []
    for i in range(span):
        block = jnp.concatenate([ref[:, i].reshape(slabs * width, grid) for ref in refs[:-1]], axis=0)
        turned.append(dot_t(restore_ref[...], block).astype(BF16))
    turned = jnp.concatenate(turned, axis=0)
    value = dot(jnp.concatenate([turned, turned], axis=1), z_ref[...])
    for i in range(span):
        out_ref[jnp.where(flip_ref[0] == 1, span - 1 - i, i)] = value[i * grid : (i + 1) * grid]


def volume_call(flip, parts, restore, table_z):
    slabs, slab, width, grid = parts[0].shape
    span = 4
    steps = slab // span
    fixed = lambda i, flip_ref: (0, 0)
    return pl.pallas_call(
        volume_kernel,
        grid_spec=pltpu.PrefetchScalarGridSpec(
            num_scalar_prefetch=1,
            grid=(steps,),
            in_specs=[pl.BlockSpec(restore.shape, fixed), pl.BlockSpec(table_z.shape, fixed)]
            + [pl.BlockSpec((slabs, span, width, grid), lambda i, flip_ref: (0, i, 0, 0))] * len(parts),
            out_specs=pl.BlockSpec(
                (span, grid, grid), lambda i, flip_ref: (jnp.where(flip_ref[0] == 1, steps - 1 - i, i), 0, 0)
            ),
        ),
        out_shape=jax.ShapeDtypeStruct((slab, grid, grid), F32),
        compiler_params=pltpu.CompilerParams(vmem_limit_bytes=48 * 2**20),
        name="volume",
    )(flip, restore, table_z, *parts)


def sorted_points(interp_cells, grid):
    dirs = interp_cells.shape[0]
    points = dirs * grid
    base = interp_cells[:, 0, :].T.reshape(-1)
    row = (base // grid + 1) & (grid - 1)
    key = row * points + jnp.arange(points, dtype=jnp.int32)
    key = lax.sort(key, is_stable=False)
    rows = jnp.arange(grid + 3, dtype=jnp.int32)
    first = jnp.sum((row[None, :] < rows[:, None]).astype(jnp.int32), axis=1)
    point = jnp.concatenate([key & (points - 1), jnp.zeros((CHUNK,), jnp.int32)])
    return first, point


def arrange_kernel(rows_ref, other_ref, eye_ref, order_ref, extra_ref, kept_ref, sent_ref, *lines):
    dirs, count, _, grid = rows_ref.shape
    blocks = LANES // count
    length = grid // blocks
    span = extra_ref.shape[0]
    each = span * blocks
    number = lax.broadcasted_iota(jnp.int32, (length, LANES), 1) // count

    def step(m, carry):
        other = other_ref[pl.ds(pl.multiple_of(2 * each * m, 2 * each), 2 * each), :]
        other = dot_t(eye_ref[...], other).astype(BF16)
        for group in range(span):
            k = each * m + blocks * group
            block = rows_ref[pl.ds(k, blocks)].reshape(2 * LANES, grid)
            turned = dot_t(eye_ref[...], block).astype(BF16)
            turned = dot(turned, order_ref[...]) + dot(other, extra_ref[group])
            for side in range(2):
                tile = [turned[q * length : (q + 1) * length, side * LANES : (side + 1) * LANES] for q in range(blocks)]
                bit = 1
                while bit < blocks:
                    low = (number & bit) == 0
                    swapped = list(tile)
                    for q in range(blocks):
                        if q & bit == 0:
                            swapped[q] = jnp.where(low, tile[q], pltpu.roll(tile[q + bit], bit * count, 1))
                            swapped[q + bit] = jnp.where(low, pltpu.roll(tile[q], LANES - bit * count, 1), tile[q + bit])
                    tile = swapped
                    bit *= 2
                for i in range(blocks):
                    lines[side][pl.ds(k + i, length, stride=dirs + PAD), :] = tile[i]
        return carry

    lax.fori_loop(0, dirs // each, step, 0)
    for side, out_ref in enumerate((kept_ref, sent_ref)):
        steps = out_ref.shape[1] // dirs
        for u in range(length):
            block = lines[side][u * (dirs + PAD) : u * (dirs + PAD) + dirs, :].astype(BF16)
            out_ref[u // steps, u % steps * dirs : (u % steps + 1) * dirs, :] = block


def arrange_call(rows, other, eye, order, extra, steps):
    dirs, count, _, grid = rows.shape
    length = grid // (LANES // count)
    vmem = pl.BlockSpec(memory_space=VMEM)
    shape = jax.ShapeDtypeStruct((length // steps, steps * dirs, LANES), BF16)
    return pl.pallas_call(
        arrange_kernel,
        out_shape=(shape, shape),
        in_specs=[vmem] * 5,
        out_specs=(vmem, vmem),
        scratch_shapes=[VMEM((length * (dirs + PAD), LANES), F32)] * 2,
        compiler_params=pltpu.CompilerParams(vmem_limit_bytes=48 * 2**20),
        name="arrange",
    )(rows, other, eye, order, extra)


def row_orders(slab):
    half = slab // 2
    blocks = LANES // slab
    span = max(1, 8 // blocks)
    down = list(range(half - 1, -1, -1))
    upper = list(range(slab - 1, half - 1, -1))
    orders, extras = [], []
    for kept, sent in (
        (list(range(1, half + 1)), list(range(half + 1, slab)) + [None]),
        (down[:-1] + [None], upper),
        (down, upper),
    ):
        order = np.zeros((2 * LANES, 2 * LANES))
        extra = np.zeros((span, 2 * span * blocks, 2 * LANES))
        for side, rows in enumerate((kept, sent)):
            for k in range(blocks):
                for i, row in enumerate(rows):
                    for r in range(2):
                        lane = side * LANES + k * slab + 2 * i + r
                        if row is not None:
                            order[(k * slab + row) * 2 + r, lane] = 1.0
                        else:
                            for group in range(span):
                                extra[group, (group * blocks + k) * 2 + r, lane] = 1.0
        orders.append(order.astype(jnp.bfloat16))
        extras.append(extra.astype(jnp.bfloat16))
    return np.stack(orders), np.stack(extras)


def paired_rows(rows, eye, slabs, steps):
    own = lax.axis_index("vol")
    dirs, slab, _, grid = rows.shape
    first = [(0, slabs // 2)] + [(i, i - 1) for i in range(1, slabs // 2 + 1)]
    other = lax.ppermute(rows[:, 0], "vol", first).reshape(2 * dirs, grid)
    kind = jnp.where(own < slabs // 2, 0, jnp.where(own == slabs // 2, 1, 2))
    order, extra = (lax.dynamic_index_in_dim(jnp.asarray(t), kind, 0, keepdims=False) for t in row_orders(slab))
    kept, sent = arrange_call(rows, other, eye, order, extra, steps)
    arrived = lax.ppermute(sent, "vol", [(i, slabs - 1 - i) for i in range(slabs)])
    return kept, arrived


def shards(images, projections, assignment, interp_cells, interp_weights):
    class_count = lax.axis_size("cls")
    slab_count = lax.axis_size("vol")
    local_count, grid = images.shape[0], images.shape[1]
    dirs = projections.shape[1]
    slab = grid // slab_count
    width = 2 * slab
    halves = LANES // width
    capacity = 2 * local_count // class_count
    steps = 16 // capacity
    groups = grid // (halves * steps)

    eye = jnp.asarray(np.eye(grid), BF16)
    outgoing = route_call(images, assignment, class_count, slab_count, width, capacity)
    outgoing, projections = lax.optimization_barrier((outgoing, projections))
    arrived = lax.all_to_all(outgoing, ("cls", "vol"), split_axis=0, concat_axis=0, tiled=True)

    kept, joined = paired_rows(projections[0], eye, slab_count, steps)
    corner_y = (interp_cells[:, 0:1, :] & (grid - 1)).astype(F32)
    weights = jnp.concatenate([interp_weights, corner_y, jnp.zeros((dirs, 3, grid), F32)], axis=1)
    weights = weights.reshape(dirs, 8, halves, groups, steps)
    weights = jnp.transpose(weights, (3, 4, 0, 2, 1)).reshape(groups, steps * dirs, 8 * halves)
    weights = jnp.pad(weights, ((0, 0), (0, 0), (0, LANES - 8 * halves)))
    plan = sorted_points(interp_cells, grid)
    table_y, table_x, table_z, restore = tables(grid, slab_count)

    arrived, kept, joined, weights, plan = lax.optimization_barrier((arrived, kept, joined, weights, plan))
    partial_value = scores_call(arrived, kept, joined, capacity, dirs, slab, slab_count)
    parts = lax.all_to_all(partial_value, "vol", split_axis=0, concat_axis=0, tiled=True)
    own = lax.axis_index("vol")
    single = (own == slab_count // 2).astype(jnp.int32).reshape(1)
    flip = (own >= slab_count // 2).astype(jnp.int32).reshape(1)
    sent, plane = scatter_call(
        single, plan, parts, arrived, weights, table_y, table_x, capacity, width, grid, slab_count
    )
    received = [lax.all_to_all(sent, "vol", split_axis=0, concat_axis=0, tiled=True)]
    if plane is not None:
        sent = planes_call(plane, table_y, table_x, slab_count, grid)
        received.append(lax.all_to_all(sent, "vol", split_axis=0, concat_axis=0, tiled=True))
    return volume_call(flip, received, restore, table_z)[None]


def solution(mesh):
    in_specs = (
        P(("cls", "vol"), None, None, None),
        P("cls", None, "vol", None, None),
        P(("cls", "vol"), None),
        P(),
        P(),
    )
    out_specs = P("cls", "vol", None, None)
    return jax.shard_map(shards, mesh=mesh, in_specs=in_specs, out_specs=out_specs, check_vma=False)
```
